128 devices in a mesh: ctx: 16 (over x_lo, z, core), wsh: 8 (over x_hi, y).
Axes of the slice: x: 4 (x_hi: 2, x_lo: 2; x = x_hi * 2 + x_lo), y: 4, z: 4, core: 2. Of those that a mesh axis runs over, the one named last changes fastest.
Arguments:
- hidden: bfloat16 [8, 2048, 1152], P('wsh', 'ctx'), may hold values from -36 to 36
- w_qkv: bfloat16 [1536, 1152], P('wsh'), may hold values from -0.1875 to 0.1875
- w_out: bfloat16 [1024, 1152], P('wsh'), may hold values from -0.1875 to 0.1875
- norm_gains: bfloat16 [1152, 4], P('wsh'), may hold values from 0.25 to 1.75
- qk_gains: bfloat16 [256, 2], P('wsh'), may hold values from 0.25 to 1.75
- w_gate_up: bfloat16 [6912, 2, 1152], P('wsh'), may hold values from -0.1875 to 0.1875
- w_down: bfloat16 [6912, 1152], P('wsh'), may hold values from -0.078125 to 0.078125
- cotangent: bfloat16 [8, 2048, 1152], P('wsh', 'ctx'), may hold values from -6 to 6
Outputs:
- out_hidden: bfloat16 [8, 2048, 1152], P('wsh', 'ctx')
- grad_hidden: bfloat16 [8, 2048, 1152], P('wsh', 'ctx')
- grad_qkv: float32 [1536, 1152], P('wsh')
- grad_out: float32 [1024, 1152], P('wsh')
- grad_norm_gains: float32 [1152, 4], P('wsh')
- grad_qk_gains: float32 [256, 2], P('wsh')
- grad_gate_up: float32 [6912, 2, 1152], P('wsh')
- grad_down: float32 [6912, 1152], P('wsh')
The draws below stay inside these ranges and needn't reach their ends.
All inputs are finite; a program needn't handle non-finite values.
Results may differ from the reference program's by a relative error of at most 0.025.
Values may be sent and summed in bfloat16 or wider, within the bound.
A program may use at most 256 MiB of HBM per device.

```python
import math
import jax
import jax.numpy as jnp
from jax import lax

D = 1152
HEADS = 4
HD = 256
FF = 6912
KB = 512
SEQ = 2048
SEQS = 8


def draw_hidden(key, part):
    key = jax.random.fold_in(key, 11)
    row_key, column_key, base_key = jax.random.split(key, 3)
    row_scale = jnp.exp(jax.random.uniform(row_key, (SEQS, SEQ, 1), jnp.float32, math.log(0.3), math.log(3.0)))
    column_scale = jnp.exp(jax.random.uniform(column_key, (D,), jnp.float32, math.log(0.3), math.log(3.0)))
    base = jnp.clip(jax.random.normal(base_key, (SEQS, SEQ, D), jnp.float32), -4.0, 4.0)
    return (base * row_scale * column_scale).astype(jnp.bfloat16)


def shard_levels(rng, dims, shards, low, largest):
    factor_of, own = 1.0, jax.random.fold_in(rng, 6)
    for position, shards_of in shards:
        heights = jnp.exp(jax.random.uniform(jax.random.fold_in(own, position), (shards_of,), jnp.float32, low / len(shards), largest / len(shards)))
        factor_of = factor_of * jnp.repeat(heights, dims[position] // shards_of).reshape([-1 if axis == position else 1 for axis in range(len(dims))])
    return factor_of


def scatter_about(key, shape, deviation, most, cuts=(), kind=jnp.bfloat16):
    array = jax.random.normal(key, shape, jnp.float32) * deviation
    if len(cuts) > 0:
        array = shard_levels(key, shape, cuts, -0.22, 0.18) * array
    return jnp.clip(array, min=-most, max=most).astype(kind)


def setup_inputs(seed: int = 0) -> dict:
    splits = jax.random.split(jax.random.key(seed), 9)
    hidden = draw_hidden(jax.random.fold_in(splits[8], 71), 0)
    w_qkv = scatter_about(splits[1], ((HEADS + 2) * HD, D), D ** -0.5, 0.1875, ((0, 8),))
    w_out = scatter_about(splits[2], (HEADS * HD, D), (HEADS * HD) ** -0.5, 0.1875, ((0, 8),))
    norm_gains = jnp.clip(1.0 + 0.15 * jax.random.normal(splits[3], (D, 4), jnp.float32), 0.25, 1.75).astype(jnp.bfloat16)
    qk_gains = jnp.clip(1.0 + 0.15 * jax.random.normal(splits[4], (HD, 2), jnp.float32), 0.25, 1.75).astype(jnp.bfloat16)
    w_gate_up = scatter_about(splits[5], (FF, 2, D), D ** -0.5, 0.1875, ((0, 8),))
    w_down = scatter_about(splits[6], (FF, D), FF ** -0.5, 0.078125, ((0, 8),))
    cotangent = scatter_about(splits[7], (SEQS, SEQ, D), 1.0, 6.0, ((0, 8), (1, 16)))
    return {"hidden": hidden, "w_qkv": w_qkv, "w_out": w_out, "norm_gains": norm_gains, "qk_gains": qk_gains, "w_gate_up": w_gate_up, "w_down": w_down, "cotangent": cotangent}


epsilon = 1e-06
rope_base = 1000000.0
masked_value = -1e+30

@jax.custom_vjp
def low(v):
    return lax.optimization_barrier(v.astype(jnp.bfloat16)).astype(jnp.float32)

@jax.custom_vjp
def low_back(v):
    return v

def low_keep(v):
    return (low(v), None)

def low_pass(kept, grad):
    return (grad,)

def back_keep(v):
    return (v, None)

def back_low(kept, grad):
    return (low(grad),)
low.defvjp(low_keep, low_pass)
low_back.defvjp(back_keep, back_low)

def product(left, right):
    return jnp.dot(left, right, precision=lax.Precision.HIGHEST)

def rms_scale(values):
    return lax.rsqrt(lax.optimization_barrier(jnp.mean(values * values, axis=-1, keepdims=True)) + epsilon)

def scaled_norm(values, gain):
    return values * rms_scale(values) * gain

def post_add(resid, branch, gain):
    return resid + branch * rms_scale(branch) * gain

def rotate(values, cosine, sine):
    half = values.shape[-1] // 2
    turned = jnp.concatenate([-values[..., half:], values[..., :half]], axis=-1)
    return values * cosine + turned * sine

def rope_tables(positions, head_dim):
    freqs = rope_base ** (-jnp.arange(0, head_dim, 2, dtype=jnp.float32) / head_dim)
    angles = positions.astype(jnp.float32)[:, None] * freqs[None, :]
    angles = jnp.concatenate([angles, angles], axis=-1)
    return (jnp.cos(angles), jnp.sin(angles))

def prepare(mixed_qk, qk_gain, cosine, sine):
    count = mixed_qk.shape[0]
    queries = mixed_qk[:, :HEADS * HD].reshape(count, HEADS, HD)
    keys = mixed_qk[:, HEADS * HD:]
    queries = rotate(scaled_norm(queries, qk_gain[:, 0]), cosine[:, None, :], sine[:, None, :]) * HD ** (-0.5)
    keys = rotate(scaled_norm(keys, qk_gain[:, 1]), cosine, sine)
    return (queries, keys)

def gating(gate, up):
    return jax.nn.gelu(gate, approximate=True) * up

def attention(queries, keys, values):
    length = queries.shape[0]

    def attend(start):
        block = lax.dynamic_slice_in_dim(queries, start, KB, 0)
        scores = low_back(jnp.einsum('qhd,kd->hqk', block, keys, precision=lax.Precision.HIGHEST))
        allowed = jnp.arange(length, dtype=jnp.int32)[None, :] <= (start + jnp.arange(KB, dtype=jnp.int32))[:, None]
        scores = jnp.where(allowed[None], scores, masked_value)
        probs = low(jax.nn.softmax(scores, axis=-1))
        result = jnp.einsum('hqk,kd->qhd', probs, values, precision=lax.Precision.HIGHEST)
        return low(low_back(result.reshape(KB, HEADS * HD)))
    starts = jnp.arange(length // KB, dtype=jnp.int32) * KB
    return lax.map(jax.checkpoint(attend), starts).reshape(length, HEADS * HD)

def layer(inputs, w_qkv, w_out, norm_gains, qk_gains, w_gate_up, w_down):
    length = inputs.shape[0]
    cosine, sine = rope_tables(jnp.arange(length, dtype=jnp.int32), HD)
    normed = low(scaled_norm(inputs, norm_gains[:, 0]))
    mixed = low_back(product(normed, w_qkv.T))
    split_at = (HEADS + 1) * HD
    values = low(mixed[:, split_at:])
    queries, keys = prepare(mixed[:, :split_at], qk_gains, cosine, sine)
    attended = attention(low(queries), low(keys), values)
    branch = low_back(product(attended, w_out))
    resid = post_add(inputs, branch, norm_gains[:, 1])
    normed2 = low(scaled_norm(resid, norm_gains[:, 2]))
    gate = low_back(product(normed2, w_gate_up[:, 0, :].T))
    up_proj = low_back(product(normed2, w_gate_up[:, 1, :].T))
    inner = low(gating(gate, up_proj))
    branch2 = low_back(product(inner, w_down))
    return post_add(resid, branch2, norm_gains[:, 3])

def reference(hidden, w_qkv, w_out, norm_gains, qk_gains, w_gate_up, w_down, cotangent):
    weights = tuple((weight.astype(jnp.float32) for weight in (w_qkv, w_out, norm_gains, qk_gains, w_gate_up, w_down)))

    def one_sequence(totals, paired):
        inputs, seq_cot = paired
        output, pull = jax.vjp(layer, inputs.astype(jnp.float32), *weights)
        grads = pull(seq_cot.astype(jnp.float32))
        totals = jax.tree.map(jnp.add, totals, tuple(grads[1:]))
        return (totals, (output.astype(jnp.bfloat16), grads[0].astype(jnp.bfloat16)))
    initial = tuple((jnp.zeros(weight.shape, jnp.float32) for weight in weights))
    totals, (outputs, grad_inputs) = lax.scan(one_sequence, initial, (hidden, cotangent))
    return (outputs, grad_inputs, totals[0], totals[1], totals[2], totals[3], totals[4], totals[5])
```

```python
import functools

import jax
import jax.numpy as jnp
from jax import lax
from jax.experimental import pallas as pl
from jax.experimental.pallas import tpu as pltpu
from jax.sharding import PartitionSpec as P

HEADS = 4
HD = 256
KB = 512
EPS = 1e-06
ROPE_BASE = 1000000.0
MASKED = -1e30
MESH = pl.DeviceIdType.MESH
BF = jnp.bfloat16
F32 = jnp.float32


def params(cid):
    return pltpu.CompilerParams(collective_id=cid, has_side_effects=True)


def cost(us):
    return pl.CostEstimate(flops=0, bytes_accessed=int(us * 3.0e6), transcendentals=0)


def exchange_kernel(axis, n, modes, *refs):
    count = len(modes)
    ins, outs = refs[:count], refs[count : 2 * count]
    send, recv, own = refs[2 * count :]
    me = lax.axis_index(axis)
    barrier = pltpu.get_barrier_semaphore()
    for step in range(1, n):
        pl.semaphore_signal(
            barrier, inc=1, device_id={axis: lax.rem(me + step, n)}, device_id_type=MESH
        )
    pl.semaphore_wait(barrier, n - 1)
    copies = []
    for step in range(1, n):
        peer = lax.rem(me + step, n)
        for i, mode in enumerate(modes):
            copies.append(
                pltpu.make_async_remote_copy(
                    src_ref=ins[i] if mode == "gather" else ins[i].at[peer],
                    dst_ref=outs[i].at[me],
                    send_sem=send.at[i, step - 1],
                    recv_sem=recv.at[i, step - 1],
                    device_id={axis: peer},
                    device_id_type=MESH,
                )
            )
            copies[-1].start()
    for i, mode in enumerate(modes):
        mine = ins[i] if mode == "gather" else ins[i].at[me]
        copies.append(pltpu.make_async_copy(mine, outs[i].at[me], own.at[i]))
        copies[-1].start()
    for copy in copies:
        copy.wait()


def exchange(axis, n, cid, name, us, *pairs):
    modes = [mode for mode, _ in pairs]
    arrays = [array for _, array in pairs]
    shapes = [
        jax.ShapeDtypeStruct(((n,) + a.shape) if m == "gather" else a.shape, a.dtype)
        for m, a in pairs
    ]
    any_spec = pl.BlockSpec(memory_space=pl.ANY)
    return pl.pallas_call(
        functools.partial(exchange_kernel, axis, n, modes),
        out_shape=shapes,
        in_specs=[any_spec] * len(pairs),
        out_specs=[any_spec] * len(pairs),
        scratch_shapes=[
            pltpu.SemaphoreType.DMA((len(pairs), n - 1)),
            pltpu.SemaphoreType.DMA((len(pairs), n - 1)),
            pltpu.SemaphoreType.DMA((len(pairs),)),
        ],
        compiler_params=params(cid),
        cost_estimate=cost(us),
        name=name,
    )(*arrays)


def weights_kernel(w_ref, g_ref, wo_ref, go_ref, send, recv, fsend, frecv, gsend, grecv, own):
    ctx, me = lax.axis_index("ctx"), lax.axis_index("wsh")
    core = lax.rem(ctx, 2)
    other = ctx + 1 - 2 * core
    half = w_ref.shape[0] // 2
    rows = pl.ds(pl.multiple_of(core * half, half), half)
    barrier = pltpu.get_barrier_semaphore()
    for step in range(1, 8):
        pl.semaphore_signal(
            barrier, inc=1, device_id={"wsh": lax.rem(me + step, 8)}, device_id_type=MESH
        )
    pl.semaphore_signal(barrier, inc=1, device_id={"ctx": other}, device_id_type=MESH)
    pl.semaphore_wait(barrier, 8)
    copies, small = [], []
    for step in range(1, 8):
        peer = lax.rem(me + step, 8)
        small.append(
            pltpu.make_async_remote_copy(
                src_ref=g_ref, dst_ref=go_ref.at[me], send_sem=gsend.at[step - 1],
                recv_sem=grecv.at[step - 1], device_id={"wsh": peer}, device_id_type=MESH,
            )
        )
        small[-1].start()
        copies.append(
            pltpu.make_async_remote_copy(
                src_ref=w_ref.at[rows], dst_ref=wo_ref.at[me, rows], send_sem=send.at[step - 1],
                recv_sem=recv.at[step - 1], device_id={"wsh": peer}, device_id_type=MESH,
            )
        )
        copies[-1].start()
    mine = [
        pltpu.make_async_copy(w_ref, wo_ref.at[me], own.at[0]),
        pltpu.make_async_copy(g_ref, go_ref.at[me], own.at[1]),
    ]
    for copy in mine:
        copy.start()
    passed = []
    for step in range(1, 8):
        copies[step - 1].wait_recv()
        source = lax.rem(me + 8 - step, 8)
        passed.append(
            pltpu.make_async_remote_copy(
                src_ref=wo_ref.at[source, rows], dst_ref=wo_ref.at[source, rows],
                send_sem=fsend.at[step - 1], recv_sem=frecv.at[step - 1],
                device_id={"ctx": other}, device_id_type=MESH,
            )
        )
        passed[-1].start()
    for copy in copies:
        copy.wait_send()
    for copy in small + passed + mine:
        copy.wait()


def gather_weights(w, packed):
    any_spec = pl.BlockSpec(memory_space=pl.ANY)
    return pl.pallas_call(
        weights_kernel,
        out_shape=[
            jax.ShapeDtypeStruct((8,) + w.shape, w.dtype),
            jax.ShapeDtypeStruct((8,) + packed.shape, packed.dtype),
        ],
        in_specs=[any_spec] * 2,
        out_specs=[any_spec] * 2,
        scratch_shapes=[pltpu.SemaphoreType.DMA((7,))] * 6 + [pltpu.SemaphoreType.DMA((2,))],
        compiler_params=params(1),
        cost_estimate=cost(27),
        name="gather_weights",
    )(w, packed)


def kv_kernel(x_ref, o_ref, send, recv, fsend, frecv, own):
    me = lax.axis_index("ctx")
    core = lax.rem(me, 2)
    other = me + 1 - 2 * core
    barrier = pltpu.get_barrier_semaphore()
    for step in range(1, 8):
        pl.semaphore_signal(
            barrier, inc=1, device_id={"ctx": lax.rem(me + 2 * step, 16)}, device_id_type=MESH
        )
    pl.semaphore_signal(barrier, inc=1, device_id={"ctx": other}, device_id_type=MESH)
    pl.semaphore_wait(barrier, 8)
    copies = []
    for step in range(1, 8):
        copies.append(
            pltpu.make_async_remote_copy(
                src_ref=x_ref, dst_ref=o_ref.at[me], send_sem=send.at[step - 1],
                recv_sem=recv.at[step - 1], device_id={"ctx": lax.rem(me + 2 * step, 16)},
                device_id_type=MESH,
            )
        )
        copies[-1].start()
    mine = pltpu.make_async_copy(x_ref, o_ref.at[me], own)
    mine.start()
    passed = [
        pltpu.make_async_remote_copy(
            src_ref=x_ref, dst_ref=o_ref.at[me], send_sem=fsend.at[0], recv_sem=frecv.at[0],
            device_id={"ctx": other}, device_id_type=MESH,
        )
    ]
    passed[0].start()
    for step in range(1, 8):
        copies[step - 1].wait_recv()
        source = lax.rem(me + 16 - 2 * step, 16)
        passed.append(
            pltpu.make_async_remote_copy(
                src_ref=o_ref.at[source], dst_ref=o_ref.at[source],
                send_sem=fsend.at[step], recv_sem=frecv.at[step],
                device_id={"ctx": other}, device_id_type=MESH,
            )
        )
        passed[-1].start()
    for copy in copies:
        copy.wait_send()
    for copy in passed + [mine]:
        copy.wait()


def gather_kv(x):
    any_spec = pl.BlockSpec(memory_space=pl.ANY)
    return pl.pallas_call(
        kv_kernel,
        out_shape=jax.ShapeDtypeStruct((16,) + x.shape, x.dtype),
        in_specs=[any_spec],
        out_specs=any_spec,
        scratch_shapes=[
            pltpu.SemaphoreType.DMA((7,)),
            pltpu.SemaphoreType.DMA((7,)),
            pltpu.SemaphoreType.DMA((8,)),
            pltpu.SemaphoreType.DMA((8,)),
            pltpu.SemaphoreType.DMA,
        ],
        compiler_params=params(2),
        cost_estimate=cost(17),
        name="gather_kv",
    )(x)


NT = (((1,), (1,)), ((), ()))
TN = (((0,), (0,)), ((), ()))


def dot(a, b, dims):
    return lax.dot_general(a, b, dims, preferred_element_type=F32)


def masked_scores(q, keys, block, ctx, tokens):
    scores = dot(q, keys, NT)
    row = lax.rem(lax.broadcasted_iota(jnp.int32, scores.shape, 0), tokens) + ctx * tokens
    col = lax.broadcasted_iota(jnp.int32, scores.shape, 1) + block * KB
    return jnp.where(col <= row, scores, MASKED)


def attend_kernel(tokens, q_ref, kv_ref, out_ref, lse_ref, top, total, accum):
    ctx = lax.axis_index("ctx")
    last = (ctx * tokens) // KB
    q = q_ref[...]

    def block_of(index):
        return pl.ds(pl.multiple_of(index * KB, KB), KB)

    scores = masked_scores(q, kv_ref[block_of(last), :HD], last, ctx, tokens)
    start = jnp.max(scores, axis=-1, keepdims=True)
    probs = jnp.exp(scores - start)
    top[...] = jnp.broadcast_to(start, top.shape)
    total[...] = jnp.broadcast_to(jnp.sum(probs, axis=-1, keepdims=True), total.shape)
    accum[...] = jnp.dot(
        probs.astype(BF), kv_ref[block_of(last), HD:], preferred_element_type=F32
    )

    def body(index, carry):
        scores = dot(q, kv_ref[block_of(index), :HD], NT)
        old = top[:, :1]
        new = jnp.maximum(old, jnp.max(scores, axis=-1, keepdims=True))
        probs = jnp.exp(scores - new)
        keep = jnp.exp(old - new)
        top[...] = jnp.broadcast_to(new, top.shape)
        total[...] = total[...] * keep + jnp.sum(probs, axis=-1, keepdims=True)
        accum[...] = accum[...] * keep + jnp.dot(
            probs.astype(BF), kv_ref[block_of(index), HD:], preferred_element_type=F32
        )
        return carry

    lax.fori_loop(0, last, body, 0)
    out_ref[...] = accum[...] / total[:, :1]
    lse_ref[...] = top[...] + jnp.log(total[...])


def attend(q, kv, tokens):
    rows = q.shape[0]
    return pl.pallas_call(
        functools.partial(attend_kernel, tokens),
        out_shape=[
            jax.ShapeDtypeStruct((rows, HD), F32),
            jax.ShapeDtypeStruct((rows, 128), F32),
        ],
        scratch_shapes=[
            pltpu.VMEM((rows, 128), F32),
            pltpu.VMEM((rows, 128), F32),
            pltpu.VMEM((rows, HD), F32),
        ],
        compiler_params=pltpu.CompilerParams(vmem_limit_bytes=40 * 2**20),
        cost_estimate=cost(12),
        name="attend",
    )(q, kv)


def attend_back_kernel(tokens, q_ref, kv_ref, out_ref, lse_ref, d_ref, dq_ref, dkv_ref):
    ctx = lax.axis_index("ctx")
    last = (ctx * tokens) // KB
    q = q_ref[...]
    d_out = d_ref[...]
    lse = lse_ref[:, :1]
    delta = jnp.sum(d_out.astype(F32) * out_ref[...], axis=-1, keepdims=True)

    def block_of(index):
        return pl.ds(pl.multiple_of(index * KB, KB), KB)

    def work(index, scores):
        block = block_of(index)
        probs = jnp.exp(scores - lse)
        d_probs = dot(d_out, kv_ref[block, HD:], NT)
        d_scores = (probs * (d_probs - delta)).astype(BF)
        dkv_ref[block, :HD] = dot(d_scores, q, TN).astype(BF)
        dkv_ref[block, HD:] = dot(probs.astype(BF), d_out, TN).astype(BF)
        return jnp.dot(d_scores, kv_ref[block, :HD], preferred_element_type=F32)

    dq_ref[...] = work(last, masked_scores(q, kv_ref[block_of(last), :HD], last, ctx, tokens))

    def body(index, carry):
        dq_ref[...] += work(index, dot(q, kv_ref[block_of(index), :HD], NT))
        return carry

    lax.fori_loop(0, last, body, 0)

    def clear(index, carry):
        dkv_ref[block_of(index), :] = jnp.zeros((KB, 2 * HD), BF)
        return carry

    lax.fori_loop(last + 1, kv_ref.shape[0] // KB, clear, 0)


def attend_back(q, kv, out, lse, d_out, tokens):
    return pl.pallas_call(
        functools.partial(attend_back_kernel, tokens),
        out_shape=[
            jax.ShapeDtypeStruct(q.shape, F32),
            jax.ShapeDtypeStruct(kv.shape, BF),
        ],
        compiler_params=pltpu.CompilerParams(vmem_limit_bytes=40 * 2**20),
        cost_estimate=cost(20),
        name="attend_back",
    )(q, kv, out, lse, d_out)


def scale_of(values):
    return lax.rsqrt(jnp.mean(values * values, axis=-1, keepdims=True) + EPS)


def norm_back(v, r, g, dy):
    gdy = g * dy
    dv = r * gdy - v * (r * r * r) * jnp.mean(gdy * v, axis=-1, keepdims=True)
    return dv, dy * v * r


def rope(v, cosine, sine):
    a, b = v[..., : HD // 2], v[..., HD // 2 :]
    return jnp.concatenate([a * cosine - b * sine, b * cosine + a * sine], axis=-1)


def rope_back(u, cosine, sine):
    a, b = u[..., : HD // 2], u[..., HD // 2 :]
    return jnp.concatenate([a * cosine + b * sine, b * cosine - a * sine], axis=-1)


def on_device(hidden, w_qkv, w_out, norm_gains, qk_gains, w_gate_up, w_down, cotangent):
    tokens = hidden.shape[1]
    width = hidden.shape[2]
    x = hidden[0].astype(F32)
    cot = cotangent[0].astype(F32)
    positions = lax.axis_index("ctx") * tokens + jnp.arange(tokens, dtype=jnp.int32)
    freqs = ROPE_BASE ** (-jnp.arange(0, HD, 2, dtype=F32) / HD)
    angles = positions.astype(F32)[:, None] * freqs[None, :]
    cosine, sine = jnp.cos(angles), jnp.sin(angles)

    gain_part, qk_part = norm_gains.shape[0], qk_gains.shape[0]
    packed = jnp.zeros((16, 256), BF)
    packed = packed.at[:4, :gain_part].set(norm_gains.T)
    packed = packed.at[4:6, :qk_part].set(qk_gains.T)
    all_qkv, all_packed = gather_weights(w_qkv, packed)
    full_qkv = all_qkv.reshape(-1, width)
    full_out = lax.all_gather(w_out, "wsh", axis=0, tiled=True)
    gains = all_packed[:, :4, :gain_part].transpose(1, 0, 2).reshape(4, width).astype(F32)
    qk_gain = all_packed[:, 4:6, :qk_part].transpose(1, 0, 2).reshape(2, HD).astype(F32)

    r0 = scale_of(x)
    normed = (x * r0 * gains[0]).astype(BF)
    normed_all = lax.all_gather(normed, "wsh", axis=0, tiled=True)
    mixed = dot(normed, full_qkv, NT)
    q_raw = mixed[:, : HEADS * HD].reshape(tokens, HEADS, HD).transpose(1, 0, 2)
    k_raw = mixed[:, HEADS * HD : (HEADS + 1) * HD]
    rq, rk = scale_of(q_raw), scale_of(k_raw)
    q_low = (rope(q_raw * rq * qk_gain[0], cosine, sine) * HD ** (-0.5)).astype(BF)
    q_low = q_low.reshape(HEADS * tokens, HD)
    k_low = rope(k_raw * rk * qk_gain[1], cosine, sine).astype(BF)
    local_kv = jnp.concatenate([k_low, mixed[:, (HEADS + 1) * HD :].astype(BF)], axis=1)
    whole_kv = gather_kv(local_kv).reshape(-1, 2 * HD)

    out_heads, lse = attend(q_low, whole_kv, tokens)
    attended = out_heads.reshape(HEADS, tokens, HD).transpose(1, 0, 2).reshape(tokens, HEADS * HD)
    attended = attended.astype(BF)
    branch = jnp.dot(attended, full_out, preferred_element_type=F32)
    r1 = scale_of(branch)
    resid = x + branch * r1 * gains[1]
    r2 = scale_of(resid)
    normed2 = (resid * r2 * gains[2]).astype(BF)

    (n2_all,) = exchange("wsh", 8, 3, "gather_normed2", 31, ("gather", normed2))
    n2_all = n2_all.reshape(-1, width)
    w_gate, w_up = w_gate_up[:, 0], w_gate_up[:, 1]
    gate, up = dot(n2_all, w_gate, NT), dot(n2_all, w_up, NT)
    gelu, gelu_pull = jax.vjp(functools.partial(jax.nn.gelu, approximate=True), gate)
    inner = (gelu * up).astype(BF)
    terms = jnp.dot(inner, w_down, preferred_element_type=F32).astype(BF)
    (parts,) = exchange("wsh", 8, 4, "scatter_branch2", 31, ("scatter", terms.reshape(8, tokens, width)))
    branch2 = jnp.sum(parts.astype(F32), axis=0)

    r3 = scale_of(branch2)
    output = (resid + branch2 * r3 * gains[3]).astype(BF)
    d_branch2, dg3 = norm_back(branch2, r3, gains[3], cot)
    (d2_all,) = exchange("wsh", 8, 5, "gather_d_branch2", 31, ("gather", d_branch2.astype(BF)))
    d2_all = d2_all.reshape(-1, width)
    d_inner = dot(d2_all, w_down, NT)
    d_gate = (gelu_pull(d_inner * up)[0]).astype(BF)
    d_up = (d_inner * gelu).astype(BF)
    terms = (
        jnp.dot(d_gate, w_gate, preferred_element_type=F32)
        + jnp.dot(d_up, w_up, preferred_element_type=F32)
    ).astype(BF)
    (parts,) = exchange("wsh", 8, 6, "scatter_d_normed2", 31, ("scatter", terms.reshape(8, tokens, width)))
    ff_grads = lax.psum(
        (
            dot(d_gate, n2_all, TN).astype(BF),
            dot(d_up, n2_all, TN).astype(BF),
            dot(inner, d2_all, TN).astype(BF),
        ),
        "ctx",
    )
    d_normed2 = jnp.sum(parts.astype(F32), axis=0)

    d_more, dg2 = norm_back(resid, r2, gains[2], d_normed2)
    d_resid = cot + d_more
    d_branch, dg1 = norm_back(branch, r1, gains[1], d_resid)
    branch_low = d_branch.astype(BF)
    db_all = lax.all_gather(branch_low, "wsh", axis=0, tiled=True)
    d_attended = dot(branch_low, full_out, NT).astype(BF)
    d_heads = d_attended.reshape(tokens, HEADS, HD).transpose(1, 0, 2).reshape(HEADS * tokens, HD)
    d_q, d_kv = attend_back(q_low, whole_kv, out_heads, lse, d_heads, tokens)
    (kv_parts,) = exchange("ctx", 16, 7, "scatter_d_kv", 31, ("scatter", d_kv.reshape(16, tokens, 2 * HD)))
    own_kv = jnp.sum(kv_parts.astype(F32), axis=0)

    dq_rot = rope_back(d_q.reshape(HEADS, tokens, HD) * HD ** (-0.5), cosine, sine)
    d_q_raw, dgq = norm_back(q_raw, rq, qk_gain[0], dq_rot)
    dk_rot = rope_back(own_kv[:, :HD], cosine, sine)
    d_k_raw, dgk = norm_back(k_raw, rk, qk_gain[1], dk_rot)
    d_mixed = jnp.concatenate(
        [d_q_raw.transpose(1, 0, 2).reshape(tokens, HEADS * HD), d_k_raw, own_kv[:, HD:]], axis=1
    ).astype(BF)
    d_normed = jnp.dot(d_mixed, full_qkv, preferred_element_type=F32)
    d_input, dg0 = norm_back(x, r0, gains[0], d_normed)
    grad_hidden = (d_resid + d_input).astype(BF)

    dg = jnp.stack([jnp.sum(term, axis=0) for term in (dg0, dg1, dg2, dg3)])
    dqk = jnp.stack([jnp.sum(dgq, axis=(0, 1)), jnp.sum(dgk, axis=0)])
    small = jnp.zeros((8, 8, 256), F32)
    small = small.at[:, :4, :gain_part].set(dg.reshape(4, 8, gain_part).transpose(1, 0, 2))
    small = small.at[:, 4:6, :qk_part].set(dqk.reshape(2, 8, qk_part).transpose(1, 0, 2))
    qkv_part, out_part = w_qkv.shape[0], w_out.shape[0]
    dm_all, at_all, small_all = exchange(
        "wsh", 8, 8, "columns_to_owners", 12,
        ("scatter", d_mixed.reshape(tokens, 8, qkv_part).transpose(1, 0, 2)),
        ("scatter", attended.reshape(tokens, 8, out_part).transpose(1, 0, 2)),
        ("scatter", small),
    )
    grad_qkv = dot(dm_all.reshape(-1, qkv_part), normed_all, TN)
    grad_out = dot(at_all.reshape(-1, out_part), db_all, TN)
    both = jnp.concatenate([grad_qkv, grad_out], axis=0).astype(BF)
    share = both.shape[0] // 16
    room = -(-share // 16) * 16
    both = jnp.pad(both.reshape(16, share, width), ((0, 0), (0, room - share), (0, 0)))
    grad_parts, small_parts = exchange(
        "ctx", 16, 9, "scatter_grads", 12, ("scatter", both), ("gather", jnp.sum(small_all, axis=0))
    )
    mine = jnp.sum(grad_parts.astype(F32), axis=0).astype(BF)
    (grads,) = exchange("ctx", 16, 10, "gather_grads", 12, ("gather", mine))
    grads = grads[:, :share].reshape(-1, width).astype(F32)
    small_sum = jnp.sum(small_parts, axis=0)
    return (
        output[None],
        grad_hidden[None],
        grads[:qkv_part],
        grads[qkv_part:],
        small_sum[:4, :gain_part].T,
        small_sum[4:6, :qk_part].T,
        jnp.stack([ff_grads[0].astype(F32), ff_grads[1].astype(F32)], axis=1),
        ff_grads[2].astype(F32),
    )


def solution(mesh):
    return jax.shard_map(
        on_device,
        mesh=mesh,
        in_specs=(
            P("wsh", "ctx", None),
            P("wsh", None),
            P("wsh", None),
            P("wsh", None),
            P("wsh", None),
            P("wsh", None, None),
            P("wsh", None),
            P("wsh", "ctx", None),
        ),
        out_specs=(
            P("wsh", "ctx", None),
            P("wsh", "ctx", None),
            P("wsh", None),
            P("wsh", None),
            P("wsh", None),
            P("wsh", None),
            P("wsh", None, None),
            P("wsh", None),
        ),
        check_vma=False,
    )
```

```python
import functools

import jax
import jax.numpy as jnp
from jax import lax
from jax.experimental import pallas as pl
from jax.experimental.pallas import tpu as pltpu
from jax.sharding import PartitionSpec as P

HEADS = 4
HD = 256
KB = 512
EPS = 1e-06
ROPE_BASE = 1000000.0
MASKED = -1e30
MESH = pl.DeviceIdType.MESH
BF = jnp.bfloat16
F32 = jnp.float32


def cost(us):
    return pl.CostEstimate(flops=0, bytes_accessed=int(us * 3.0e6), transcendentals=0)


class Place:
    def __init__(self):
        ctx, wsh = lax.axis_index("ctx"), lax.axis_index("wsh")
        self.ctx, self.wsh = ctx, wsh
        self.chip, self.core = lax.div(ctx, 2), lax.rem(ctx, 2)
        self.h, self.y = lax.div(wsh, 4), lax.rem(wsh, 4)
        self.yp, self.ym, self.y2 = (lax.rem(self.y + k, 4) for k in (1, 3, 2))
        self.up = {"wsh": self.h * 4 + self.yp}
        self.down = {"wsh": self.h * 4 + self.ym}
        self.across = {"wsh": (1 - self.h) * 4 + self.y}
        self.twin = {"ctx": ctx + 1 - 2 * self.core}

    def chips(self, step):
        return {"ctx": lax.rem(self.ctx + 2 * step, 16)}

    def row(self, step):
        return {"wsh": lax.rem(self.wsh + step, 8)}

    def peers(self, groups):
        found = []
        if "near" in groups and "row" not in groups:
            found += [self.up, self.down, self.across]
        if "row" in groups:
            found += [self.row(step) for step in range(1, 8)]
        if "chips" in groups:
            found += [self.chips(step) for step in range(1, 8)]
        if "twin" in groups:
            found.append(self.twin)
        if "others" in groups:
            found += [{"ctx": lax.rem(self.ctx + 2 * s + 1, 16)} for s in range(8)]
        return found


def remote(src, dst, sems, i, device):
    return pltpu.make_async_remote_copy(
        src_ref=src, dst_ref=dst, send_sem=sems.at[0, i], recv_sem=sems.at[1, i],
        device_id=device, device_id_type=MESH,
    )


def meet(place, groups):
    barrier = pltpu.get_barrier_semaphore()
    peers = place.peers(groups)
    for peer in peers:
        pl.semaphore_signal(barrier, inc=1, device_id=peer, device_id_type=MESH)
    pl.semaphore_wait(barrier, len(peers))


class GatherWsh:
    def __init__(self, array, pair=False):
        self.arrays, self.pair = [array], pair
        self.groups = {"near", "twin"} if pair else {"near"}
        self.outs = [jax.ShapeDtypeStruct((8,) + array.shape, array.dtype)]
        self.out_spaces, self.in_spaces = [pl.ANY], [pl.ANY]
        self.scratch = [pltpu.SemaphoreType.DMA((2, 18 if pair else 9)), pltpu.SemaphoreType.DMA]

    def run(self, p, ins, outs, scratch):
        (x,), (o,), (sems, own) = ins, outs, scratch
        size = x.shape[0] // (2 if self.pair else 1)
        base = pl.multiple_of(p.core * size, size) if self.pair else 0
        half = size // 2
        every, low, high = pl.ds(base, size), pl.ds(base, half), pl.ds(base + half, half)
        other = (1 - p.h) * 4
        mine = p.h * 4
        copies = {}

        def send(i, block, rows, device, source=None):
            source = o.at[block, rows] if source is None else source
            copies[i] = remote(source, o.at[block, rows], sems, i, device)
            copies[i].start()

        def arrived(i, block, rows):
            copies[i].wait_recv()
            if self.pair:
                send(9 + i, block, rows, p.twin)

        send(2, p.wsh, every, p.across, x.at[every])
        send(0, p.wsh, every, p.up, x.at[every])
        send(1, p.wsh, every, p.down, x.at[every])
        local = pltpu.make_async_copy(x, o.at[p.wsh], own)
        local.start()
        yield
        arrived(2, other + p.y, every)
        send(5, other + p.y, every, p.up)
        send(6, other + p.y, every, p.down)
        yield
        arrived(0, mine + p.ym, every)
        send(3, mine + p.ym, low, p.up)
        arrived(1, mine + p.yp, every)
        send(4, mine + p.yp, high, p.down)
        yield
        arrived(5, other + p.ym, every)
        send(7, other + p.ym, low, p.up)
        arrived(6, other + p.yp, every)
        send(8, other + p.yp, high, p.down)
        yield
        arrived(3, mine + p.y2, low)
        arrived(4, mine + p.y2, high)
        yield
        arrived(7, other + p.y2, low)
        arrived(8, other + p.y2, high)
        yield
        for i, copy in copies.items():
            copy.wait_send()
            if i >= 9:
                copy.wait_recv()
        local.wait()


class ScatterWsh:
    def __init__(self, array):
        _, rows, width = array.shape
        self.arrays, self.groups = [array], {"near"}
        self.outs = [jax.ShapeDtypeStruct((rows, width), F32)]
        self.in_spaces, self.out_spaces = [pltpu.VMEM], [pltpu.VMEM]
        half = pltpu.VMEM((2, rows // 2, width), BF)
        whole = pltpu.VMEM((2, rows, width), BF)
        self.scratch = [half, half, half, half, whole, whole, pltpu.VMEM((2, rows, width), BF)]
        self.scratch.append(pltpu.SemaphoreType.DMA((2, 13)))

    def run(self, p, ins, outs, scratch):
        (x,), (o,), (buf_a, buf_b, sum_c, sum_d, buf_c, buf_d, buf_e, sems) = ins, outs, scratch
        half = x.shape[1] // 2
        low, high = pl.ds(0, half), pl.ds(half, half)
        planes = ((1 - p.h) * 4, p.h * 4)
        copies = {}

        def send(i, source, target, device):
            copies[i] = remote(source, target, sems, i, device)
            copies[i].start()

        for k, plane in enumerate(planes):
            send(k, x.at[plane + p.y2, low], buf_a.at[k], p.up)
            send(2 + k, x.at[plane + p.y2, high], buf_b.at[k], p.down)
            send(4 + k, x.at[plane + p.yp, high], buf_c.at[k, high], p.up)
            send(6 + k, x.at[plane + p.ym, low], buf_d.at[k, low], p.down)
        for k, plane in enumerate(planes):
            yield
            copies[k].wait_recv()
            sum_c[k] = (x[plane + p.yp, :half].astype(F32) + buf_a[k].astype(F32)).astype(BF)
            send(8 + k, sum_c.at[k], buf_c.at[k, low], p.up)
            copies[2 + k].wait_recv()
            sum_d[k] = (x[plane + p.ym, half:].astype(F32) + buf_b[k].astype(F32)).astype(BF)
            send(10 + k, sum_d.at[k], buf_d.at[k, high], p.down)
        for k, plane in enumerate(planes):
            yield
            for i in (4, 6, 8, 10):
                copies[i + k].wait_recv()
            total = x[plane + p.y].astype(F32) + buf_c[k].astype(F32) + buf_d[k].astype(F32)
            if k == 0:
                buf_e[0] = total.astype(BF)
                send(12, buf_e.at[0], buf_e.at[1], p.across)
            else:
                yield
                copies[12].wait_recv()
                o[...] = total + buf_e[1].astype(F32)
        for copy in copies.values():
            copy.wait_send()


class DirectWsh:
    def __init__(self, mode, array):
        self.mode, self.arrays, self.groups = mode, [array], {"row"}
        shape = ((8,) + array.shape) if mode == "gather" else array.shape
        self.outs = [jax.ShapeDtypeStruct(shape, array.dtype)]
        self.in_spaces, self.out_spaces = [pl.ANY], [pl.ANY]
        self.scratch = [pltpu.SemaphoreType.DMA((2, 7)), pltpu.SemaphoreType.DMA]

    def run(self, p, ins, outs, scratch):
        (x,), (o,), (sems, own) = ins, outs, scratch
        pick = (lambda i: x) if self.mode == "gather" else (lambda i: x.at[i])
        copies = []
        for step in range(1, 8):
            to = p.row(step)
            copies.append(remote(pick(to["wsh"]), o.at[p.wsh], sems, step - 1, to))
            copies[-1].start()
        copies.append(pltpu.make_async_copy(pick(p.wsh), o.at[p.wsh], own))
        copies[-1].start()
        yield
        yield
        yield
        for copy in copies:
            copy.wait()


class GatherCtx:
    def __init__(self, array):
        self.arrays, self.groups = [array], {"chips", "twin"}
        self.outs = [jax.ShapeDtypeStruct((16,) + array.shape, array.dtype)]
        self.in_spaces, self.out_spaces = [pl.ANY], [pl.ANY]
        self.scratch = [pltpu.SemaphoreType.DMA((2, 15)), pltpu.SemaphoreType.DMA]

    def run(self, p, ins, outs, scratch):
        (x,), (o,), (sems, own) = ins, outs, scratch
        copies = []
        for step in range(1, 8):
            copies.append(remote(x, o.at[p.ctx], sems, step - 1, p.chips(step)))
            copies[-1].start()
        local = pltpu.make_async_copy(x, o.at[p.ctx], own)
        local.start()
        passed = [remote(x, o.at[p.ctx], sems, 7, p.twin)]
        passed[0].start()
        for step in range(1, 8):
            if step % 2 == 1:
                yield
            copies[step - 1].wait_recv()
            source = lax.rem(p.ctx + 16 - 2 * step, 16)
            passed.append(remote(o.at[source], o.at[source], sems, 7 + step, p.twin))
            passed[-1].start()
        yield
        for copy in copies:
            copy.wait_send()
        for copy in passed + [local]:
            copy.wait()


class ScatterCtx:
    def __init__(self, array):
        _, _, rows, width = array.shape
        self.arrays, self.groups = [array], {"chips", "twin"}
        self.outs = [jax.ShapeDtypeStruct((rows, width), F32)]
        self.in_spaces, self.out_spaces = [pltpu.VMEM], [pltpu.VMEM]
        self.scratch = [pltpu.VMEM((8, rows, width), BF)] * 3 + [pltpu.SemaphoreType.DMA((2, 15))]

    def run(self, p, ins, outs, scratch):
        (x,), (o,), (pair, sums, got, sems) = ins, outs, scratch
        copies = []
        order = list(range(1, 8)) + [0]
        for i, step in enumerate(order):
            chip = lax.rem(p.chip + step, 8)
            copies.append(remote(x.at[chip, 1 - p.core], pair.at[chip], sems, i, p.twin))
            copies[-1].start()
        for i, step in enumerate(order):
            if i % 3 == 0:
                yield
            chip = lax.rem(p.chip + step, 8)
            copies[i].wait_recv()
            both = x[chip, p.core].astype(F32) + pair[chip].astype(F32)
            if step > 0:
                sums[chip] = both.astype(BF)
                copies.append(remote(sums.at[chip], got.at[p.chip], sems, 7 + step, p.chips(step)))
                copies[-1].start()
            else:
                o[...] = both
        for step in range(1, 8):
            if step % 3 == 1:
                yield
            copies[7 + step].wait_recv()
            o[...] += got[lax.rem(p.chip + 8 - step, 8)].astype(F32)
        for copy in copies:
            copy.wait_send()


class SumCtx:
    def __init__(self, array):
        _, _, rows, width = array.shape
        self.arrays, self.groups = [array], {"chips", "twin"}
        self.outs = [jax.ShapeDtypeStruct(array.shape, BF)]
        self.in_spaces, self.out_spaces = [pltpu.VMEM], [pltpu.VMEM]
        self.scratch = [pltpu.VMEM((8, rows, width), BF)] * 3 + [pltpu.SemaphoreType.DMA((2, 23))]

    def run(self, p, ins, outs, scratch):
        (x,), (o,), (pair, sums, got, sems) = ins, outs, scratch
        first = remote(x.at[:, 1 - p.core], pair, sems, 0, p.twin)
        first.start()
        first.wait_recv()
        copies = [first]
        for step in range(1, 8):
            chip = lax.rem(p.chip + step, 8)
            sums[chip] = (x[chip, p.core].astype(F32) + pair[chip].astype(F32)).astype(BF)
            copies.append(remote(sums.at[chip], got.at[p.chip], sems, step, p.chips(step)))
            copies[-1].start()
        total = x[p.chip, p.core].astype(F32) + pair[p.chip].astype(F32)
        yield
        for step in range(1, 8):
            copies[step].wait_recv()
            total = total + got[lax.rem(p.chip + 8 - step, 8)].astype(F32)
        o[p.chip, p.core] = total.astype(BF)
        mine = o.at[p.chip, p.core]
        spread = []
        for step in range(1, 8):
            spread.append(remote(mine, mine, sems, 7 + step, p.chips(step)))
            spread[-1].start()
        passed = [remote(mine, mine, sems, 15, p.twin)]
        passed[0].start()
        yield
        for step in range(1, 8):
            spread[step - 1].wait_recv()
            piece = o.at[lax.rem(p.chip + 8 - step, 8), p.core]
            passed.append(remote(piece, piece, sems, 15 + step, p.twin))
            passed[-1].start()
        for copy in copies + spread:
            copy.wait_send()
        for copy in passed:
            copy.wait()


class ShareCtx:
    def __init__(self, array):
        self.arrays, self.groups = [array], {"chips", "twin", "others"}
        self.outs = [jax.ShapeDtypeStruct((16,) + array.shape, array.dtype)]
        self.in_spaces, self.out_spaces = [pl.ANY], [pl.ANY]
        self.scratch = [pltpu.SemaphoreType.DMA((2, 15)), pltpu.SemaphoreType.DMA]

    def run(self, p, ins, outs, scratch):
        (x,), (o,), (sems, own) = ins, outs, scratch
        copies = []
        for step in range(1, 16):
            to = {"ctx": lax.rem(p.ctx + step, 16)}
            copies.append(remote(x, o.at[p.ctx], sems, step - 1, to))
            copies[-1].start()
        copies.append(pltpu.make_async_copy(x, o.at[p.ctx], own))
        copies[-1].start()
        yield
        yield
        for copy in copies:
            copy.wait()


def transfer_kernel(parts, *refs):
    place = Place()
    groups = set().union(*(part.groups for part in parts))
    if "others" in groups:
        groups = groups - {"twin"}
    meet(place, groups)
    refs = list(refs)

    def take(count):
        taken = refs[:count]
        del refs[:count]
        return taken

    ins = [take(len(part.arrays)) for part in parts]
    outs = [take(len(part.outs)) for part in parts]
    scratch = [take(len(part.scratch)) for part in parts]
    active = [part.run(place, i, o, s) for part, i, o, s in zip(parts, ins, outs, scratch)]
    while active:
        active = [run for run in active if next(run, "end") != "end"]


def transfer(cid, name, us, *parts):
    spec = lambda space: pl.BlockSpec(memory_space=space)
    return pl.pallas_call(
        functools.partial(transfer_kernel, parts),
        out_shape=[out for part in parts for out in part.outs],
        in_specs=[spec(s) for part in parts for s in part.in_spaces],
        out_specs=[spec(s) for part in parts for s in part.out_spaces],
        scratch_shapes=[s for part in parts for s in part.scratch],
        compiler_params=pltpu.CompilerParams(
            collective_id=cid, has_side_effects=True, vmem_limit_bytes=40 * 2**20
        ),
        cost_estimate=cost(us),
        name=name,
    )(*[array for part in parts for array in part.arrays])


def interleave_kernel(gate_ref, up_ref, out_ref):
    out_ref[:, 0, :] = gate_ref[...].astype(F32)
    out_ref[:, 1, :] = up_ref[...].astype(F32)


def interleave(gate, up):
    rows, width = gate.shape
    step = 96
    spec = pl.BlockSpec((step, width), lambda i: (i, 0))
    return pl.pallas_call(
        interleave_kernel,
        grid=(rows // step,),
        out_shape=jax.ShapeDtypeStruct((rows, 2, width), F32),
        in_specs=[spec, spec],
        out_specs=pl.BlockSpec((step, 2, width), lambda i: (i, 0, 0)),
        cost_estimate=cost(6),
        name="interleave",
    )(gate, up)


NT = (((1,), (1,)), ((), ()))
TN = (((0,), (0,)), ((), ()))


def dot(a, b, dims):
    return lax.dot_general(a, b, dims, preferred_element_type=F32)


def masked_scores(q, keys, block, ctx, tokens):
    scores = dot(q, keys, NT)
    row = lax.rem(lax.broadcasted_iota(jnp.int32, scores.shape, 0), tokens) + ctx * tokens
    col = lax.broadcasted_iota(jnp.int32, scores.shape, 1) + block * KB
    return jnp.where(col <= row, scores, MASKED)


def attend_kernel(tokens, q_ref, kv_ref, out_ref, lse_ref, top, total, accum):
    ctx = lax.axis_index("ctx")
    last = (ctx * tokens) // KB
    q = q_ref[...]

    def block_of(index):
        return pl.ds(pl.multiple_of(index * KB, KB), KB)

    scores = masked_scores(q, kv_ref[block_of(last), :HD], last, ctx, tokens)
    start = jnp.max(scores, axis=-1, keepdims=True)
    probs = jnp.exp(scores - start)
    top[...] = jnp.broadcast_to(start, top.shape)
    total[...] = jnp.broadcast_to(jnp.sum(probs, axis=-1, keepdims=True), total.shape)
    accum[...] = jnp.dot(
        probs.astype(BF), kv_ref[block_of(last), HD:], preferred_element_type=F32
    )

    def body(index, carry):
        scores = dot(q, kv_ref[block_of(index), :HD], NT)
        old = top[:, :1]
        new = jnp.maximum(old, jnp.max(scores, axis=-1, keepdims=True))
        probs = jnp.exp(scores - new)
        keep = jnp.exp(old - new)
        top[...] = jnp.broadcast_to(new, top.shape)
        total[...] = total[...] * keep + jnp.sum(probs, axis=-1, keepdims=True)
        accum[...] = accum[...] * keep + jnp.dot(
            probs.astype(BF), kv_ref[block_of(index), HD:], preferred_element_type=F32
        )
        return carry

    lax.fori_loop(0, last, body, 0)
    out_ref[...] = accum[...] / total[:, :1]
    lse_ref[...] = top[...] + jnp.log(total[...])


def attend(q, kv, tokens):
    rows = q.shape[0]
    return pl.pallas_call(
        functools.partial(attend_kernel, tokens),
        out_shape=[
            jax.ShapeDtypeStruct((rows, HD), F32),
            jax.ShapeDtypeStruct((rows, 128), F32),
        ],
        scratch_shapes=[
            pltpu.VMEM((rows, 128), F32),
            pltpu.VMEM((rows, 128), F32),
            pltpu.VMEM((rows, HD), F32),
        ],
        compiler_params=pltpu.CompilerParams(vmem_limit_bytes=40 * 2**20),
        cost_estimate=cost(12),
        name="attend",
    )(q, kv)


def attend_back_kernel(tokens, q_ref, kv_ref, out_ref, lse_ref, d_ref, dq_ref, dkv_ref):
    ctx = lax.axis_index("ctx")
    last = (ctx * tokens) // KB
    q = q_ref[...]
    d_out = d_ref[...]
    lse = lse_ref[:, :1]
    delta = jnp.sum(d_out.astype(F32) * out_ref[...], axis=-1, keepdims=True)

    def block_of(index):
        return pl.ds(pl.multiple_of(index * KB, KB), KB)

    def work(index, scores):
        block = block_of(index)
        probs = jnp.exp(scores - lse)
        d_probs = dot(d_out, kv_ref[block, HD:], NT)
        d_scores = (probs * (d_probs - delta)).astype(BF)
        dkv_ref[block, :HD] = dot(d_scores, q, TN).astype(BF)
        dkv_ref[block, HD:] = dot(probs.astype(BF), d_out, TN).astype(BF)
        return jnp.dot(d_scores, kv_ref[block, :HD], preferred_element_type=F32)

    dq_ref[...] = work(last, masked_scores(q, kv_ref[block_of(last), :HD], last, ctx, tokens))

    def body(index, carry):
        dq_ref[...] += work(index, dot(q, kv_ref[block_of(index), :HD], NT))
        return carry

    lax.fori_loop(0, last, body, 0)

    def clear(index, carry):
        dkv_ref[block_of(index), :] = jnp.zeros((KB, 2 * HD), BF)
        return carry

    lax.fori_loop(last + 1, kv_ref.shape[0] // KB, clear, 0)


def attend_back(q, kv, out, lse, d_out, tokens):
    return pl.pallas_call(
        functools.partial(attend_back_kernel, tokens),
        out_shape=[
            jax.ShapeDtypeStruct(q.shape, F32),
            jax.ShapeDtypeStruct(kv.shape, BF),
        ],
        compiler_params=pltpu.CompilerParams(vmem_limit_bytes=40 * 2**20),
        cost_estimate=cost(20),
        name="attend_back",
    )(q, kv, out, lse, d_out)


def scale_of(values):
    return lax.rsqrt(jnp.mean(values * values, axis=-1, keepdims=True) + EPS)


def norm_back(v, r, g, dy):
    gdy = g * dy
    dv = r * gdy - v * (r * r * r) * jnp.mean(gdy * v, axis=-1, keepdims=True)
    return dv, dy * v * r


def rope(v, cosine, sine):
    a, b = v[..., : HD // 2], v[..., HD // 2 :]
    return jnp.concatenate([a * cosine - b * sine, b * cosine + a * sine], axis=-1)


def rope_back(u, cosine, sine):
    a, b = u[..., : HD // 2], u[..., HD // 2 :]
    return jnp.concatenate([a * cosine + b * sine, b * cosine - a * sine], axis=-1)


def on_device(hidden, w_qkv, w_out, norm_gains, qk_gains, w_gate_up, w_down, cotangent):
    tokens = hidden.shape[1]
    width = hidden.shape[2]
    x = hidden[0].astype(F32)
    cot = cotangent[0].astype(F32)
    positions = lax.axis_index("ctx") * tokens + jnp.arange(tokens, dtype=jnp.int32)
    freqs = ROPE_BASE ** (-jnp.arange(0, HD, 2, dtype=F32) / HD)
    angles = positions.astype(F32)[:, None] * freqs[None, :]
    cosine, sine = jnp.cos(angles), jnp.sin(angles)

    gain_part, qk_part = norm_gains.shape[0], qk_gains.shape[0]
    packed = jnp.concatenate(
        [
            jnp.pad(norm_gains.T, ((0, 0), (0, 256 - gain_part))),
            jnp.pad(qk_gains.T, ((0, 10), (0, 256 - qk_part))),
        ]
    )
    all_qkv, all_out, all_packed = transfer(
        1, "gather_weights", 30,
        GatherWsh(w_qkv, pair=True), GatherWsh(w_out, pair=True), DirectWsh("gather", packed),
    )
    full_qkv, full_out = all_qkv.reshape(-1, width), all_out.reshape(-1, width)
    gains = all_packed[:, :4, :gain_part].transpose(1, 0, 2).reshape(4, width).astype(F32)
    qk_gain = all_packed[:, 4:6, :qk_part].transpose(1, 0, 2).reshape(2, HD).astype(F32)

    r0 = scale_of(x)
    normed = (x * r0 * gains[0]).astype(BF)
    mixed = dot(normed, full_qkv, NT)
    q_raw = mixed[:, : HEADS * HD].reshape(tokens, HEADS, HD).transpose(1, 0, 2)
    k_raw = mixed[:, HEADS * HD : (HEADS + 1) * HD]
    rq, rk = scale_of(q_raw), scale_of(k_raw)
    q_low = (rope(q_raw * rq * qk_gain[0], cosine, sine) * HD ** (-0.5)).astype(BF)
    q_low = q_low.reshape(HEADS * tokens, HD)
    k_low = rope(k_raw * rk * qk_gain[1], cosine, sine).astype(BF)
    local_kv = jnp.concatenate([k_low, mixed[:, (HEADS + 1) * HD :].astype(BF)], axis=1)
    whole_kv, normed_all = transfer(2, "gather_kv", 25, GatherCtx(local_kv), GatherWsh(normed))
    whole_kv, normed_all = whole_kv.reshape(-1, 2 * HD), normed_all.reshape(-1, width)

    out_heads, lse = attend(q_low, whole_kv, tokens)
    attended = out_heads.reshape(HEADS, tokens, HD).transpose(1, 0, 2).reshape(tokens, HEADS * HD)
    attended = attended.astype(BF)
    branch = jnp.dot(attended, full_out, preferred_element_type=F32)
    r1 = scale_of(branch)
    resid = x + branch * r1 * gains[1]
    r2 = scale_of(resid)
    normed2 = (resid * r2 * gains[2]).astype(BF)

    (n2_all,) = transfer(3, "gather_normed2", 24, GatherWsh(normed2))
    n2_all = n2_all.reshape(-1, width)
    w_gate, w_up = w_gate_up[:, 0], w_gate_up[:, 1]
    gate, up = dot(n2_all, w_gate, NT), dot(n2_all, w_up, NT)
    gelu, gelu_pull = jax.vjp(functools.partial(jax.nn.gelu, approximate=True), gate)
    inner = (gelu * up).astype(BF)
    terms = jnp.dot(inner, w_down, preferred_element_type=F32).astype(BF)
    (branch2,) = transfer(4, "scatter_branch2", 24, ScatterWsh(terms.reshape(8, tokens, width)))

    r3 = scale_of(branch2)
    output = (resid + branch2 * r3 * gains[3]).astype(BF)
    d_branch2, dg3 = norm_back(branch2, r3, gains[3], cot)
    (d2_all,) = transfer(5, "gather_d_branch2", 24, GatherWsh(d_branch2.astype(BF)))
    d2_all = d2_all.reshape(-1, width)
    d_inner = dot(d2_all, w_down, NT)
    d_gate = (gelu_pull(d_inner * up)[0]).astype(BF)
    d_up = (d_inner * gelu).astype(BF)
    terms = (
        jnp.dot(d_gate, w_gate, preferred_element_type=F32)
        + jnp.dot(d_up, w_up, preferred_element_type=F32)
    ).astype(BF)
    (d_normed2,) = transfer(6, "scatter_d_normed2", 24, ScatterWsh(terms.reshape(8, tokens, width)))
    ff_grads = lax.psum(
        (
            dot(d_gate, n2_all, TN).astype(BF),
            dot(d_up, n2_all, TN).astype(BF),
            dot(inner, d2_all, TN).astype(BF),
        ),
        "ctx",
    )

    d_more, dg2 = norm_back(resid, r2, gains[2], d_normed2)
    d_resid = cot + d_more
    d_branch, dg1 = norm_back(branch, r1, gains[1], d_resid)
    branch_low = d_branch.astype(BF)
    d_attended = dot(branch_low, full_out, NT).astype(BF)
    d_heads = d_attended.reshape(tokens, HEADS, HD).transpose(1, 0, 2).reshape(HEADS * tokens, HD)
    d_q, d_kv = attend_back(q_low, whole_kv, out_heads, lse, d_heads, tokens)
    qkv_part, out_part = w_qkv.shape[0], w_out.shape[0]
    own_kv, db_all, at_all = transfer(
        7, "scatter_d_kv", 30,
        ScatterCtx(d_kv.reshape(8, 2, tokens, 2 * HD)),
        GatherWsh(branch_low),
        DirectWsh("scatter", attended.reshape(tokens, 8, out_part).transpose(1, 0, 2)),
    )
    grad_out = dot(at_all.reshape(-1, out_part), db_all.reshape(-1, width), TN)

    dq_rot = rope_back(d_q.reshape(HEADS, tokens, HD) * HD ** (-0.5), cosine, sine)
    d_q_raw, dgq = norm_back(q_raw, rq, qk_gain[0], dq_rot)
    dk_rot = rope_back(own_kv[:, :HD], cosine, sine)
    d_k_raw, dgk = norm_back(k_raw, rk, qk_gain[1], dk_rot)
    d_mixed = jnp.concatenate(
        [d_q_raw.transpose(1, 0, 2).reshape(tokens, HEADS * HD), d_k_raw, own_kv[:, HD:]], axis=1
    ).astype(BF)
    d_normed = jnp.dot(d_mixed, full_qkv, preferred_element_type=F32)
    d_input, dg0 = norm_back(x, r0, gains[0], d_normed)
    grad_hidden = (d_resid + d_input).astype(BF)

    dg = jnp.stack([jnp.sum(term, axis=0) for term in (dg0, dg1, dg2, dg3)])
    dqk = jnp.stack([jnp.sum(dgq, axis=(0, 1)), jnp.sum(dgk, axis=0)])
    dg = jnp.pad(dg.reshape(4, 8, gain_part).transpose(1, 0, 2), ((0, 0), (0, 0), (0, 256 - gain_part)))
    dqk = jnp.pad(dqk.reshape(2, 8, qk_part).transpose(1, 0, 2), ((0, 0), (0, 2), (0, 256 - qk_part)))
    dm_all, small_all = transfer(
        8, "columns_to_owners", 12,
        DirectWsh("scatter", d_mixed.reshape(tokens, 8, qkv_part).transpose(1, 0, 2)),
        DirectWsh("scatter", jnp.concatenate([dg, dqk], axis=1)),
    )
    grad_qkv = dot(dm_all.reshape(-1, qkv_part), normed_all, TN)
    both = jnp.concatenate([grad_qkv, grad_out], axis=0).astype(BF)
    share = both.shape[0] // 16
    room = -(-share // 16) * 16
    both = jnp.pad(both.reshape(8, 2, share, width), ((0, 0), (0, 0), (0, room - share), (0, 0)))
    grads, small_parts = transfer(
        9, "sum_grads", 25, SumCtx(both), ShareCtx(jnp.sum(small_all, axis=0))
    )
    grads = grads[:, :, :share].reshape(-1, width).astype(F32)
    small_sum = jnp.sum(small_parts, axis=0)
    return (
        output[None],
        grad_hidden[None],
        grads[:qkv_part],
        grads[qkv_part:],
        small_sum[:4, :gain_part].T,
        small_sum[4:6, :qk_part].T,
        interleave(ff_grads[0], ff_grads[1]),
        ff_grads[2].astype(F32),
    )


def solution(mesh):
    return jax.shard_map(
        on_device,
        mesh=mesh,
        in_specs=(
            P("wsh", "ctx", None),
            P("wsh", None),
            P("wsh", None),
            P("wsh", None),
            P("wsh", None),
            P("wsh", None, None),
            P("wsh", None),
            P("wsh", "ctx", None),
        ),
        out_specs=(
            P("wsh", "ctx", None),
            P("wsh", "ctx", None),
            P("wsh", None),
            P("wsh", None),
            P("wsh", None),
            P("wsh", None),
            P("wsh", None, None),
            P("wsh", None),
        ),
        check_vma=False,
    )
```

```python
import functools
import math

import jax
import jax.numpy as jnp
from jax import lax
from jax.experimental import pallas as pl
from jax.experimental.pallas import tpu as pltpu
from jax.sharding import PartitionSpec as P

HEADS = 4
HD = 256
KB = 512
EPS = 1e-06
ROPE_BASE = 1000000.0
MASKED = -1e30
MESH = pl.DeviceIdType.MESH
BF = jnp.bfloat16
F32 = jnp.float32
HBM = pltpu.HBM


def cost(us):
    return pl.CostEstimate(flops=0, bytes_accessed=int(us * 3.0e6), transcendentals=0)


class Grid:
    def __init__(self, axis, index, core):
        self.axis, self.core = axis, core
        self.h, self.y = lax.div(index, 4), lax.rem(index, 4)
        self.yp, self.ym, self.y2 = (lax.rem(self.y + k, 4) for k in (1, 3, 2))
        self.up, self.down = self.device(self.h, self.yp), self.device(self.h, self.ym)
        self.across = self.device(1 - self.h, self.y)

    def block(self, h, y):
        return h * 4 + y if self.axis == "wsh" else (h * 4 + y) * 2 + self.core

    def device(self, h, y):
        return {self.axis: self.block(h, y)}


class Place:
    def __init__(self):
        self.ctx, self.wsh = lax.axis_index("ctx"), lax.axis_index("wsh")
        self.chip, self.core = lax.div(self.ctx, 2), lax.rem(self.ctx, 2)
        self.grids = {"wsh": Grid("wsh", self.wsh, 0), "ctx": Grid("ctx", self.chip, self.core)}
        self.twin = {"ctx": self.ctx + 1 - 2 * self.core}

    def chips(self, step):
        return {"ctx": lax.rem(self.ctx + 2 * step, 16)}

    def row(self, step):
        return {"wsh": lax.rem(self.wsh + step, 8)}

    def peers(self, groups):
        found = []
        for axis, whole in (("wsh", "row"), ("ctx", "chips")):
            if axis in groups and whole not in groups:
                grid = self.grids[axis]
                found += [grid.up, grid.down, grid.across]
        if "row" in groups:
            found += [self.row(step) for step in range(1, 8)]
        if "chips" in groups:
            found += [self.chips(step) for step in range(1, 8)]
        if "others" in groups:
            found += [{"ctx": lax.rem(self.ctx + 2 * s + 1, 16)} for s in range(8)]
        elif "twin" in groups:
            found.append(self.twin)
        return found


def remote(src, dst, sems, i, device):
    return pltpu.make_async_remote_copy(
        src_ref=src, dst_ref=dst, send_sem=sems.at[0, i], recv_sem=sems.at[1, i],
        device_id=device, device_id_type=MESH,
    )


def meet(place, groups):
    barrier = pltpu.get_barrier_semaphore()
    peers = place.peers(groups)
    for peer in peers:
        pl.semaphore_signal(barrier, inc=1, device_id=peer, device_id_type=MESH)
    pl.semaphore_wait(barrier, len(peers))


def split_rows(count):
    return (count // 2 + 15) // 16 * 16


class Gather:
    def __init__(self, array, axis="wsh", pair=False):
        self.arrays, self.axis, self.pair = [array], axis, pair
        self.twins = pair or axis == "ctx"
        self.groups = {axis, "twin"} if self.twins else {axis}
        count = 16 if axis == "ctx" else 8
        self.outs = [jax.ShapeDtypeStruct((count,) + array.shape, array.dtype)]
        self.out_spaces, self.in_spaces = [HBM], [HBM]
        self.scratch = [pltpu.SemaphoreType.DMA((2, 19)), pltpu.SemaphoreType.DMA]

    def run(self, p, ins, outs, scratch):
        (x,), (o,), (sems, own) = ins, outs, scratch
        g = p.grids[self.axis]
        size = x.shape[0] // (2 if self.pair else 1)
        base = pl.multiple_of(p.core * size, size) if self.pair else 0
        half = split_rows(size)
        every, low, high = pl.ds(base, size), pl.ds(base, half), pl.ds(base + half, size - half)
        h, other = g.h, 1 - g.h
        me = g.block(h, g.y)
        copies = {}

        def send(i, block, rows, device, source=None):
            source = o.at[block, rows] if source is None else source
            copies[i] = remote(source, o.at[block, rows], sems, i, device)
            copies[i].start()

        def arrived(i, block, rows):
            copies[i].wait_recv()
            if self.twins:
                send(9 + i, block, rows, p.twin)

        send(2, me, every, g.across, x.at[every])
        send(0, me, every, g.up, x.at[every])
        send(1, me, every, g.down, x.at[every])
        if self.axis == "ctx":
            send(18, me, every, p.twin, x)
        local = pltpu.make_async_copy(x, o.at[me], own)
        local.start()
        yield
        block = g.block(other, g.y)
        arrived(2, block, every)
        send(5, block, every, g.up)
        send(6, block, every, g.down)
        yield
        block = g.block(h, g.ym)
        arrived(0, block, every)
        send(3, block, low, g.up)
        yield
        block = g.block(h, g.yp)
        arrived(1, block, every)
        send(4, block, high, g.down)
        yield
        block = g.block(other, g.ym)
        arrived(5, block, every)
        send(7, block, low, g.up)
        yield
        block = g.block(other, g.yp)
        arrived(6, block, every)
        send(8, block, high, g.down)
        yield
        block = g.block(h, g.y2)
        arrived(3, block, low)
        arrived(4, block, high)
        yield
        block = g.block(other, g.y2)
        arrived(7, block, low)
        arrived(8, block, high)
        yield
        for i, copy in copies.items():
            copy.wait_send()
            if i >= 9:
                copy.wait_recv()
        local.wait()


class Scatter:
    def __init__(self, array, axis="wsh", dtype=F32):
        _, rows, width = array.shape
        self.arrays, self.axis, self.groups = [array], axis, {axis}
        self.outs = [jax.ShapeDtypeStruct((rows, width), dtype)]
        self.in_spaces, self.out_spaces = [pltpu.VMEM], [pltpu.VMEM]
        half = split_rows(rows)
        low, high = pltpu.VMEM((2, half, width), BF), pltpu.VMEM((2, rows - half, width), BF)
        whole = pltpu.VMEM((2, rows, width), BF)
        self.scratch = [low, high, low, high, whole, whole, whole, pltpu.SemaphoreType.DMA((2, 13))]

    def run(self, p, ins, outs, scratch):
        (x,), (o,), (buf_a, buf_b, sum_c, sum_d, buf_c, buf_d, buf_e, sems) = ins, outs, scratch
        g = p.grids[self.axis]
        rows = o.shape[0]
        half = split_rows(rows)
        low, high = pl.ds(0, half), pl.ds(half, rows - half)
        planes = ((1 - g.h) * 4, g.h * 4)
        copies = {}

        def send(i, source, target, device):
            copies[i] = remote(source, target, sems, i, device)
            copies[i].start()

        for k, plane in enumerate(planes):
            send(k, x.at[plane + g.y2, low], buf_a.at[k], g.up)
            send(2 + k, x.at[plane + g.y2, high], buf_b.at[k], g.down)
            send(4 + k, x.at[plane + g.yp, high], buf_c.at[k, high], g.up)
            send(6 + k, x.at[plane + g.ym, low], buf_d.at[k, low], g.down)
        for k, plane in enumerate(planes):
            yield
            copies[k].wait_recv()
            sum_c[k] = (x[plane + g.yp, :half].astype(F32) + buf_a[k].astype(F32)).astype(BF)
            send(8 + k, sum_c.at[k], buf_c.at[k, low], g.up)
            yield
            copies[2 + k].wait_recv()
            sum_d[k] = (x[plane + g.ym, half:].astype(F32) + buf_b[k].astype(F32)).astype(BF)
            send(10 + k, sum_d.at[k], buf_d.at[k, high], g.down)
        for k, plane in enumerate(planes):
            yield
            for i in (4, 6, 8, 10):
                copies[i + k].wait_recv()
            total = x[plane + g.y].astype(F32) + buf_c[k].astype(F32) + buf_d[k].astype(F32)
            if k == 0:
                buf_e[0] = total.astype(BF)
                send(12, buf_e.at[0], buf_e.at[1], g.across)
            else:
                yield
                copies[12].wait_recv()
                o[...] = (total + buf_e[1].astype(F32)).astype(o.dtype)
        for copy in copies.values():
            copy.wait_send()


class DirectWsh:
    def __init__(self, mode, array):
        self.mode, self.arrays, self.groups = mode, [array], {"row"}
        shape = ((8,) + array.shape) if mode == "gather" else array.shape
        self.outs = [jax.ShapeDtypeStruct(shape, array.dtype)]
        self.in_spaces, self.out_spaces = [HBM], [HBM]
        self.scratch = [pltpu.SemaphoreType.DMA((2, 7)), pltpu.SemaphoreType.DMA]

    def run(self, p, ins, outs, scratch):
        (x,), (o,), (sems, own) = ins, outs, scratch
        pick = (lambda i: x) if self.mode == "gather" else (lambda i: x.at[i])
        copies = []
        for step in range(1, 8):
            to = p.row(step)
            copies.append(remote(pick(to["wsh"]), o.at[p.wsh], sems, step - 1, to))
            copies[-1].start()
        copies.append(pltpu.make_async_copy(pick(p.wsh), o.at[p.wsh], own))
        copies[-1].start()
        yield
        yield
        yield
        for copy in copies:
            copy.wait()


class ScatterCtx:
    def __init__(self, array):
        _, _, rows, width = array.shape
        self.arrays, self.groups = [array], {"chips", "twin"}
        self.outs = [jax.ShapeDtypeStruct((rows, width), F32)]
        self.in_spaces, self.out_spaces = [pltpu.VMEM], [pltpu.VMEM]
        self.scratch = [pltpu.VMEM((8, rows, width), BF)] * 3 + [pltpu.SemaphoreType.DMA((2, 15))]

    def run(self, p, ins, outs, scratch):
        (x,), (o,), (pair, sums, got, sems) = ins, outs, scratch
        copies = []
        order = list(range(1, 8)) + [0]
        for i, step in enumerate(order):
            chip = lax.rem(p.chip + step, 8)
            copies.append(remote(x.at[chip, 1 - p.core], pair.at[chip], sems, i, p.twin))
            copies[-1].start()
        for i, step in enumerate(order):
            if i % 3 == 0:
                yield
            chip = lax.rem(p.chip + step, 8)
            copies[i].wait_recv()
            both = x[chip, p.core].astype(F32) + pair[chip].astype(F32)
            if step > 0:
                sums[chip] = both.astype(BF)
                copies.append(remote(sums.at[chip], got.at[p.chip], sems, 7 + step, p.chips(step)))
                copies[-1].start()
            else:
                o[...] = both
        for step in range(1, 8):
            if step % 3 == 1:
                yield
            copies[7 + step].wait_recv()
            o[...] += got[lax.rem(p.chip + 8 - step, 8)].astype(F32)
        for copy in copies:
            copy.wait_send()


class SumCtx:
    def __init__(self, array):
        _, _, rows, width = array.shape
        self.arrays, self.groups = [array], {"chips", "twin"}
        self.outs = [jax.ShapeDtypeStruct(array.shape, BF)]
        self.in_spaces, self.out_spaces = [pltpu.VMEM], [pltpu.VMEM]
        self.scratch = [pltpu.VMEM((8, rows, width), BF)] * 3 + [pltpu.SemaphoreType.DMA((2, 23))]

    def run(self, p, ins, outs, scratch):
        (x,), (o,), (pair, sums, got, sems) = ins, outs, scratch
        first = remote(x.at[:, 1 - p.core], pair, sems, 0, p.twin)
        first.start()
        first.wait_recv()
        copies = [first]
        for step in range(1, 8):
            chip = lax.rem(p.chip + step, 8)
            sums[chip] = (x[chip, p.core].astype(F32) + pair[chip].astype(F32)).astype(BF)
            copies.append(remote(sums.at[chip], got.at[p.chip], sems, step, p.chips(step)))
            copies[-1].start()
        total = x[p.chip, p.core].astype(F32) + pair[p.chip].astype(F32)
        yield
        for step in range(1, 8):
            copies[step].wait_recv()
            total = total + got[lax.rem(p.chip + 8 - step, 8)].astype(F32)
        o[p.chip, p.core] = total.astype(BF)
        mine = o.at[p.chip, p.core]
        spread = []
        for step in range(1, 8):
            spread.append(remote(mine, mine, sems, 7 + step, p.chips(step)))
            spread[-1].start()
        passed = [remote(mine, mine, sems, 15, p.twin)]
        passed[0].start()
        yield
        for step in range(1, 8):
            spread[step - 1].wait_recv()
            piece = o.at[lax.rem(p.chip + 8 - step, 8), p.core]
            passed.append(remote(piece, piece, sems, 15 + step, p.twin))
            passed[-1].start()
        for copy in copies + spread:
            copy.wait_send()
        for copy in passed:
            copy.wait()


class ShareCtx:
    def __init__(self, array):
        self.arrays, self.groups = [array], {"chips", "twin", "others"}
        self.outs = [jax.ShapeDtypeStruct((16,) + array.shape, array.dtype)]
        self.in_spaces, self.out_spaces = [HBM], [HBM]
        self.scratch = [pltpu.SemaphoreType.DMA((2, 15)), pltpu.SemaphoreType.DMA]

    def run(self, p, ins, outs, scratch):
        (x,), (o,), (sems, own) = ins, outs, scratch
        copies = []
        for step in range(1, 16):
            to = {"ctx": lax.rem(p.ctx + step, 16)}
            copies.append(remote(x, o.at[p.ctx], sems, step - 1, to))
            copies[-1].start()
        copies.append(pltpu.make_async_copy(x, o.at[p.ctx], own))
        copies[-1].start()
        yield
        yield
        for copy in copies:
            copy.wait()


def rows_loop(count, body):
    lax.fori_loop(0, count // 16, lambda i, _: (body(pl.ds(pl.multiple_of(i * 16, 16), 16)), 0)[1], 0)


class FeedForwardGrads:
    def __init__(self, d_gate, d_up, inner, normed, d_branch):
        units, width = d_gate.shape[1], normed.shape[1]
        self.arrays, self.groups = [d_gate, d_up, inner, normed, d_branch], {"ctx", "twin"}
        granules = -(-3 * units // 256)
        early = granules * 5 // 9
        self.pieces = (early * 16, (granules - early) * 16)
        sums = [pltpu.VMEM((8, rows, width), BF) for rows in self.pieces]
        late = jax.ShapeDtypeStruct(sums[1].shape, BF)
        self.scatter = Scatter(jax.ShapeDtypeStruct(sums[0].shape, BF), "ctx", BF)
        self.outs = self.scatter.outs + [late]
        self.in_spaces, self.out_spaces = [pltpu.VMEM] * 5, [pltpu.VMEM] * 2
        self.scratch = [pltpu.VMEM((16 * rows, width), BF) for rows in self.pieces]
        self.scratch += sums + sums[:1] + [pltpu.SemaphoreType.DMA((2, 16))] + self.scatter.scratch

    def run(self, p, ins, outs, scratch):
        d_gate, d_up, inner, normed, d_branch = ins
        first, second, pair_first, pair_second, sums, sems, *rest = scratch
        units = d_gate.shape[1]
        split = first.shape[0]
        twins = []

        def put(at, value):
            end = at + value.shape[0]
            if at < split:
                first[at : min(end, split)] = value[: min(end, split) - at]
            if end > split:
                second[max(at, split) - split : end - split] = value[max(at, split) - at :]

        def swap(whole, pair, number):
            size = pair.shape[1]
            for chip in range(8):
                there = pl.ds(pl.multiple_of((2 * chip + 1 - p.core) * size, 16), size)
                twins.append(remote(whole.at[there], pair.at[chip], sems, 8 * number + chip, p.twin))
                twins[-1].start()

        def add(whole, pair, result, number):
            size = pair.shape[1]
            for chip in range(8):
                here = pl.ds(pl.multiple_of((2 * chip + p.core) * size, 16), size)
                twins[8 * number + chip].wait_recv()
                result[chip] = (whole[here].astype(F32) + pair[chip].astype(F32)).astype(BF)

        yield
        started = False
        for number, (left, right) in enumerate(((d_gate, normed), (d_up, normed), (inner, d_branch))):
            for start in range(0, units, 256):
                stop = min(start + 256, units)
                put(number * units + start, dot(left[:, start:stop], right[...], TN).astype(BF))
                if not started and number * units + stop >= split:
                    started = True
                    swap(first, pair_first, 0)
            yield
        missing = second.shape[0] - (3 * units - split)
        if missing:
            second[second.shape[0] - missing :] = jnp.zeros((missing, second.shape[1]), BF)
        swap(second, pair_second, 1)
        add(first, pair_first, sums, 0)
        middle = self.scatter.run(p, [sums], outs[:1], rest)
        next(middle)
        add(second, pair_second, outs[1], 1)
        yield
        yield from middle
        for copy in twins:
            copy.wait_send()


class Unpair:
    def __init__(self, array):
        self.arrays, self.groups = [array], set()
        self.outs = [jax.ShapeDtypeStruct((array.shape[0], array.shape[2]), BF)] * 2
        self.in_spaces, self.out_spaces, self.scratch = [pltpu.VMEM], [pltpu.VMEM] * 2, []

    def run(self, p, ins, outs, scratch):
        def step(rows):
            outs[0][rows] = ins[0][rows, 0, :]
            outs[1][rows] = ins[0][rows, 1, :]

        rows_loop(ins[0].shape[0], step)
        yield


class Tables:
    def __init__(self, tokens):
        self.tokens, self.arrays, self.groups = tokens, [], set()
        self.outs = [jax.ShapeDtypeStruct((tokens, HD // 2), F32)] * 2
        self.in_spaces, self.out_spaces, self.scratch = [], [pltpu.VMEM] * 2, []

    def run(self, p, ins, outs, scratch):
        shape = outs[0].shape
        token = lax.broadcasted_iota(jnp.int32, shape, 0) + p.ctx * self.tokens
        power = lax.broadcasted_iota(jnp.int32, shape, 1).astype(F32) * (-2.0 / HD)
        angles = token.astype(F32) * jnp.exp(power * math.log(ROPE_BASE))
        outs[0][...] = jnp.cos(angles)
        outs[1][...] = jnp.sin(angles)
        yield


def transfer_kernel(parts, *refs):
    place = Place()
    groups = set().union(*(part.groups for part in parts))
    if "others" in groups:
        groups = groups - {"twin"}
    meet(place, groups)
    refs = list(refs)

    def take(count):
        taken = refs[:count]
        del refs[:count]
        return taken

    ins = [take(len(part.arrays)) for part in parts]
    outs = [take(len(part.outs)) for part in parts]
    scratch = [take(len(part.scratch)) for part in parts]
    active = [part.run(place, i, o, s) for part, i, o, s in zip(parts, ins, outs, scratch)]
    while active:
        active = [run for run in active if next(run, "end") != "end"]


def transfer(cid, name, us, *parts):
    spec = lambda space: pl.BlockSpec(memory_space=space)
    return pl.pallas_call(
        functools.partial(transfer_kernel, parts),
        out_shape=[out for part in parts for out in part.outs],
        in_specs=[spec(s) for part in parts for s in part.in_spaces],
        out_specs=[spec(s) for part in parts for s in part.out_spaces],
        scratch_shapes=[s for part in parts for s in part.scratch],
        compiler_params=pltpu.CompilerParams(
            collective_id=cid, has_side_effects=True, vmem_limit_bytes=48 * 2**20
        ),
        cost_estimate=cost(us),
        name=name,
    )(*[array for part in parts for array in part.arrays])


NT = (((1,), (1,)), ((), ()))
TN = (((0,), (0,)), ((), ()))


def dot(a, b, dims):
    return lax.dot_general(a, b, dims, preferred_element_type=F32)


def masked_scores(q, keys, block, ctx, tokens):
    scores = dot(q, keys, NT)
    row = lax.rem(lax.broadcasted_iota(jnp.int32, scores.shape, 0), tokens) + ctx * tokens
    col = lax.broadcasted_iota(jnp.int32, scores.shape, 1) + block * KB
    return jnp.where(col <= row, scores, MASKED)


def widen_kernel(first, gate_ref, up_ref, more_ref, low_ref, both_ref, down_ref):
    both_ref[:, 0, :] = gate_ref[...].astype(F32)
    down_ref[...] = low_ref[...].astype(F32)

    @pl.when(pl.program_id(0) < first)
    def _():
        both_ref[:, 1, :] = up_ref[...].astype(F32)

    @pl.when(pl.program_id(0) >= first)
    def _():
        both_ref[:, 1, :] = more_ref[...].astype(F32)


def widen(early, late, rows):
    width = early.shape[1]
    step = 96
    count = rows // step
    first = early.shape[0] // step - count
    spec = lambda index: pl.BlockSpec((step, width), lambda i: (index(i), 0))
    return pl.pallas_call(
        functools.partial(widen_kernel, first),
        grid=(count,),
        out_shape=[
            jax.ShapeDtypeStruct((rows, 2, width), F32),
            jax.ShapeDtypeStruct((rows, width), F32),
        ],
        in_specs=[
            spec(lambda i: i),
            spec(lambda i: jnp.minimum(i, first - 1) + count),
            spec(lambda i: jnp.maximum(i - first, 0)),
            spec(lambda i: i + count - first),
        ],
        out_specs=[pl.BlockSpec((step, 2, width), lambda i: (i, 0, 0)), spec(lambda i: i)],
        cost_estimate=cost(9),
        name="widen",
    )(early, early, late, late)


def scale_of(values):
    return lax.rsqrt(jnp.mean(values * values, axis=-1, keepdims=True) + EPS)


def norm_back(v, r, g, dy):
    gdy = g * dy
    dv = r * gdy - v * (r * r * r) * jnp.mean(gdy * v, axis=-1, keepdims=True)
    return dv, dy * v * r


def rope(v, cosine, sine):
    a, b = v[..., : HD // 2], v[..., HD // 2 :]
    return jnp.concatenate([a * cosine - b * sine, b * cosine + a * sine], axis=-1)


def rope_back(u, cosine, sine):
    a, b = u[..., : HD // 2], u[..., HD // 2 :]
    return jnp.concatenate([a * cosine + b * sine, b * cosine - a * sine], axis=-1)


def compute(kernel, name, us, outs, scratch, *args):
    return pl.pallas_call(
        kernel,
        out_shape=[jax.ShapeDtypeStruct(shape, dtype) for shape, dtype in outs],
        scratch_shapes=scratch,
        compiler_params=pltpu.CompilerParams(vmem_limit_bytes=28 * 2**20),
        cost_estimate=cost(us),
        name=name,
    )(*args)


def tiled(kernel, name, us, widths, rowed, whole):
    rows, step = rowed[0].shape[0], 256
    spec = lambda width: pl.BlockSpec((step, width), lambda i: (i, 0))
    return pl.pallas_call(
        kernel,
        grid=(rows // step,),
        out_shape=[jax.ShapeDtypeStruct((rows, width), BF) for width in widths],
        in_specs=[spec(a.shape[1]) for a in rowed]
        + [pl.BlockSpec(a.shape, lambda i: (0, 0)) for a in whole],
        out_specs=[spec(width) for width in widths],
        compiler_params=pltpu.CompilerParams(vmem_limit_bytes=40 * 2**20),
        cost_estimate=cost(us),
        name=name,
    )(*rowed, *whole)


def forward_kernel(n_ref, gate_ref, up_ref, down_ref, inner_ref, gelu_ref, slope_ref, terms_ref):
    gate = dot(n_ref[...], gate_ref[...], NT)
    up = dot(n_ref[...], up_ref[...], NT)
    bend, grow = math.sqrt(2.0 / math.pi), 0.044715
    square = gate * gate
    wave = jnp.tanh(bend * gate * (1.0 + grow * square))
    rise = 0.5 * (1.0 + wave)
    gelu = gate * rise
    slope = rise + 0.5 * bend * gate * (1.0 - wave * wave) * (1.0 + 3.0 * grow * square)
    gelu_ref[...] = gelu.astype(BF)
    slope_ref[...] = (up * slope).astype(BF)
    inner_ref[...] = (gelu * up).astype(BF)
    terms_ref[...] = jnp.dot(inner_ref[...], down_ref[...], preferred_element_type=F32).astype(BF)


def backward_kernel(d_ref, gelu_ref, slope_ref, gate_ref, up_ref, down_ref, dgate_ref, dup_ref, terms_ref):
    d_inner = dot(d_ref[...], down_ref[...], NT)
    dgate_ref[...] = (d_inner * slope_ref[...].astype(F32)).astype(BF)
    dup_ref[...] = (d_inner * gelu_ref[...].astype(F32)).astype(BF)
    terms_ref[...] = (
        jnp.dot(dgate_ref[...], gate_ref[...], preferred_element_type=F32)
        + jnp.dot(dup_ref[...], up_ref[...], preferred_element_type=F32)
    ).astype(BF)


def prepare_kernel(x_ref, w_ref, g_ref, qk_ref, cos_ref, sin_ref, normed_ref, raw_ref, q_ref, kv_ref):
    x = x_ref[...].astype(F32)
    tokens = x.shape[0]
    normed = (x * scale_of(x) * g_ref[0:1]).astype(BF)
    normed_ref[...] = normed
    raw_ref[...] = dot(normed, w_ref[...], NT)
    cosine, sine = cos_ref[...], sin_ref[...]
    for head in range(HEADS + 1):
        v = raw_ref[:, head * HD : (head + 1) * HD]
        column = 0 if head < HEADS else 1
        turned = rope(v * scale_of(v) * qk_ref[column : column + 1], cosine, sine)
        if head < HEADS:
            q_ref[head * tokens : (head + 1) * tokens] = (turned * HD ** (-0.5)).astype(BF)
        else:
            kv_ref[:, :HD] = turned.astype(BF)
    kv_ref[:, HD:] = raw_ref[:, (HEADS + 1) * HD :].astype(BF)


def attend_kernel(q_ref, kv_ref, x_ref, w_ref, g_ref, out_ref, lse_ref, att_ref, branch_ref,
                  resid_ref, normed_ref, top, total, accum):
    ctx = lax.axis_index("ctx")
    tokens = x_ref.shape[0]
    last = lax.div(ctx * tokens, KB)
    q = q_ref[...]

    def block_of(index):
        return pl.ds(pl.multiple_of(index * KB, KB), KB)

    scores = masked_scores(q, kv_ref[block_of(last), :HD], last, ctx, tokens)
    start = jnp.max(scores, axis=-1, keepdims=True)
    probs = jnp.exp(scores - start)
    top[...] = jnp.broadcast_to(start, top.shape)
    total[...] = jnp.broadcast_to(jnp.sum(probs, axis=-1, keepdims=True), total.shape)
    accum[...] = jnp.dot(
        probs.astype(BF), kv_ref[block_of(last), HD:], preferred_element_type=F32
    )

    def body(index, carry):
        scores = dot(q, kv_ref[block_of(index), :HD], NT)
        old = top[:, :1]
        new = jnp.maximum(old, jnp.max(scores, axis=-1, keepdims=True))
        probs = jnp.exp(scores - new)
        keep = jnp.exp(old - new)
        top[...] = jnp.broadcast_to(new, top.shape)
        total[...] = total[...] * keep + jnp.sum(probs, axis=-1, keepdims=True)
        accum[...] = accum[...] * keep + jnp.dot(
            probs.astype(BF), kv_ref[block_of(index), HD:], preferred_element_type=F32
        )
        return carry

    lax.fori_loop(0, last, body, 0)
    out_ref[...] = accum[...] / total[:, :1]
    lse_ref[...] = top[...] + jnp.log(total[...])
    for head in range(HEADS):
        att_ref[:, head * HD : (head + 1) * HD] = out_ref[
            head * tokens : (head + 1) * tokens
        ].astype(BF)
    branch = jnp.dot(att_ref[...], w_ref[...], preferred_element_type=F32)
    branch_ref[...] = branch
    resid = x_ref[...].astype(F32) + branch * scale_of(branch) * g_ref[1:2]
    resid_ref[...] = resid
    normed_ref[...] = (resid * scale_of(resid) * g_ref[2:3]).astype(BF)


def attend_back_kernel(dn_ref, resid_ref, branch_ref, cot_ref, g_ref, w_ref, q_ref, kv_ref, out_ref,
                       lse_ref, dres_ref, low_ref, dg_ref, dq_ref, dkv_ref, d_ref):
    ctx = lax.axis_index("ctx")
    tokens = resid_ref.shape[0]
    last = lax.div(ctx * tokens, KB)
    resid = resid_ref[...]
    d_more, dg2 = norm_back(resid, scale_of(resid), g_ref[2:3], dn_ref[...])
    d_resid = cot_ref[...].astype(F32) + d_more
    dres_ref[...] = d_resid
    branch = branch_ref[...]
    d_branch, dg1 = norm_back(branch, scale_of(branch), g_ref[1:2], d_resid)
    low_ref[...] = d_branch.astype(BF)
    dg_ref[0:1] = jnp.sum(dg1, axis=0, keepdims=True)
    dg_ref[1:2] = jnp.sum(dg2, axis=0, keepdims=True)
    d_att = dot(low_ref[...], w_ref[...], NT)
    for head in range(HEADS):
        d_ref[head * tokens : (head + 1) * tokens] = d_att[:, head * HD : (head + 1) * HD].astype(BF)
    q = q_ref[...]
    d_out = d_ref[...]
    lse = lse_ref[:, :1]
    delta = jnp.sum(d_out.astype(F32) * out_ref[...], axis=-1, keepdims=True)

    def block_of(index):
        return pl.ds(pl.multiple_of(index * KB, KB), KB)

    def work(index, scores):
        block = block_of(index)
        probs = jnp.exp(scores - lse)
        d_probs = dot(d_out, kv_ref[block, HD:], NT)
        d_scores = (probs * (d_probs - delta)).astype(BF)
        dkv_ref[block, :HD] = dot(d_scores, q, TN).astype(BF)
        dkv_ref[block, HD:] = dot(probs.astype(BF), d_out, TN).astype(BF)
        return jnp.dot(d_scores, kv_ref[block, :HD], preferred_element_type=F32)

    dq_ref[...] = work(last, masked_scores(q, kv_ref[block_of(last), :HD], last, ctx, tokens))

    def body(index, carry):
        dq_ref[...] += work(index, dot(q, kv_ref[block_of(index), :HD], NT))
        return carry

    lax.fori_loop(0, last, body, 0)

    def clear(index, carry):
        dkv_ref[block_of(index), :] = jnp.zeros((KB, 2 * HD), BF)
        return carry

    lax.fori_loop(last + 1, kv_ref.shape[0] // KB, clear, 0)


def finish_kernel(own_ref, dq_ref, raw_ref, cos_ref, sin_ref, w_ref, x_ref, g_ref, qk_ref, dres_ref,
                  parts_ref, grad_ref, dg_ref, dqk_ref, mixed_ref):
    tokens = x_ref.shape[0]
    cosine, sine = cos_ref[...], sin_ref[...]
    total = jnp.zeros((1, HD), F32)
    for head in range(HEADS + 1):
        v = raw_ref[:, head * HD : (head + 1) * HD]
        if head < HEADS:
            u = dq_ref[head * tokens : (head + 1) * tokens] * HD ** (-0.5)
        else:
            u = own_ref[:, :HD]
        column = 0 if head < HEADS else 1
        dv, dg = norm_back(
            v, scale_of(v), qk_ref[column : column + 1], rope_back(u, cosine, sine)
        )
        mixed_ref[:, head * HD : (head + 1) * HD] = dv.astype(BF)
        dg = jnp.sum(dg, axis=0, keepdims=True)
        if head < HEADS:
            total = total + dg
        else:
            dqk_ref[0:1] = total
            dqk_ref[1:2] = dg
    mixed_ref[:, (HEADS + 1) * HD :] = own_ref[:, HD:].astype(BF)
    d_mixed = mixed_ref[...]
    part = parts_ref.shape[2]
    for i in range(parts_ref.shape[0]):
        parts_ref[i] = d_mixed[:, i * part : (i + 1) * part]
    d_normed = jnp.dot(d_mixed, w_ref[...], preferred_element_type=F32)
    x = x_ref[...].astype(F32)
    d_input, dg0 = norm_back(x, scale_of(x), g_ref[0:1], d_normed)
    dg_ref[...] = jnp.sum(dg0, axis=0, keepdims=True)
    grad_ref[...] = (dres_ref[...] + d_input).astype(BF)


def on_device(hidden, w_qkv, w_out, norm_gains, qk_gains, w_gate_up, w_down, cotangent):
    tokens = hidden.shape[1]
    width = hidden.shape[2]
    cot = cotangent[0].astype(F32)
    gain_part, qk_part = norm_gains.shape[0], qk_gains.shape[0]
    packed = jnp.concatenate(
        [
            jnp.pad(norm_gains.T, ((0, 0), (0, 256 - gain_part))),
            jnp.pad(qk_gains.T, ((0, 10), (0, 256 - qk_part))),
        ]
    )
    all_packed, all_qkv, all_out, cosine, sine, w_gate, w_up = transfer(
        1, "gather_weights", 30,
        DirectWsh("gather", packed), Gather(w_qkv, pair=True), Gather(w_out, pair=True), Tables(tokens),
        Unpair(w_gate_up),
    )
    full_qkv, full_out = all_qkv.reshape(-1, width), all_out.reshape(-1, width)
    gains = all_packed[:, :4, :gain_part].transpose(1, 0, 2).reshape(4, width).astype(F32)
    qk_gain = all_packed[:, 4:6, :qk_part].transpose(1, 0, 2).reshape(2, HD).astype(F32)

    heads = HEADS * tokens
    normed, raw, q_low, local_kv = compute(
        prepare_kernel, "prepare", 6,
        [((tokens, width), BF), ((tokens, (HEADS + 2) * HD), F32), ((heads, HD), BF), ((tokens, 2 * HD), BF)],
        [], hidden[0], full_qkv, gains, qk_gain, cosine, sine,
    )
    normed_all, whole_kv = transfer(2, "gather_kv", 25, Gather(normed), Gather(local_kv, "ctx"))
    whole_kv, normed_all = whole_kv.reshape(-1, 2 * HD), normed_all.reshape(-1, width)
    out_heads, lse, attended, branch, resid, normed2 = compute(
        attend_kernel, "attend", 10,
        [((heads, HD), F32), ((heads, 128), F32), ((tokens, HEADS * HD), BF), ((tokens, width), F32),
         ((tokens, width), F32), ((tokens, width), BF)],
        [pltpu.VMEM((heads, 128), F32), pltpu.VMEM((heads, 128), F32), pltpu.VMEM((heads, HD), F32)],
        q_low, whole_kv, hidden[0], full_out, gains,
    )

    (n2_all,) = transfer(3, "gather_normed2", 24, Gather(normed2))
    n2_all = n2_all.reshape(-1, width)
    units = w_down.shape[0]
    inner, gelu, slope, terms = tiled(
        forward_kernel, "feed_forward", 10, [units, units, units, width], [n2_all], [w_gate, w_up, w_down]
    )
    (branch2,) = transfer(4, "scatter_branch2", 24, Scatter(terms.reshape(8, tokens, width)))

    r3 = scale_of(branch2)
    output = (resid + branch2 * r3 * gains[3]).astype(BF)
    d_branch2, dg3 = norm_back(branch2, r3, gains[3], cot)
    (d2_all,) = transfer(5, "gather_d_branch2", 24, Gather(d_branch2.astype(BF)))
    d2_all = d2_all.reshape(-1, width)
    d_gate, d_up, terms = tiled(
        backward_kernel, "feed_forward_back", 8, [units, units, width],
        [d2_all, gelu, slope], [w_gate, w_up, w_down],
    )
    d_normed2, ff_early, ff_sums = transfer(
        6, "scatter_d_normed2", 40,
        Scatter(terms.reshape(8, tokens, width)),
        FeedForwardGrads(d_gate, d_up, inner, n2_all, d2_all),
    )

    d_resid, branch_low, dg12, d_q, d_kv = compute(
        attend_back_kernel, "attend_back", 10,
        [((tokens, width), F32), ((tokens, width), BF), ((2, width), F32), ((heads, HD), F32),
         (whole_kv.shape, BF)],
        [pltpu.VMEM((heads, HD), BF)],
        d_normed2, resid, branch, cotangent[0], gains, full_out, q_low, whole_kv, out_heads, lse,
    )
    qkv_part, out_part = w_qkv.shape[0], w_out.shape[0]
    at_all, db_all, own_kv, ff_late = transfer(
        7, "scatter_d_kv", 30,
        DirectWsh("scatter", attended.reshape(tokens, 8, out_part).transpose(1, 0, 2)),
        Gather(branch_low),
        ScatterCtx(d_kv.reshape(8, 2, tokens, 2 * HD)),
        Scatter(ff_sums, "ctx", BF),
    )
    grad_out = dot(at_all.reshape(-1, out_part), db_all.reshape(-1, width), TN)
    d_mixed, grad_hidden, dg0, dqk, _ = compute(
        finish_kernel, "finish", 6,
        [((8, tokens, qkv_part), BF), ((tokens, width), BF), ((1, width), F32), ((2, HD), F32),
         ((tokens, (HEADS + 2) * HD), BF)],
        [], own_kv, d_q, raw, cosine, sine, full_qkv, hidden[0], gains, qk_gain, d_resid,
    )

    dg = jnp.concatenate([dg0, dg12, jnp.sum(dg3, axis=0, keepdims=True)])
    dg = jnp.pad(dg.reshape(4, 8, gain_part).transpose(1, 0, 2), ((0, 0), (0, 0), (0, 256 - gain_part)))
    dqk = jnp.pad(dqk.reshape(2, 8, qk_part).transpose(1, 0, 2), ((0, 0), (0, 2), (0, 256 - qk_part)))
    dm_all, small_all, early_all = transfer(
        8, "columns_to_owners", 12,
        DirectWsh("scatter", d_mixed),
        DirectWsh("scatter", jnp.concatenate([dg, dqk], axis=1)),
        Gather(ff_early, "ctx"),
    )
    grad_qkv = dot(dm_all.reshape(-1, qkv_part), normed_all, TN)
    both = jnp.concatenate([grad_qkv, grad_out], axis=0).astype(BF)
    share = both.shape[0] // 16
    room = -(-share // 16) * 16
    both = jnp.pad(both.reshape(8, 2, share, width), ((0, 0), (0, 0), (0, room - share), (0, 0)))
    small_parts, grads, late_all = transfer(
        9, "sum_grads", 40,
        ShareCtx(jnp.sum(small_all, axis=0)), SumCtx(both), Gather(ff_late, "ctx"),
    )
    grad_gate_up, grad_down = widen(
        early_all.reshape(-1, width), late_all.reshape(-1, width), units
    )
    grads = grads[:, :, :share].reshape(-1, width).astype(F32)
    small_sum = jnp.sum(small_parts, axis=0)
    return (
        output[None],
        grad_hidden[None],
        grads[:qkv_part],
        grads[qkv_part:],
        small_sum[:4, :gain_part].T,
        small_sum[4:6, :qk_part].T,
        grad_gate_up,
        grad_down,
    )


def solution(mesh):
    return jax.shard_map(
        on_device,
        mesh=mesh,
        in_specs=(
            P("wsh", "ctx", None),
            P("wsh", None),
            P("wsh", None),
            P("wsh", None),
            P("wsh", None),
            P("wsh", None, None),
            P("wsh", None),
            P("wsh", "ctx", None),
        ),
        out_specs=(
            P("wsh", "ctx", None),
            P("wsh", "ctx", None),
            P("wsh", None),
            P("wsh", None),
            P("wsh", None),
            P("wsh", None),
            P("wsh", None, None),
            P("wsh", None),
        ),
        check_vma=False,
    )
```

```python
import functools
import math

import jax
import jax.numpy as jnp
from jax import lax
from jax.experimental import pallas as pl
from jax.experimental.pallas import tpu as pltpu
from jax.sharding import PartitionSpec as P

HEADS = 4
HD = 256
KB = 512
EPS = 1e-06
ROPE_BASE = 1000000.0
MASKED = -1e30
MESH = pl.DeviceIdType.MESH
BF = jnp.bfloat16
F32 = jnp.float32
HBM = pltpu.HBM
ROOM = 60 * 2**20


def cost(us):
    return pl.CostEstimate(flops=0, bytes_accessed=int(us * 3.0e6), transcendentals=0)


class Grid:
    def __init__(self, axis, index, core):
        self.axis, self.core = axis, core
        self.h, self.y = lax.div(index, 4), lax.rem(index, 4)
        self.yp, self.ym, self.y2 = (lax.rem(self.y + k, 4) for k in (1, 3, 2))
        self.up, self.down = self.device(self.h, self.yp), self.device(self.h, self.ym)
        self.across = self.device(1 - self.h, self.y)

    def block(self, h, y):
        return h * 4 + y if self.axis == "wsh" else (h * 4 + y) * 2 + self.core

    def device(self, h, y):
        return {self.axis: self.block(h, y)}


class Place:
    def __init__(self):
        self.ctx, self.wsh = lax.axis_index("ctx"), lax.axis_index("wsh")
        self.chip, self.core = lax.div(self.ctx, 2), lax.rem(self.ctx, 2)
        self.grids = {"wsh": Grid("wsh", self.wsh, 0), "ctx": Grid("ctx", self.chip, self.core)}
        self.twin = {"ctx": self.ctx + 1 - 2 * self.core}

    def chips(self, step):
        return {"ctx": lax.rem(self.ctx + 2 * step, 16)}

    def row(self, step):
        return {"wsh": lax.rem(self.wsh + step, 8)}

    def peers(self, groups):
        found = []
        for axis, whole in (("wsh", "row"), ("ctx", "chips")):
            if axis in groups and whole not in groups:
                grid = self.grids[axis]
                found += [grid.up, grid.down, grid.across]
        if "row" in groups:
            found += [self.row(step) for step in range(1, 8)]
        if "chips" in groups:
            found += [self.chips(step) for step in range(1, 8)]
        if "others" in groups:
            found += [{"ctx": lax.rem(self.ctx + 2 * s + 1, 16)} for s in range(8)]
        elif "twin" in groups:
            found.append(self.twin)
        return found


def remote(src, dst, sems, i, device):
    return pltpu.make_async_remote_copy(
        src_ref=src, dst_ref=dst, send_sem=sems.at[0, i], recv_sem=sems.at[1, i],
        device_id=device, device_id_type=MESH,
    )


def meet(place, groups):
    barrier = pltpu.get_barrier_semaphore()
    peers = place.peers(groups)
    for peer in peers:
        pl.semaphore_signal(barrier, inc=1, device_id=peer, device_id_type=MESH)
    pl.semaphore_wait(barrier, len(peers))


def split_rows(count):
    return (count // 2 + 15) // 16 * 16


class Gather:
    def __init__(self, array, axis="wsh", pair=False):
        self.arrays, self.axis, self.pair = [array], axis, pair
        self.twins = pair or axis == "ctx"
        self.groups = {axis, "twin"} if self.twins else {axis}
        count = 16 if axis == "ctx" else 8
        self.outs = [jax.ShapeDtypeStruct((count,) + array.shape, array.dtype)]
        self.out_spaces, self.in_spaces = [HBM], [HBM]
        self.scratch = [pltpu.SemaphoreType.DMA((2, 19)), pltpu.SemaphoreType.DMA]

    def run(self, p, ins, outs, scratch):
        (x,), (o,), (sems, own) = ins, outs, scratch
        g = p.grids[self.axis]
        size = x.shape[0] // (2 if self.pair else 1)
        base = pl.multiple_of(p.core * size, size) if self.pair else 0
        half = split_rows(size)
        every, low, high = pl.ds(base, size), pl.ds(base, half), pl.ds(base + half, size - half)
        h, other = g.h, 1 - g.h
        me = g.block(h, g.y)
        copies = {}

        def send(i, block, rows, device, source=None):
            source = o.at[block, rows] if source is None else source
            copies[i] = remote(source, o.at[block, rows], sems, i, device)
            copies[i].start()

        def arrived(i, block, rows):
            copies[i].wait_recv()
            if self.twins:
                send(9 + i, block, rows, p.twin)

        send(2, me, every, g.across, x.at[every])
        send(0, me, every, g.up, x.at[every])
        send(1, me, every, g.down, x.at[every])
        if self.axis == "ctx":
            send(18, me, every, p.twin, x)
        local = pltpu.make_async_copy(x, o.at[me], own)
        local.start()
        yield
        block = g.block(other, g.y)
        arrived(2, block, every)
        send(5, block, every, g.up)
        send(6, block, every, g.down)
        yield
        block = g.block(h, g.ym)
        arrived(0, block, every)
        send(3, block, low, g.up)
        yield
        block = g.block(h, g.yp)
        arrived(1, block, every)
        send(4, block, high, g.down)
        yield
        block = g.block(other, g.ym)
        arrived(5, block, every)
        send(7, block, low, g.up)
        yield
        block = g.block(other, g.yp)
        arrived(6, block, every)
        send(8, block, high, g.down)
        yield
        block = g.block(h, g.y2)
        arrived(3, block, low)
        arrived(4, block, high)
        yield
        block = g.block(other, g.y2)
        arrived(7, block, low)
        arrived(8, block, high)
        yield
        for i, copy in copies.items():
            copy.wait_send()
            if i >= 9:
                copy.wait_recv()
        local.wait()


class Scatter:
    def __init__(self, array, axis="wsh", dtype=F32):
        _, rows, width = array.shape
        self.arrays, self.axis, self.groups = [array], axis, {axis}
        self.outs = [jax.ShapeDtypeStruct((rows, width), dtype)]
        self.in_spaces, self.out_spaces = [pltpu.VMEM], [pltpu.VMEM]
        half = split_rows(rows)
        low, high = pltpu.VMEM((2, half, width), BF), pltpu.VMEM((2, rows - half, width), BF)
        whole = pltpu.VMEM((2, rows, width), BF)
        self.scratch = [low, high, low, high, whole, whole, whole, pltpu.SemaphoreType.DMA((2, 13))]

    def run(self, p, ins, outs, scratch):
        (x,), (o,), (buf_a, buf_b, sum_c, sum_d, buf_c, buf_d, buf_e, sems) = ins, outs, scratch
        g = p.grids[self.axis]
        rows = o.shape[0]
        half = split_rows(rows)
        low, high = pl.ds(0, half), pl.ds(half, rows - half)
        planes = ((1 - g.h) * 4, g.h * 4)
        copies = {}

        def send(i, source, target, device):
            copies[i] = remote(source, target, sems, i, device)
            copies[i].start()

        for k, plane in enumerate(planes):
            send(k, x.at[plane + g.y2, low], buf_a.at[k], g.up)
            send(2 + k, x.at[plane + g.y2, high], buf_b.at[k], g.down)
            send(4 + k, x.at[plane + g.yp, high], buf_c.at[k, high], g.up)
            send(6 + k, x.at[plane + g.ym, low], buf_d.at[k, low], g.down)
        for k, plane in enumerate(planes):
            yield
            copies[k].wait_recv()
            sum_c[k] = (x[plane + g.yp, :half].astype(F32) + buf_a[k].astype(F32)).astype(BF)
            send(8 + k, sum_c.at[k], buf_c.at[k, low], g.up)
            yield
            copies[2 + k].wait_recv()
            sum_d[k] = (x[plane + g.ym, half:].astype(F32) + buf_b[k].astype(F32)).astype(BF)
            send(10 + k, sum_d.at[k], buf_d.at[k, high], g.down)
        for k, plane in enumerate(planes):
            yield
            for i in (4, 6, 8, 10):
                copies[i + k].wait_recv()
            total = x[plane + g.y].astype(F32) + buf_c[k].astype(F32) + buf_d[k].astype(F32)
            if k == 0:
                buf_e[0] = total.astype(BF)
                send(12, buf_e.at[0], buf_e.at[1], g.across)
            else:
                yield
                copies[12].wait_recv()
                o[...] = (total + buf_e[1].astype(F32)).astype(o.dtype)
        for copy in copies.values():
            copy.wait_send()


class DirectWsh:
    def __init__(self, mode, array, turns=9):
        self.mode, self.arrays, self.groups, self.turns = mode, [array], {"row"}, turns
        shape = ((8,) + array.shape) if mode == "gather" else array.shape
        self.outs = [jax.ShapeDtypeStruct(shape, array.dtype)]
        self.in_spaces, self.out_spaces = [HBM], [HBM]
        self.scratch = [pltpu.SemaphoreType.DMA((2, 7)), pltpu.SemaphoreType.DMA]

    def run(self, p, ins, outs, scratch):
        (x,), (o,), (sems, own) = ins, outs, scratch
        pick = (lambda i: x) if self.mode == "gather" else (lambda i: x.at[i])
        copies = []
        for step in range(1, 8):
            to = p.row(step)
            copies.append(remote(pick(to["wsh"]), o.at[p.wsh], sems, step - 1, to))
            copies[-1].start()
        copies.append(pltpu.make_async_copy(pick(p.wsh), o.at[p.wsh], own))
        copies[-1].start()
        for _ in range(self.turns):
            yield
        for copy in copies:
            copy.wait()


class ScatterCtx:
    def __init__(self, array):
        _, _, rows, width = array.shape
        self.arrays, self.groups = [array], {"chips", "twin"}
        self.outs = [jax.ShapeDtypeStruct((rows, width), F32)]
        self.in_spaces, self.out_spaces = [pltpu.VMEM], [pltpu.VMEM]
        self.scratch = [pltpu.VMEM((8, rows, width), BF)] * 3 + [pltpu.SemaphoreType.DMA((2, 15))]

    def run(self, p, ins, outs, scratch):
        (x,), (o,), (pair, sums, got, sems) = ins, outs, scratch
        copies = []
        order = list(range(1, 8)) + [0]
        for i, step in enumerate(order):
            chip = lax.rem(p.chip + step, 8)
            copies.append(remote(x.at[2 * chip + 1 - p.core], pair.at[chip], sems, i, p.twin))
            copies[-1].start()
        for i, step in enumerate(order):
            if i % 3 == 0:
                yield
            chip = lax.rem(p.chip + step, 8)
            copies[i].wait_recv()
            both = x[2 * chip + p.core].astype(F32) + pair[chip].astype(F32)
            if step > 0:
                sums[chip] = both.astype(BF)
                copies.append(remote(sums.at[chip], got.at[p.chip], sems, 7 + step, p.chips(step)))
                copies[-1].start()
            else:
                o[...] = both
        for step in range(1, 8):
            if step % 3 == 1:
                yield
            copies[7 + step].wait_recv()
            o[...] += got[lax.rem(p.chip + 8 - step, 8)].astype(F32)
        for copy in copies:
            copy.wait_send()


class SumCtx:
    def __init__(self, d_mixed, normed, attended, d_branch):
        width = normed.shape[-1]
        self.share = (d_mixed.shape[-1] + attended.shape[-1]) // 16
        rows = -(-self.share // 16) * 16
        self.arrays, self.groups = [d_mixed, normed, attended, d_branch], {"chips", "twin"}
        self.outs = [jax.ShapeDtypeStruct((8, 2, rows, width), BF)]
        self.in_spaces, self.out_spaces = [pltpu.VMEM] * 4, [pltpu.VMEM]
        self.scratch = [pltpu.VMEM((8, 2, rows, width), BF)]
        self.scratch += [pltpu.VMEM((8, rows, width), BF)] * 3 + [pltpu.SemaphoreType.DMA((2, 23))]

    def product(self, ins, x):
        d_mixed, normed, attended, d_branch = ins
        width = normed.shape[-1]
        flat = lambda ref: ref[...].reshape(-1, ref.shape[-1])
        parts = (dot(flat(d_mixed), flat(normed), TN), dot(flat(attended), flat(d_branch), TN))
        both = jnp.concatenate(parts, axis=0)
        blank = jnp.zeros((x.shape[2] - self.share, width), F32)
        for i in range(16):
            rows = both[i * self.share : (i + 1) * self.share]
            x[i // 2, i % 2] = jnp.concatenate([rows, blank], axis=0).astype(BF)

    def run(self, p, ins, outs, scratch):
        (o,), (x, pair, sums, got, sems) = outs, scratch
        self.product(ins, x)
        first = remote(x.at[:, 1 - p.core], pair, sems, 0, p.twin)
        first.start()
        first.wait_recv()
        copies = [first]
        for step in range(1, 8):
            chip = lax.rem(p.chip + step, 8)
            sums[chip] = (x[chip, p.core].astype(F32) + pair[chip].astype(F32)).astype(BF)
            copies.append(remote(sums.at[chip], got.at[p.chip], sems, step, p.chips(step)))
            copies[-1].start()
        total = x[p.chip, p.core].astype(F32) + pair[p.chip].astype(F32)
        yield
        for step in range(1, 8):
            copies[step].wait_recv()
            total = total + got[lax.rem(p.chip + 8 - step, 8)].astype(F32)
        o[p.chip, p.core] = total.astype(BF)
        mine = o.at[p.chip, p.core]
        spread = []
        for step in range(1, 8):
            spread.append(remote(mine, mine, sems, 7 + step, p.chips(step)))
            spread[-1].start()
        passed = [remote(mine, mine, sems, 15, p.twin)]
        passed[0].start()
        yield
        for step in range(1, 8):
            spread[step - 1].wait_recv()
            piece = o.at[lax.rem(p.chip + 8 - step, 8), p.core]
            passed.append(remote(piece, piece, sems, 15 + step, p.twin))
            passed[-1].start()
        for copy in copies + spread:
            copy.wait_send()
        for copy in passed:
            copy.wait()


class ShareCtx:
    def __init__(self, array):
        self.arrays, self.groups = [array], {"chips", "twin", "others"}
        self.outs = [jax.ShapeDtypeStruct((16,) + array.shape, array.dtype)]
        self.in_spaces, self.out_spaces = [HBM], [HBM]
        self.scratch = [pltpu.SemaphoreType.DMA((2, 15)), pltpu.SemaphoreType.DMA]

    def run(self, p, ins, outs, scratch):
        (x,), (o,), (sems, own) = ins, outs, scratch
        copies = []
        for step in range(1, 16):
            to = {"ctx": lax.rem(p.ctx + step, 16)}
            copies.append(remote(x, o.at[p.ctx], sems, step - 1, to))
            copies[-1].start()
        copies.append(pltpu.make_async_copy(x, o.at[p.ctx], own))
        copies[-1].start()
        for _ in range(9):
            yield
        for copy in copies:
            copy.wait()


def rows_loop(count, body):
    lax.fori_loop(0, count // 16, lambda i, _: (body(pl.ds(pl.multiple_of(i * 16, 16), 16)), 0)[1], 0)


class FeedForwardGrads:
    def __init__(self, d_gate, d_up, inner, normed, d_branch):
        units, width = d_gate.shape[1], normed.shape[1]
        self.arrays, self.groups = [d_gate, d_up, inner, normed, d_branch], {"ctx", "twin"}
        granules = -(-3 * units // 256)
        early = granules * 5 // 9
        self.pieces = (early * 16, (granules - early) * 16)
        sums = [pltpu.VMEM((8, rows, width), BF) for rows in self.pieces]
        self.scatters = [Scatter(jax.ShapeDtypeStruct(b.shape, BF), "ctx", BF) for b in sums]
        self.outs = self.scatters[0].outs + self.scatters[1].outs
        self.in_spaces, self.out_spaces = [pltpu.VMEM] * 5, [pltpu.VMEM] * 2
        self.scratch = [pltpu.VMEM((16 * rows, width), BF) for rows in self.pieces]
        self.scratch += sums + sums + [pltpu.SemaphoreType.DMA((2, 16))]
        self.scratch += self.scatters[0].scratch + self.scatters[1].scratch

    def run(self, p, ins, outs, scratch):
        d_gate, d_up, inner, normed, d_branch = ins
        first, second, pair_first, pair_second, sums, sums_second, sems, *rest = scratch
        count = len(self.scatters[0].scratch)
        units = d_gate.shape[1]
        split = first.shape[0]
        twins = []

        def put(at, value):
            end = at + value.shape[0]
            if at < split:
                first[at : min(end, split)] = value[: min(end, split) - at]
            if end > split:
                second[max(at, split) - split : end - split] = value[max(at, split) - at :]

        def swap(whole, pair, number):
            size = pair.shape[1]
            for chip in range(8):
                there = pl.ds(pl.multiple_of((2 * chip + 1 - p.core) * size, 16), size)
                twins.append(remote(whole.at[there], pair.at[chip], sems, 8 * number + chip, p.twin))
                twins[-1].start()

        def add(whole, pair, result, number):
            size = pair.shape[1]
            for chip in range(8):
                here = pl.ds(pl.multiple_of((2 * chip + p.core) * size, 16), size)
                twins[8 * number + chip].wait_recv()
                result[chip] = (whole[here].astype(F32) + pair[chip].astype(F32)).astype(BF)

        yield
        started = False
        for number, (left, right) in enumerate(((d_gate, normed), (d_up, normed), (inner, d_branch))):
            for start in range(0, units, 256):
                stop = min(start + 256, units)
                put(number * units + start, dot(left[:, start:stop], right[...], TN).astype(BF))
                if not started and number * units + stop >= split:
                    started = True
                    swap(first, pair_first, 0)
            yield
        missing = second.shape[0] - (3 * units - split)
        if missing:
            second[second.shape[0] - missing :] = jnp.zeros((missing, second.shape[1]), BF)
        swap(second, pair_second, 1)
        add(first, pair_first, sums, 0)
        turns = [self.scatters[0].run(p, [sums], outs[:1], rest[:count])]
        next(turns[0])
        add(second, pair_second, sums_second, 1)
        turns.append(self.scatters[1].run(p, [sums_second], outs[1:], rest[count:]))
        while turns:
            turns = [turn for turn in turns if next(turn, "end") != "end"]
            yield
        for copy in twins:
            copy.wait_send()


def unpair(both, gate, up):
    step = 96
    for start in range(0, gate.shape[0], step):
        def move(rows):
            here = pl.ds(pl.multiple_of(rows.start + start, 16), 16)
            gate[here] = both[here, 0, :]
            up[here] = both[here, 1, :]

        rows_loop(step, move)
        yield


def ring_blocks(g, x, o, sems):
    rows = x.shape[0]
    half = rows // 2
    low, high = (0, half), (half, half)
    copies = {}

    def at(slot, part=(0, rows)):
        return o.at[pl.ds(slot * rows + part[0], part[1])]

    def send(i, source, target, device):
        copies[i] = remote(source, target, sems, i, device)
        copies[i].start()

    send(2, x, at(1), g.across)
    send(0, x, at(2), g.up)
    send(1, x, at(3), g.down)
    o[:rows] = x[...]
    copies[2].wait_recv()
    send(5, at(1), at(4), g.up)
    send(6, at(1), at(5), g.down)
    yield 0
    copies[0].wait_recv()
    send(3, at(2, low), at(6, low), g.up)
    copies[1].wait_recv()
    send(4, at(3, high), at(6, high), g.down)
    yield 1
    copies[5].wait_recv()
    send(7, at(4, low), at(7, low), g.up)
    copies[6].wait_recv()
    send(8, at(5, high), at(7, high), g.down)
    yield 2
    for i in (3, 4, 7, 8):
        copies[i].wait_recv()
    yield 3
    for copy in copies.values():
        copy.wait_send()


class RingSum:
    slots = {"opposite": (7, 6), "up": (5, 3), "down": (4, 2), "own": (1, 0)}

    def __init__(self, g, x, o, scratch):
        self.g, self.x, self.o = g, x, o
        self.buf_a, self.buf_b, self.sum_c, self.sum_d, self.buf_c, self.buf_d, self.buf_e, self.sems = scratch
        self.rows = o.shape[0]
        self.half = self.rows // 2
        self.copies = {}

    @staticmethod
    def scratch(rows, width):
        half, whole = pltpu.VMEM((2, rows // 2, width), BF), pltpu.VMEM((2, rows, width), BF)
        return [half, half, half, half, whole, whole, whole, pltpu.SemaphoreType.DMA((2, 13))]

    def at(self, place, k, part):
        return pl.ds(self.slots[place][k] * self.rows + part * self.half, self.half * (1 if part < 2 else 2))

    def send(self, i, source, target, device):
        self.copies[i] = remote(source, target, self.sems, i, device)
        self.copies[i].start()

    def near(self, k):
        low, high = pl.ds(0, self.half), pl.ds(self.half, self.half)
        self.send(4 + k, self.x.at[self.at("up", k, 1)], self.buf_c.at[k, high], self.g.up)
        self.send(6 + k, self.x.at[self.at("down", k, 0)], self.buf_d.at[k, low], self.g.down)

    def far(self, k):
        self.send(k, self.x.at[self.at("opposite", k, 0)], self.buf_a.at[k], self.g.up)
        self.send(2 + k, self.x.at[self.at("opposite", k, 1)], self.buf_b.at[k], self.g.down)

    def rest(self):
        x, copies = self.x, self.copies
        low, high = pl.ds(0, self.half), pl.ds(self.half, self.half)
        for k in range(2):
            yield
            copies[k].wait_recv()
            self.sum_c[k] = (x[self.at("up", k, 0)].astype(F32) + self.buf_a[k].astype(F32)).astype(BF)
            self.send(8 + k, self.sum_c.at[k], self.buf_c.at[k, low], self.g.up)
            copies[2 + k].wait_recv()
            self.sum_d[k] = (x[self.at("down", k, 1)].astype(F32) + self.buf_b[k].astype(F32)).astype(BF)
            self.send(10 + k, self.sum_d.at[k], self.buf_d.at[k, high], self.g.down)
        for k in range(2):
            yield
            for i in (4, 6, 8, 10):
                copies[i + k].wait_recv()
            slot = self.slots["own"][k] * self.rows
            total = x[slot : slot + self.rows].astype(F32) + self.buf_c[k].astype(F32) + self.buf_d[k].astype(F32)
            if k == 0:
                self.buf_e[0] = total.astype(BF)
                self.send(12, self.buf_e.at[0], self.buf_e.at[1], self.g.across)
            else:
                yield
                copies[12].wait_recv()
                self.o[...] = total + self.buf_e[1].astype(F32)
        for copy in copies.values():
            copy.wait_send()


def forward_block(n, w_gate, w_up, w_down, inner_ref, gelu_ref, slope_ref, terms_ref, rows):
    gate = dot(n, w_gate[...], NT)
    up = dot(n, w_up[...], NT)
    bend, grow = math.sqrt(2.0 / math.pi), 0.044715
    square = gate * gate
    wave = jnp.tanh(bend * gate * (1.0 + grow * square))
    rise = 0.5 * (1.0 + wave)
    gelu = gate * rise
    slope = rise + 0.5 * bend * gate * (1.0 - wave * wave) * (1.0 + 3.0 * grow * square)
    gelu_ref[rows] = gelu.astype(BF)
    slope_ref[rows] = (up * slope).astype(BF)
    inner_ref[rows] = (gelu * up).astype(BF)
    terms_ref[rows] = jnp.dot(inner_ref[rows], w_down[...], preferred_element_type=F32).astype(BF)


class FeedForward:
    def __init__(self, normed, resid, cot, gains, w_gate, w_up, w_down, first_normed):
        (rows, width), units = normed.shape, w_down.shape[0]
        self.arrays = [normed, resid, cot, gains, w_gate, w_up, w_down, first_normed]
        self.gather = Gather(first_normed)
        tokens = jax.ShapeDtypeStruct((8 * rows, width), BF)
        hidden = jax.ShapeDtypeStruct((8 * rows, units), BF)
        self.grads = FeedForwardGrads(hidden, hidden, hidden, tokens, tokens)
        self.groups = {"wsh"} | self.grads.groups
        shapes = [((rows, width), BF), ((1, width), F32), ((rows, width), F32)]
        self.outs = [jax.ShapeDtypeStruct(*shape) for shape in shapes] + self.grads.outs
        self.outs += self.gather.outs
        self.in_spaces, self.out_spaces = [pltpu.VMEM] * 7 + [HBM], [pltpu.VMEM] * 5 + [HBM]
        wide, narrow = pltpu.VMEM(tokens.shape, BF), pltpu.VMEM(hidden.shape, BF)
        self.scratch = [wide] * 3 + [narrow] * 5 + [pltpu.VMEM((rows, width), F32), pltpu.VMEM((rows, width), BF)]
        self.scratch += [pltpu.SemaphoreType.DMA((2, 9))] * 2
        self.scratch += RingSum.scratch(rows, width) * 2 + self.grads.scratch + self.gather.scratch

    def run(self, p, ins, outs, scratch):
        x, resid, cot, gains, w_gate, w_up, w_down, first_normed = ins
        out, dg, d_normed, *grads, first_all = outs
        tokens, terms, d_all, inner, gelu, slope, d_gate, d_up, branch, low, sems, back_sems, *rest = scratch
        g = p.grids["wsh"]
        count = len(RingSum.scratch(*x.shape))
        there = RingSum(g, terms, branch, rest[:count])
        back = RingSum(g, terms, d_normed, rest[count : 2 * count])
        pair = 2 * x.shape[0]

        def sends(ring, i):
            if i in (1, 2):
                ring.near(2 - i)
            if i == 3:
                ring.far(0)
                ring.far(1)

        p.ready(0)
        for i in ring_blocks(g, x, tokens, sems):
            if i == 0:
                p.ready()
            rows = slice(i * pair, (i + 1) * pair)
            forward_block(tokens[rows], w_gate, w_up, w_down, inner, gelu, slope, terms, rows)
            sends(there, i)
        yield from there.rest()
        total, gain, c = branch[...], gains[3:4], cot[...].astype(F32)
        scale = scale_of(total)
        d_branch, dg_terms = norm_back(total, scale, gain, c)
        low[...] = d_branch.astype(BF)
        out[...] = (resid[...] + total * scale * gain).astype(BF)
        dg[...] = jnp.sum(dg_terms, axis=0, keepdims=True)
        for i in ring_blocks(g, low, d_all, back_sems):
            rows = slice(i * pair, (i + 1) * pair)
            d_inner = dot(d_all[rows], w_down[...], NT)
            d_gate[rows] = (d_inner * slope[rows].astype(F32)).astype(BF)
            d_up[rows] = (d_inner * gelu[rows].astype(F32)).astype(BF)
            terms[rows] = (
                jnp.dot(d_gate[rows], w_gate[...], preferred_element_type=F32)
                + jnp.dot(d_up[rows], w_up[...], preferred_element_type=F32)
            ).astype(BF)
            sends(back, i)
        last = len(self.gather.scratch)

        def others():
            yield from back.rest()
            yield from self.gather.run(p, [first_normed], [first_all], rest[-last:])

        turns = [
            self.grads.run(p, [d_gate, d_up, inner, tokens, d_all], grads, rest[2 * count : -last]),
            others(),
        ]
        while turns:
            turns = [turn for turn in turns if next(turn, "end") != "end"]
            yield


class Tables:
    def __init__(self, tokens):
        self.tokens, self.arrays, self.groups = tokens, [], set()
        self.outs = [jax.ShapeDtypeStruct((tokens, HD // 2), F32)] * 2
        self.in_spaces, self.out_spaces, self.scratch = [], [pltpu.VMEM] * 2, []

    def run(self, p, ins, outs, scratch):
        shape = outs[0].shape
        token = lax.broadcasted_iota(jnp.int32, shape, 0) + p.ctx * self.tokens
        power = lax.broadcasted_iota(jnp.int32, shape, 1).astype(F32) * (-2.0 / HD)
        angles = token.astype(F32) * jnp.exp(power * math.log(ROPE_BASE))
        outs[0][...] = jnp.cos(angles)
        outs[1][...] = jnp.sin(angles)
        yield


def transfer_kernel(parts, ins, outs, scratch, ready, store):
    place = Place()
    place.ready, place.store = ready, store
    meet(place, set().union(*(part.groups for part in parts)))

    def take(refs, counts):
        refs = list(refs)
        return [[refs.pop(0) for _ in range(count)] for count in counts]

    ins = take(ins, [len(part.arrays) for part in parts])
    outs = take(outs, [len(part.outs) for part in parts])
    scratch = take(scratch, [len(part.scratch) for part in parts])
    active = [part.run(place, i, o, s) for part, i, o, s in zip(parts, ins, outs, scratch)]
    while active:
        active = [run for run in active if next(run, "end") != "end"]


def staged(body, name, us, arrays, in_spaces, outs, out_spaces, scratch, cid=None):
    picked_in = [i for i, space in enumerate(in_spaces) if space == pltpu.VMEM]
    picked_out = [i for i, space in enumerate(out_spaces) if space == pltpu.VMEM]
    held = [pltpu.VMEM(arrays[i].shape, arrays[i].dtype) for i in picked_in]
    held += [pltpu.VMEM(outs[i].shape, outs[i].dtype) for i in picked_out]
    counts = (len(arrays), len(outs), len(picked_in), len(picked_out))

    def kernel(*refs):
        ends = [sum(counts[:k]) for k in range(5)]
        far_in, far_out, near_in, near_out = (refs[ends[k] : ends[k + 1]] for k in range(4))
        in_sems, out_sems, *rest = refs[ends[4] :]
        ins, results = list(far_in), list(far_out)
        loads = []
        for k, i in enumerate(picked_in):
            loads.append(pltpu.make_async_copy(far_in[i], near_in[k], in_sems.at[k]))
            loads[-1].start()
            ins[i] = near_in[k]
        for k, i in enumerate(picked_out):
            results[i] = near_out[k]

        waiting = dict(zip(picked_in, loads))

        def ready(*indices):
            for i in indices or tuple(waiting):
                waiting.pop(i).wait()

        stores = {}

        def store(i):
            k = picked_out.index(i)
            stores[i] = pltpu.make_async_copy(near_out[k], far_out[i], out_sems.at[k])
            stores[i].start()

        body(ins, results, rest, ready, store)
        for i in picked_out:
            if i not in stores:
                store(i)
        for copy in stores.values():
            copy.wait()

    sems = [pltpu.SemaphoreType.DMA((max(len(picked), 1),)) for picked in (picked_in, picked_out)]
    extra = {} if cid is None else {"collective_id": cid, "has_side_effects": True}
    return pl.pallas_call(
        kernel,
        out_shape=list(outs),
        in_specs=[pl.BlockSpec(memory_space=HBM)] * counts[0],
        out_specs=[pl.BlockSpec(memory_space=HBM)] * counts[1],
        scratch_shapes=held + sems + list(scratch),
        compiler_params=pltpu.CompilerParams(vmem_limit_bytes=ROOM, **extra),
        cost_estimate=cost(us),
        name=name,
    )(*arrays)


def transfer(cid, name, us, *parts):
    every = lambda field: [item for part in parts for item in getattr(part, field)]
    return staged(
        functools.partial(transfer_kernel, parts), name, us, every("arrays"), every("in_spaces"),
        every("outs"), every("out_spaces"), every("scratch"), cid,
    )


NT = (((1,), (1,)), ((), ()))
TN = (((0,), (0,)), ((), ()))


def dot(a, b, dims):
    return lax.dot_general(a, b, dims, preferred_element_type=F32)


def masked_scores(q, keys, block, ctx, tokens):
    scores = dot(q, keys, NT)
    row = lax.rem(lax.broadcasted_iota(jnp.int32, scores.shape, 0), tokens) + ctx * tokens
    col = lax.broadcasted_iota(jnp.int32, scores.shape, 1) + block * KB
    return jnp.where(col <= row, scores, MASKED)


def widen_kernel(first, gate_ref, up_ref, more_ref, low_ref, grads_ref, small_ref, both_ref, down_ref, qkv_ref, out_ref,
                 sum_ref):
    @pl.when(pl.program_id(0) == 0)
    def _():
        share, split = (qkv_ref.shape[0] + out_ref.shape[0]) // 16, qkv_ref.shape[0]
        for i in range(16):
            value = grads_ref[i // 2, i % 2].astype(F32)
            start, stop = i * share, (i + 1) * share
            middle = min(max(split, start), stop)
            if middle > start:
                qkv_ref[start:middle] = value[: middle - start]
            if stop > middle:
                out_ref[middle - split : stop - split] = value[middle - start : share]
        sum_ref[...] = jnp.sum(small_ref[...], axis=0)

    both_ref[:, 0, :] = gate_ref[...].astype(F32)
    down_ref[...] = low_ref[...].astype(F32)

    @pl.when(pl.program_id(0) < first)
    def _():
        both_ref[:, 1, :] = up_ref[...].astype(F32)

    @pl.when(pl.program_id(0) >= first)
    def _():
        both_ref[:, 1, :] = more_ref[...].astype(F32)


def widen(early, late, rows, grads, small, parts):
    width = early.shape[1]
    step = 96
    count = rows // step
    first = early.shape[0] // step - count
    spec = lambda index: pl.BlockSpec((step, width), lambda i: (index(i), 0))
    whole = lambda shape: pl.BlockSpec(shape, lambda i: (0,) * len(shape))
    return pl.pallas_call(
        functools.partial(widen_kernel, first),
        grid=(count,),
        out_shape=[
            jax.ShapeDtypeStruct((rows, 2, width), F32),
            jax.ShapeDtypeStruct((rows, width), F32),
            jax.ShapeDtypeStruct((parts[0], width), F32),
            jax.ShapeDtypeStruct((parts[1], width), F32),
            jax.ShapeDtypeStruct(small.shape[1:], F32),
        ],
        in_specs=[
            spec(lambda i: i),
            spec(lambda i: jnp.minimum(i, first - 1) + count),
            spec(lambda i: jnp.maximum(i - first, 0)),
            spec(lambda i: i + count - first),
            whole(grads.shape),
            whole(small.shape),
        ],
        out_specs=[
            pl.BlockSpec((step, 2, width), lambda i: (i, 0, 0)),
            spec(lambda i: i),
            whole((parts[0], width)),
            whole((parts[1], width)),
            whole(small.shape[1:]),
        ],
        cost_estimate=cost(9),
        name="widen",
    )(early, early, late, late, grads, small)


def scale_of(values):
    return lax.rsqrt(jnp.mean(values * values, axis=-1, keepdims=True) + EPS)


def norm_back(v, r, g, dy):
    gdy = g * dy
    dv = r * gdy - v * (r * r * r) * jnp.mean(gdy * v, axis=-1, keepdims=True)
    return dv, dy * v * r


def rope(v, cosine, sine):
    a, b = v[..., : HD // 2], v[..., HD // 2 :]
    return jnp.concatenate([a * cosine - b * sine, b * cosine + a * sine], axis=-1)


def rope_back(u, cosine, sine):
    a, b = u[..., : HD // 2], u[..., HD // 2 :]
    return jnp.concatenate([a * cosine + b * sine, b * cosine - a * sine], axis=-1)


def compute(kernel, name, us, outs, scratch, *args):
    def body(ins, results, rest, ready, store):
        ready()
        kernel(*ins, *results, *rest)

    outs = [jax.ShapeDtypeStruct(shape, dtype) for shape, dtype in outs]
    return staged(
        body, name, us, args, [pltpu.VMEM] * len(args), outs, [pltpu.VMEM] * len(outs), scratch
    )


def prepare_kernel(parts, x_ref, w_ref, packed_ref, cos_ref, sin_ref, g_ref, qk_ref, normed_ref, raw_ref, q_ref, kv_ref):
    gain_part, qk_part = parts
    g_ref[...] = jnp.zeros_like(g_ref)
    qk_ref[...] = jnp.zeros_like(qk_ref)
    for i in range(packed_ref.shape[0]):
        values = packed_ref[i].astype(F32)
        g_ref[0:4, i * gain_part : (i + 1) * gain_part] = values[0:4, :gain_part]
        qk_ref[0:2, i * qk_part : (i + 1) * qk_part] = values[4:6, :qk_part]
    x = x_ref[...].astype(F32)
    tokens = x.shape[0]
    normed = (x * scale_of(x) * g_ref[0:1]).astype(BF)
    normed_ref[...] = normed
    raw_ref[...] = dot(normed, w_ref[...].reshape(-1, w_ref.shape[-1]), NT)
    cosine, sine = cos_ref[...], sin_ref[...]
    for head in range(HEADS + 1):
        v = raw_ref[:, head * HD : (head + 1) * HD]
        column = 0 if head < HEADS else 1
        turned = rope(v * scale_of(v) * qk_ref[column : column + 1], cosine, sine)
        if head < HEADS:
            q_ref[head * tokens : (head + 1) * tokens] = (turned * HD ** (-0.5)).astype(BF)
        else:
            kv_ref[:, :HD] = turned.astype(BF)
    kv_ref[:, HD:] = raw_ref[:, (HEADS + 1) * HD :].astype(BF)


def attend_kernel(q_ref, kv_ref, x_ref, w_ref, g_ref, out_ref, lse_ref, parts_ref, branch_ref,
                  resid_ref, normed_ref, top, total, accum, att_ref, ctx):
    tokens = x_ref.shape[0]
    last = lax.div(ctx * tokens, KB)
    q = q_ref[...]

    def block_of(index, half):
        per = KB // tokens
        return kv_ref[pl.ds(index * per, per), :, half * HD : (half + 1) * HD].reshape(KB, HD)

    scores = masked_scores(q, block_of(last, 0), last, ctx, tokens)
    start = jnp.max(scores, axis=-1, keepdims=True)
    probs = jnp.exp(scores - start)
    top[...] = jnp.broadcast_to(start, top.shape)
    total[...] = jnp.broadcast_to(jnp.sum(probs, axis=-1, keepdims=True), total.shape)
    accum[...] = jnp.dot(
        probs.astype(BF), block_of(last, 1), preferred_element_type=F32
    )

    def body(index, carry):
        scores = dot(q, block_of(index, 0), NT)
        old = top[:, :1]
        new = jnp.maximum(old, jnp.max(scores, axis=-1, keepdims=True))
        probs = jnp.exp(scores - new)
        keep = jnp.exp(old - new)
        top[...] = jnp.broadcast_to(new, top.shape)
        total[...] = total[...] * keep + jnp.sum(probs, axis=-1, keepdims=True)
        accum[...] = accum[...] * keep + jnp.dot(
            probs.astype(BF), block_of(index, 1), preferred_element_type=F32
        )
        return carry

    lax.fori_loop(0, last, body, 0)
    out_ref[...] = accum[...] / total[:, :1]
    lse_ref[...] = top[...] + jnp.log(total[...])
    for head in range(HEADS):
        att_ref[:, head * HD : (head + 1) * HD] = out_ref[
            head * tokens : (head + 1) * tokens
        ].astype(BF)
    part = parts_ref.shape[2]
    for i in range(parts_ref.shape[0]):
        parts_ref[i] = att_ref[:, i * part : (i + 1) * part]
    branch = jnp.dot(att_ref[...], w_ref[...].reshape(-1, w_ref.shape[-1]), preferred_element_type=F32)
    branch_ref[...] = branch
    resid = x_ref[...].astype(F32) + branch * scale_of(branch) * g_ref[1:2]
    resid_ref[...] = resid
    normed_ref[...] = (resid * scale_of(resid) * g_ref[2:3]).astype(BF)


def attend_back_kernel(dn_ref, resid_ref, branch_ref, cot_ref, g_ref, w_ref, q_ref, kv_ref, out_ref,
                       lse_ref, dres_ref, low_ref, dg_ref, dq_ref, dkv_ref, d_ref, ctx):
    tokens = resid_ref.shape[0]
    last = lax.div(ctx * tokens, KB)
    resid = resid_ref[...]
    d_more, dg2 = norm_back(resid, scale_of(resid), g_ref[2:3], dn_ref[...])
    d_resid = cot_ref[...].astype(F32) + d_more
    dres_ref[...] = d_resid
    branch = branch_ref[...]
    d_branch, dg1 = norm_back(branch, scale_of(branch), g_ref[1:2], d_resid)
    low_ref[...] = d_branch.astype(BF)
    dg_ref[0:1] = jnp.sum(dg1, axis=0, keepdims=True)
    dg_ref[1:2] = jnp.sum(dg2, axis=0, keepdims=True)
    d_att = dot(low_ref[...], w_ref[...], NT)
    for head in range(HEADS):
        d_ref[head * tokens : (head + 1) * tokens] = d_att[:, head * HD : (head + 1) * HD].astype(BF)
    q = q_ref[...]
    d_out = d_ref[...]
    lse = lse_ref[:, :1]
    delta = jnp.sum(d_out.astype(F32) * out_ref[...], axis=-1, keepdims=True)

    def block_of(index):
        return pl.ds(pl.multiple_of(index * KB, KB), KB)

    def work(index, scores):
        block = block_of(index)
        probs = jnp.exp(scores - lse)
        d_probs = dot(d_out, kv_ref[block, HD:], NT)
        d_scores = (probs * (d_probs - delta)).astype(BF)
        d_keys = dot(d_scores, q, TN).astype(BF)
        d_values = dot(probs.astype(BF), d_out, TN).astype(BF)
        for i in range(KB // tokens):
            part = slice(i * tokens, (i + 1) * tokens)
            dkv_ref[index * (KB // tokens) + i, :, :HD] = d_keys[part]
            dkv_ref[index * (KB // tokens) + i, :, HD:] = d_values[part]
        return jnp.dot(d_scores, kv_ref[block, :HD], preferred_element_type=F32)

    dq_ref[...] = work(last, masked_scores(q, kv_ref[block_of(last), :HD], last, ctx, tokens))

    def body(index, carry):
        dq_ref[...] += work(index, dot(q, kv_ref[block_of(index), :HD], NT))
        return carry

    lax.fori_loop(0, last, body, 0)

    def clear(index, carry):
        dkv_ref[index] = jnp.zeros(dkv_ref.shape[1:], BF)
        return carry

    lax.fori_loop((last + 1) * (KB // tokens), dkv_ref.shape[0], clear, 0)


def finish_kernel(sizes, own_ref, dq_ref, raw_ref, cos_ref, sin_ref, w_ref, x_ref, g_ref, qk_ref, dres_ref, dg12_ref,
                  dg3_ref, parts_ref, grad_ref, small_ref, mixed_ref, dqk_ref):
    tokens = x_ref.shape[0]
    cosine, sine = cos_ref[...], sin_ref[...]
    total = jnp.zeros((1, HD), F32)
    for head in range(HEADS + 1):
        v = raw_ref[:, head * HD : (head + 1) * HD]
        if head < HEADS:
            u = dq_ref[head * tokens : (head + 1) * tokens] * HD ** (-0.5)
        else:
            u = own_ref[:, :HD]
        column = 0 if head < HEADS else 1
        dv, dg = norm_back(
            v, scale_of(v), qk_ref[column : column + 1], rope_back(u, cosine, sine)
        )
        mixed_ref[:, head * HD : (head + 1) * HD] = dv.astype(BF)
        dg = jnp.sum(dg, axis=0, keepdims=True)
        if head < HEADS:
            total = total + dg
        else:
            dqk_ref[0:1] = total
            dqk_ref[1:2] = dg
    mixed_ref[:, (HEADS + 1) * HD :] = own_ref[:, HD:].astype(BF)
    d_mixed = mixed_ref[...]
    part = parts_ref.shape[2]
    for i in range(parts_ref.shape[0]):
        parts_ref[i] = d_mixed[:, i * part : (i + 1) * part]
    d_normed = jnp.dot(d_mixed, w_ref[...], preferred_element_type=F32)
    x = x_ref[...].astype(F32)
    d_input, dg0 = norm_back(x, scale_of(x), g_ref[0:1], d_normed)
    dg = (jnp.sum(dg0, axis=0, keepdims=True), dg12_ref[0:1], dg12_ref[1:2], dg3_ref[...])
    small_ref[...] = jnp.zeros_like(small_ref)
    for i in range(small_ref.shape[0]):
        for row in range(4):
            small_ref[i, row : row + 1, : sizes[0]] = dg[row][:, i * sizes[0] : (i + 1) * sizes[0]]
        small_ref[i, 4:6, : sizes[1]] = dqk_ref[:, i * sizes[1] : (i + 1) * sizes[1]]
    grad_ref[...] = (dres_ref[...] + d_input).astype(BF)


class Front:
    def __init__(self, parts, x, packed, w_qkv, w_out, w_gate_up):
        self.parts = parts
        self.arrays = [x, packed, w_qkv, w_out, w_gate_up]
        like = lambda shape, dtype=BF: jax.ShapeDtypeStruct(shape, dtype)
        (rows, width), units = x.shape, w_gate_up.shape[0]
        heads = HEADS * rows
        self.subs = {
            "packed": DirectWsh("gather", packed),
            "qkv": Gather(w_qkv, pair=True),
            "out": Gather(w_out, pair=True),
            "kv": Gather(like((rows, 2 * HD)), "ctx"),
        }
        self.tables = Tables(rows)
        self.groups = set().union(*(sub.groups for sub in self.subs.values()))
        self.outs = [
            like((8, width), F32), like((8, HD), F32), like((rows, width)), like((rows, (HEADS + 2) * HD), F32),
            like((heads, HD)), self.subs["kv"].outs[0], self.subs["qkv"].outs[0], self.subs["out"].outs[0],
            *self.tables.outs, like((units, width)), like((units, width)),
            like((heads, HD), F32), like((heads, 128), F32), like((8, rows, w_out.shape[0])), like((rows, width), F32),
            like((rows, width), F32), like((rows, width)),
        ]
        self.in_spaces, self.out_spaces = [pltpu.VMEM] * 5, [pltpu.VMEM] * len(self.outs)
        self.scratch = [
            pltpu.VMEM((8,) + packed.shape, BF), pltpu.VMEM((rows, 2 * HD), BF), pltpu.VMEM((heads, 128), F32),
            pltpu.VMEM((heads, 128), F32), pltpu.VMEM((heads, HD), F32), pltpu.VMEM((rows, HEADS * HD), BF),
        ]
        self.own = len(self.scratch)
        for sub in self.subs.values():
            self.scratch += sub.scratch

    def run(self, p, ins, outs, scratch):
        x, packed, w_qkv, w_out, w_gate_up = ins
        (gains, qk_gain, normed, raw, q, kv_all, qkv_all, out_all, cosine, sine, w_gate, w_up, heads, lse, parts,
         branch, resid, normed2) = outs
        packed_all, kv, top, total, accum, att = scratch[: self.own]
        rest = list(scratch[self.own :])
        held = {name: [rest.pop(0) for _ in sub.scratch] for name, sub in self.subs.items()}

        def begin(name, source, result):
            return self.subs[name].run(p, [source], [result], held[name])

        p.ready(1, 2)
        small = begin("packed", packed, packed_all)
        first = begin("qkv", w_qkv, qkv_all)
        next(small)
        next(first)
        for _ in self.tables.run(p, [], [cosine, sine], []):
            pass
        p.ready()
        split = unpair(w_gate_up, w_gate, w_up)
        second = begin("out", w_out, out_all)
        for i, _ in enumerate(first):
            next(split, None)
            if i >= 2:
                next(second, None)
        for _ in small:
            pass
        prepare_kernel(
            self.parts, x, qkv_all, packed_all, cosine, sine, gains, qk_gain, normed, raw, q, kv
        )
        p.store(2)
        p.store(6)
        turns = [begin("kv", kv, kv_all), second, split]
        while turns:
            turns = [turn for turn in turns if next(turn, "end") != "end"]
            yield
        for i in (3, 4, 5, 7, 10, 11):
            p.store(i)
        attend_kernel(
            q, kv_all, x, out_all, gains, heads, lse, parts, branch, resid, normed2, top, total, accum,
            att, p.ctx,
        )


class Back:
    attention = ("d_normed", "resid", "branch", "cot", "gains", "w_out", "q", "kv", "out", "lse")
    names = attention + (
        "raw", "cosine", "sine", "w_qkv", "x", "qk_gain", "dg3", "attended", "normed", "early", "late"
    )

    def __init__(self, parts, **arrays):
        self.parts = parts
        self.arrays = [arrays[name] for name in self.names]
        like = lambda shape, dtype=BF: jax.ShapeDtypeStruct(shape, dtype)
        (rows, width), heads = arrays["resid"].shape, arrays["q"].shape[0]
        qkv = arrays["w_qkv"].shape[0] // 8
        out = arrays["attended"].shape[2]
        mixed, small = like((8, rows, qkv)), like((8, 8, 256), F32)
        every = like((8, rows, width))
        self.subs = {
            "early": Gather(arrays["early"], "ctx"),
            "late": Gather(arrays["late"], "ctx"),
            "kv": ScatterCtx(like((8, 2, rows, 2 * HD))),
            "d_branch": Gather(like((rows, width))),
            "attended": DirectWsh("scatter", arrays["attended"]),
            "mixed": DirectWsh("scatter", mixed, 3),
            "small": DirectWsh("scatter", small, 3),
            "sum": SumCtx(mixed, every, like((8, rows, out)), every),
            "share": ShareCtx(like((8, 256), F32)),
        }
        self.groups = set().union(*(sub.groups for sub in self.subs.values()))
        self.outs = [like((rows, width))]
        self.outs += [self.subs[name].outs[0] for name in ("sum", "share", "early", "late")]
        self.in_spaces = [pltpu.VMEM] * (len(self.names) - 2) + [HBM] * 2
        self.out_spaces = [pltpu.VMEM, pltpu.VMEM, HBM, HBM, HBM]
        shapes = [
            ((rows, width), F32), ((rows, width), BF), ((2, width), F32), ((heads, HD), F32), ((8 * 2, rows, 2 * HD), BF),
            ((heads, HD), BF), ((rows, 2 * HD), F32), ((8, rows, width), BF), ((8, rows, out), BF), ((8, rows, qkv), BF),
            ((8, 8, 256), F32), ((8, rows, qkv), BF), ((8, 8, 256), F32), ((8, 256), F32),
            ((rows, (HEADS + 2) * HD), BF), ((2, HD), F32),
        ]
        self.own = len(shapes)
        self.scratch = [pltpu.VMEM(*shape) for shape in shapes]
        for sub in self.subs.values():
            self.scratch += sub.scratch

    def run(self, p, ins, outs, scratch):
        a = dict(zip(self.names, ins))
        grad, grads, small_parts, early_all, late_all = outs
        (d_resid, low, dg12, d_q, d_kv, d_heads, own_kv, db_all, at_all, d_mixed, small, dm_all, small_all, small_sum,
         mixed, dqk) = scratch[: self.own]
        rest = list(scratch[self.own :])
        held = {}
        for name, sub in self.subs.items():
            held[name] = [rest.pop(0) for _ in sub.scratch]

        def begin(name, sources, result):
            return self.subs[name].run(p, sources, [result], held[name])

        early = begin("early", [a["early"]], early_all)
        late = begin("late", [a["late"]], late_all)
        attended = begin("attended", [a["attended"]], at_all)
        next(early)
        p.ready()
        next(attended)
        attend_back_kernel(
            *(a[name] for name in self.attention),
            d_resid, low, dg12, d_q, d_kv, d_heads, p.ctx,
        )
        kv = begin("kv", [d_kv], own_kv)
        turns = [kv, begin("d_branch", [low], db_all), early]
        while kv in turns:
            turns = [turn for turn in turns if next(turn, "end") != "end"]
        finish_kernel(
            self.parts, own_kv, d_q, a["raw"], a["cosine"], a["sine"], a["w_qkv"], a["x"], a["gains"], a["qk_gain"],
            d_resid, dg12, a["dg3"], d_mixed, grad, small, mixed, dqk,
        )
        columns = [begin("mixed", [d_mixed], dm_all), begin("small", [small], small_all)]
        turns = columns + turns + [late]
        while any(turn in turns for turn in columns):
            turns = [turn for turn in turns if next(turn, "end") != "end"]
        for turn in turns[:-1] if late in turns else turns:
            for _ in turn:
                pass
        for _ in attended:
            pass
        small_sum[...] = jnp.sum(small_all[...], axis=0)
        share = begin("share", [small_sum], small_parts)
        total = begin("sum", [dm_all, a["normed"], at_all, db_all], grads)
        turns = [share, total] + ([late] if late in turns else [])
        while turns:
            turns = [turn for turn in turns if next(turn, "end") != "end"]
            yield


def on_device(hidden, w_qkv, w_out, norm_gains, qk_gains, w_gate_up, w_down, cotangent):
    tokens = hidden.shape[1]
    width = hidden.shape[2]
    gain_part, qk_part = norm_gains.shape[0], qk_gains.shape[0]
    packed = jnp.concatenate(
        [
            jnp.pad(norm_gains.T, ((0, 0), (0, 256 - gain_part))),
            jnp.pad(qk_gains.T, ((0, 10), (0, 256 - qk_part))),
        ]
    )
    (gains, qk_gain, normed, raw, q_low, whole_kv, full_qkv, full_out, cosine, sine, w_gate, w_up, out_heads, lse,
     attended, branch, resid, normed2) = transfer(
        1, "front", 70, Front((gain_part, qk_part), hidden[0], packed, w_qkv, w_out, w_gate_up)
    )
    full_qkv, full_out = full_qkv.reshape(-1, width), full_out.reshape(-1, width)
    whole_kv = whole_kv.reshape(-1, 2 * HD)

    output, dg3, d_normed2, ff_early, ff_late, normed_all = transfer(
        3, "feed_forward", 100, FeedForward(normed2, resid, cotangent[0], gains, w_gate, w_up, w_down, normed)
    )
    grad_hidden, grads, small_parts, early_all, late_all = transfer(
        7, "backward", 80,
        Back(
            (gain_part, qk_part), d_normed=d_normed2, resid=resid, branch=branch, cot=cotangent[0], gains=gains,
            w_out=full_out, q=q_low, kv=whole_kv, out=out_heads, lse=lse, raw=raw, cosine=cosine, sine=sine,
            w_qkv=full_qkv, x=hidden[0], qk_gain=qk_gain, dg3=dg3, attended=attended, normed=normed_all,
            early=ff_early, late=ff_late,
        ),
    )
    grad_gate_up, grad_down, grad_qkv, grad_out, small_sum = widen(
        early_all.reshape(-1, width), late_all.reshape(-1, width), w_down.shape[0], grads, small_parts,
        (w_qkv.shape[0], w_out.shape[0]),
    )
    return (
        output[None],
        grad_hidden[None],
        grad_qkv,
        grad_out,
        small_sum[:4, :gain_part].T,
        small_sum[4:6, :qk_part].T,
        grad_gate_up,
        grad_down,
    )


def solution(mesh):
    return jax.shard_map(
        on_device,
        mesh=mesh,
        in_specs=(
            P("wsh", "ctx", None),
            P("wsh", None),
            P("wsh", None),
            P("wsh", None),
            P("wsh", None),
            P("wsh", None, None),
            P("wsh", None),
            P("wsh", "ctx", None),
        ),
        out_specs=(
            P("wsh", "ctx", None),
            P("wsh", "ctx", None),
            P("wsh", None),
            P("wsh", None),
            P("wsh", None),
            P("wsh", None),
            P("wsh", None, None),
            P("wsh", None),
        ),
        check_vma=False,
    )
```

```python
import functools
import math

import jax
import jax.numpy as jnp
from jax import lax
from jax.experimental import pallas as pl
from jax.experimental.pallas import tpu as pltpu
from jax.sharding import PartitionSpec as P

HEADS = 4
HD = 256
KB = 512
EPS = 1e-06
ROPE_BASE = 1000000.0
MASKED = -1e30
MESH = pl.DeviceIdType.MESH
BF = jnp.bfloat16
F32 = jnp.float32
HBM = pltpu.HBM
ROOM = 60 * 2**20


def cost(us):
    return pl.CostEstimate(flops=0, bytes_accessed=int(us * 3.0e6), transcendentals=0)


class Grid:
    def __init__(self, axis, index, core):
        self.axis, self.core = axis, core
        self.h, self.y = lax.div(index, 4), lax.rem(index, 4)
        self.yp, self.ym, self.y2 = (lax.rem(self.y + k, 4) for k in (1, 3, 2))
        self.up, self.down = self.device(self.h, self.yp), self.device(self.h, self.ym)
        self.across = self.device(1 - self.h, self.y)

    def block(self, h, y):
        return h * 4 + y if self.axis == "wsh" else (h * 4 + y) * 2 + self.core

    def device(self, h, y):
        return {self.axis: self.block(h, y)}


class Place:
    def __init__(self):
        self.ctx, self.wsh = lax.axis_index("ctx"), lax.axis_index("wsh")
        self.chip, self.core = lax.div(self.ctx, 2), lax.rem(self.ctx, 2)
        self.grids = {"wsh": Grid("wsh", self.wsh, 0), "ctx": Grid("ctx", self.chip, self.core)}
        self.twin = {"ctx": self.ctx + 1 - 2 * self.core}

    def chips(self, step):
        return {"ctx": lax.rem(self.ctx + 2 * step, 16)}

    def row(self, step):
        return {"wsh": lax.rem(self.wsh + step, 8)}

    def peers(self, groups):
        found = []
        for axis, whole in (("wsh", "row"), ("ctx", "chips")):
            if axis in groups and whole not in groups:
                grid = self.grids[axis]
                found += [grid.up, grid.down, grid.across]
        if "row" in groups:
            found += [self.row(step) for step in range(1, 8)]
        if "chips" in groups:
            found += [self.chips(step) for step in range(1, 8)]
        if "others" in groups:
            found += [{"ctx": lax.rem(self.ctx + 2 * s + 1, 16)} for s in range(8)]
        elif "twin" in groups:
            found.append(self.twin)
        return found


def remote(src, dst, sems, i, device):
    return pltpu.make_async_remote_copy(
        src_ref=src, dst_ref=dst, send_sem=sems.at[0, i], recv_sem=sems.at[1, i],
        device_id=device, device_id_type=MESH,
    )


def meet(place, groups):
    barrier = pltpu.get_barrier_semaphore()
    peers = place.peers(groups)
    for peer in peers:
        pl.semaphore_signal(barrier, inc=1, device_id=peer, device_id_type=MESH)
    pl.semaphore_wait(barrier, len(peers))


def split_rows(count):
    return (count // 2 + 15) // 16 * 16


class Gather:
    def __init__(self, array, axis="wsh", pair=False, ring=False):
        self.arrays, self.axis, self.pair, self.ring = [array], axis, pair, ring
        self.twins = pair or axis == "ctx"
        self.groups = {axis, "twin"} if self.twins else {axis}
        count = 16 if axis == "ctx" else 8
        self.outs = [jax.ShapeDtypeStruct((count,) + array.shape, array.dtype)]
        self.out_spaces, self.in_spaces = [HBM], [HBM]
        self.scratch = [pltpu.SemaphoreType.DMA((2, 19)), pltpu.SemaphoreType.DMA]

    def run(self, p, ins, outs, scratch):
        (x,), (o,), (sems, own) = ins, outs, scratch
        g = p.grids[self.axis]
        size = x.shape[0] // (2 if self.pair else 1)
        base = pl.multiple_of(p.core * size, size) if self.pair else 0
        half = split_rows(size)
        every, low, high = pl.ds(base, size), pl.ds(base, half), pl.ds(base + half, size - half)
        h, other = g.h, 1 - g.h
        me = g.block(h, g.y)
        copies = {}

        def send(i, block, rows, device, source=None):
            source = o.at[block, rows] if source is None else source
            copies[i] = remote(source, o.at[block, rows], sems, i, device)
            copies[i].start()

        def arrived(i, block, rows):
            copies[i].wait_recv()
            if self.twins:
                send(9 + i, block, rows, p.twin)

        send(2, me, every, g.across, x.at[every])
        send(0, me, every, g.up, x.at[every])
        send(1, me, every, g.down, x.at[every])
        if self.axis == "ctx":
            send(18, me, every, p.twin, x)
        local = pltpu.make_async_copy(x, o.at[me], own)
        local.start()
        yield
        if self.ring:
            across = lambda i, place, rows: send(i, g.block(h, place), rows, g.across)
            arrived(0, g.block(h, g.ym), every)
            send(3, g.block(h, g.ym), low, g.up)
            across(5, g.ym, every)
            yield
            arrived(1, g.block(h, g.yp), every)
            send(4, g.block(h, g.yp), high, g.down)
            across(6, g.yp, every)
            yield
            arrived(2, g.block(other, g.y), every)
            arrived(3, g.block(h, g.y2), low)
            across(7, g.y2, low)
            yield
            arrived(4, g.block(h, g.y2), high)
            across(8, g.y2, high)
            yield
            arrived(5, g.block(other, g.ym), every)
            yield
            arrived(6, g.block(other, g.yp), every)
            yield
            arrived(7, g.block(other, g.y2), low)
            arrived(8, g.block(other, g.y2), high)
            yield
            for i, copy in copies.items():
                copy.wait_send()
                if i >= 9:
                    copy.wait_recv()
            local.wait()
            return
        block = g.block(other, g.y)
        arrived(2, block, every)
        send(5, block, every, g.up)
        send(6, block, every, g.down)
        yield
        block = g.block(h, g.ym)
        arrived(0, block, every)
        send(3, block, low, g.up)
        yield
        block = g.block(h, g.yp)
        arrived(1, block, every)
        send(4, block, high, g.down)
        yield
        block = g.block(other, g.ym)
        arrived(5, block, every)
        send(7, block, low, g.up)
        yield
        block = g.block(other, g.yp)
        arrived(6, block, every)
        send(8, block, high, g.down)
        yield
        block = g.block(h, g.y2)
        arrived(3, block, low)
        arrived(4, block, high)
        yield
        block = g.block(other, g.y2)
        arrived(7, block, low)
        arrived(8, block, high)
        yield
        for i, copy in copies.items():
            copy.wait_send()
            if i >= 9:
                copy.wait_recv()
        local.wait()


class Scatter:
    def __init__(self, array, axis="wsh", dtype=F32):
        _, rows, width = array.shape
        self.arrays, self.axis, self.groups = [array], axis, {axis}
        self.outs = [jax.ShapeDtypeStruct((rows, width), dtype)]
        self.in_spaces, self.out_spaces = [pltpu.VMEM], [pltpu.VMEM]
        half = split_rows(rows)
        low, high = pltpu.VMEM((2, half, width), BF), pltpu.VMEM((2, rows - half, width), BF)
        whole = pltpu.VMEM((2, rows, width), BF)
        self.scratch = [low, high, low, high, whole, whole, whole, pltpu.SemaphoreType.DMA((2, 13))]

    def run(self, p, ins, outs, scratch):
        (x,), (o,), (buf_a, buf_b, sum_c, sum_d, buf_c, buf_d, buf_e, sems) = ins, outs, scratch
        g = p.grids[self.axis]
        rows = o.shape[0]
        half = split_rows(rows)
        low, high = pl.ds(0, half), pl.ds(half, rows - half)
        planes = ((1 - g.h) * 4, g.h * 4)
        copies = {}

        def send(i, source, target, device):
            copies[i] = remote(source, target, sems, i, device)
            copies[i].start()

        for k, plane in enumerate(planes):
            send(k, x.at[plane + g.y2, low], buf_a.at[k], g.up)
            send(2 + k, x.at[plane + g.y2, high], buf_b.at[k], g.down)
            send(4 + k, x.at[plane + g.yp, high], buf_c.at[k, high], g.up)
            send(6 + k, x.at[plane + g.ym, low], buf_d.at[k, low], g.down)
        for k, plane in enumerate(planes):
            yield
            copies[k].wait_recv()
            sum_c[k] = (x[plane + g.yp, :half].astype(F32) + buf_a[k].astype(F32)).astype(BF)
            send(8 + k, sum_c.at[k], buf_c.at[k, low], g.up)
            yield
            copies[2 + k].wait_recv()
            sum_d[k] = (x[plane + g.ym, half:].astype(F32) + buf_b[k].astype(F32)).astype(BF)
            send(10 + k, sum_d.at[k], buf_d.at[k, high], g.down)
        for k, plane in enumerate(planes):
            yield
            for i in (4, 6, 8, 10):
                copies[i + k].wait_recv()
            total = x[plane + g.y].astype(F32) + buf_c[k].astype(F32) + buf_d[k].astype(F32)
            if k == 0:
                buf_e[0] = total.astype(BF)
                send(12, buf_e.at[0], buf_e.at[1], g.across)
            else:
                yield
                copies[12].wait_recv()
                o[...] = (total + buf_e[1].astype(F32)).astype(o.dtype)
        for copy in copies.values():
            copy.wait_send()


class DirectWsh:
    def __init__(self, mode, array, turns=9):
        self.mode, self.arrays, self.groups, self.turns = mode, [array], {"row"}, turns
        shape = ((8,) + array.shape) if mode == "gather" else array.shape
        self.outs = [jax.ShapeDtypeStruct(shape, array.dtype)]
        self.in_spaces, self.out_spaces = [HBM], [HBM]
        self.scratch = [pltpu.SemaphoreType.DMA((2, 7)), pltpu.SemaphoreType.DMA]

    def run(self, p, ins, outs, scratch):
        (x,), (o,), (sems, own) = ins, outs, scratch
        pick = (lambda i: x) if self.mode == "gather" else (lambda i: x.at[i])
        copies = []
        for step in range(1, 8):
            to = p.row(step)
            copies.append(remote(pick(to["wsh"]), o.at[p.wsh], sems, step - 1, to))
            copies[-1].start()
        copies.append(pltpu.make_async_copy(pick(p.wsh), o.at[p.wsh], own))
        copies[-1].start()
        for _ in range(self.turns):
            yield
        for copy in copies:
            copy.wait()


class ScatterCtx:
    def __init__(self, array):
        _, _, rows, width = array.shape
        self.arrays, self.groups = [array], {"chips", "twin"}
        self.outs = [jax.ShapeDtypeStruct((rows, width), F32)]
        self.in_spaces, self.out_spaces = [pltpu.VMEM], [pltpu.VMEM]
        self.scratch = [pltpu.VMEM((8, rows, width), BF)] * 3 + [pltpu.SemaphoreType.DMA((2, 15))]

    def run(self, p, ins, outs, scratch):
        (x,), (o,), (pair, sums, got, sems) = ins, outs, scratch
        copies = []
        order = list(range(1, 8)) + [0]
        for i, step in enumerate(order):
            chip = lax.rem(p.chip + step, 8)
            copies.append(remote(x.at[2 * chip + 1 - p.core], pair.at[chip], sems, i, p.twin))
            copies[-1].start()
        for i, step in enumerate(order):
            if i == 0:
                yield
            chip = lax.rem(p.chip + step, 8)
            copies[i].wait_recv()
            both = x[2 * chip + p.core].astype(F32) + pair[chip].astype(F32)
            if step > 0:
                sums[chip] = both.astype(BF)
                copies.append(remote(sums.at[chip], got.at[p.chip], sems, 7 + step, p.chips(step)))
                copies[-1].start()
            else:
                o[...] = both
        for step in range(1, 8):
            if step % 3 == 1:
                yield
            copies[7 + step].wait_recv()
            o[...] += got[lax.rem(p.chip + 8 - step, 8)].astype(F32)
        for copy in copies:
            copy.wait_send()


class SumCtx:
    def __init__(self, d_mixed, normed, attended, d_branch):
        width = normed.shape[-1]
        self.share = (d_mixed.shape[-1] + attended.shape[-1]) // 16
        rows = -(-self.share // 16) * 16
        self.arrays, self.groups = [d_mixed, normed, attended, d_branch], {"chips", "twin"}
        self.outs = [jax.ShapeDtypeStruct((8, 2, rows, width), BF)]
        self.in_spaces, self.out_spaces = [pltpu.VMEM] * 4, [pltpu.VMEM]
        self.scratch = [pltpu.VMEM((8, 2, rows, width), BF)]
        self.scratch += [pltpu.VMEM((8, rows, width), BF)] * 3 + [pltpu.SemaphoreType.DMA((2, 23))]

    def product(self, ins, x):
        d_mixed, normed, attended, d_branch = ins
        width = normed.shape[-1]
        flat = lambda ref: ref[...].reshape(-1, ref.shape[-1])
        parts = (dot(flat(d_mixed), flat(normed), TN), dot(flat(attended), flat(d_branch), TN))
        both = jnp.concatenate(parts, axis=0)
        blank = jnp.zeros((x.shape[2] - self.share, width), F32)
        for i in range(16):
            rows = both[i * self.share : (i + 1) * self.share]
            x[i // 2, i % 2] = jnp.concatenate([rows, blank], axis=0).astype(BF)

    def run(self, p, ins, outs, scratch):
        (o,), (x, pair, sums, got, sems) = outs, scratch
        self.product(ins, x)
        first = remote(x.at[:, 1 - p.core], pair, sems, 0, p.twin)
        first.start()
        first.wait_recv()
        copies = [first]
        for step in range(1, 8):
            chip = lax.rem(p.chip + step, 8)
            sums[chip] = (x[chip, p.core].astype(F32) + pair[chip].astype(F32)).astype(BF)
            copies.append(remote(sums.at[chip], got.at[p.chip], sems, step, p.chips(step)))
            copies[-1].start()
        total = x[p.chip, p.core].astype(F32) + pair[p.chip].astype(F32)
        yield
        for step in range(1, 8):
            copies[step].wait_recv()
            total = total + got[lax.rem(p.chip + 8 - step, 8)].astype(F32)
        o[p.chip, p.core] = total.astype(BF)
        mine = o.at[p.chip, p.core]
        spread = []
        for step in range(1, 8):
            spread.append(remote(mine, mine, sems, 7 + step, p.chips(step)))
            spread[-1].start()
        passed = [remote(mine, mine, sems, 15, p.twin)]
        passed[0].start()
        yield
        for step in range(1, 8):
            spread[step - 1].wait_recv()
            piece = o.at[lax.rem(p.chip + 8 - step, 8), p.core]
            passed.append(remote(piece, piece, sems, 15 + step, p.twin))
            passed[-1].start()
        for copy in copies + spread:
            copy.wait_send()
        for copy in passed:
            copy.wait()


class ShareCtx:
    def __init__(self, array):
        self.arrays, self.groups = [array], {"chips", "twin", "others"}
        self.outs = [jax.ShapeDtypeStruct((16,) + array.shape, array.dtype)]
        self.in_spaces, self.out_spaces = [HBM], [HBM]
        self.scratch = [pltpu.SemaphoreType.DMA((2, 15)), pltpu.SemaphoreType.DMA]

    def run(self, p, ins, outs, scratch):
        (x,), (o,), (sems, own) = ins, outs, scratch
        copies = []
        for step in range(1, 16):
            to = {"ctx": lax.rem(p.ctx + step, 16)}
            copies.append(remote(x, o.at[p.ctx], sems, step - 1, to))
            copies[-1].start()
        copies.append(pltpu.make_async_copy(x, o.at[p.ctx], own))
        copies[-1].start()
        for _ in range(9):
            yield
        for copy in copies:
            copy.wait()


def rows_loop(count, body):
    lax.fori_loop(0, count // 16, lambda i, _: (body(pl.ds(pl.multiple_of(i * 16, 16), 16)), 0)[1], 0)


class FeedForwardGrads:
    def __init__(self, d_gate, d_up, inner, normed, d_branch):
        units, width = d_gate.shape[1], normed.shape[1]
        self.arrays, self.groups = [d_gate, d_up, inner, normed, d_branch], {"ctx", "twin"}
        granules = -(-3 * units // 256)
        early = granules * 5 // 9
        self.pieces = (early * 16, (granules - early) * 16)
        sums = [pltpu.VMEM((8, rows, width), BF) for rows in self.pieces]
        pieces = [jax.ShapeDtypeStruct(b.shape, BF) for b in sums]
        self.scatters = [Scatter(piece, "ctx", BF) for piece in pieces]
        self.outs = self.scatters[0].outs + self.scatters[1].outs
        self.in_spaces, self.out_spaces = [pltpu.VMEM] * 5, [pltpu.VMEM] * 2
        self.scratch = [pltpu.VMEM((16 * rows, width), BF) for rows in self.pieces]
        self.scratch += sums + sums + [pltpu.SemaphoreType.DMA((2, 16))]
        self.scratch += self.scatters[0].scratch + self.scatters[1].scratch

    def run(self, p, ins, outs, scratch):
        d_gate, d_up, inner, normed, d_branch = ins
        first, second, pair_first, pair_second, sums, sums_second, sems, *rest = scratch
        count = len(self.scatters[0].scratch)
        units = d_gate.shape[1]
        split = first.shape[0]
        twins = []

        def put(at, value):
            end = at + value.shape[0]
            if at < split:
                first[at : min(end, split)] = value[: min(end, split) - at]
            if end > split:
                second[max(at, split) - split : end - split] = value[max(at, split) - at :]

        def swap(whole, pair, number):
            size = pair.shape[1]
            for chip in range(8):
                there = pl.ds(pl.multiple_of((2 * chip + 1 - p.core) * size, 16), size)
                twins.append(remote(whole.at[there], pair.at[chip], sems, 8 * number + chip, p.twin))
                twins[-1].start()

        def add(whole, pair, result, number):
            size = pair.shape[1]
            for chip in range(8):
                here = pl.ds(pl.multiple_of((2 * chip + p.core) * size, 16), size)
                twins[8 * number + chip].wait_recv()
                result[chip] = (whole[here].astype(F32) + pair[chip].astype(F32)).astype(BF)

        started = False
        for number, (left, right) in enumerate(((d_gate, normed), (d_up, normed), (inner, d_branch))):
            for start in range(0, units, 256):
                stop = min(start + 256, units)
                put(number * units + start, dot(left[:, start:stop], right[...], TN).astype(BF))
                if not started and number * units + stop >= split:
                    started = True
                    swap(first, pair_first, 0)
            if started:
                yield
        missing = second.shape[0] - (3 * units - split)
        if missing:
            second[second.shape[0] - missing :] = jnp.zeros((missing, second.shape[1]), BF)
        swap(second, pair_second, 1)
        add(first, pair_first, sums, 0)
        turns = [self.scatters[0].run(p, [sums], outs[:1], rest[:count])]
        next(turns[0])
        add(second, pair_second, sums_second, 1)
        turns.append(self.scatters[1].run(p, [sums_second], outs[1:], rest[count:]))
        while turns:
            turns = [turn for turn in turns if next(turn, "end") != "end"]
            yield
        for copy in twins:
            copy.wait_send()


def unpair(both, gate, up):
    step = 96
    for start in range(0, gate.shape[0], step):
        def move(rows):
            here = pl.ds(pl.multiple_of(rows.start + start, 16), 16)
            gate[here] = both[here, 0, :]
            up[here] = both[here, 1, :]

        rows_loop(step, move)
        yield


def ring_blocks(g, x, o, sems):
    rows = x.shape[0]
    half = rows // 2
    low, high = (0, half), (half, half)
    copies = {}

    def at(slot, part=(0, rows)):
        return o.at[pl.ds(slot * rows + part[0], part[1])]

    def send(i, source, target, device):
        copies[i] = remote(source, target, sems, i, device)
        copies[i].start()

    send(2, x, at(1), g.across)
    send(0, x, at(2), g.up)
    send(1, x, at(3), g.down)
    o[:rows] = x[...]
    copies[2].wait_recv()
    send(5, at(1), at(4), g.up)
    send(6, at(1), at(5), g.down)
    yield 0
    copies[0].wait_recv()
    send(3, at(2, low), at(6, low), g.up)
    copies[1].wait_recv()
    send(4, at(3, high), at(6, high), g.down)
    yield 1
    copies[5].wait_recv()
    send(7, at(4, low), at(7, low), g.up)
    copies[6].wait_recv()
    send(8, at(5, high), at(7, high), g.down)
    yield 2
    for i in (3, 4, 7, 8):
        copies[i].wait_recv()
    yield 3
    for copy in copies.values():
        copy.wait_send()


class RingSum:
    slots = {"opposite": (7, 6), "up": (5, 3), "down": (4, 2), "own": (1, 0)}

    def __init__(self, g, x, o, scratch):
        self.g, self.x, self.o = g, x, o
        self.buf_a, self.buf_b, self.sum_c, self.sum_d, self.buf_c, self.buf_d, self.buf_e, self.sems = scratch
        self.rows = o.shape[0]
        self.half = self.rows // 2
        self.copies = {}

    @staticmethod
    def scratch(rows, width):
        half, whole = pltpu.VMEM((2, rows // 2, width), BF), pltpu.VMEM((2, rows, width), BF)
        return [half, half, half, half, whole, whole, whole, pltpu.SemaphoreType.DMA((2, 13))]

    def at(self, place, k, part):
        return pl.ds(self.slots[place][k] * self.rows + part * self.half, self.half * (1 if part < 2 else 2))

    def send(self, i, source, target, device):
        self.copies[i] = remote(source, target, self.sems, i, device)
        self.copies[i].start()

    def near(self, k):
        low, high = pl.ds(0, self.half), pl.ds(self.half, self.half)
        self.send(4 + k, self.x.at[self.at("up", k, 1)], self.buf_c.at[k, high], self.g.up)
        self.send(6 + k, self.x.at[self.at("down", k, 0)], self.buf_d.at[k, low], self.g.down)

    def far(self, k):
        self.send(k, self.x.at[self.at("opposite", k, 0)], self.buf_a.at[k], self.g.up)
        self.send(2 + k, self.x.at[self.at("opposite", k, 1)], self.buf_b.at[k], self.g.down)

    def rest(self):
        x, copies = self.x, self.copies
        low, high = pl.ds(0, self.half), pl.ds(self.half, self.half)
        for k in range(2):
            yield
            copies[k].wait_recv()
            self.sum_c[k] = (x[self.at("up", k, 0)].astype(F32) + self.buf_a[k].astype(F32)).astype(BF)
            self.send(8 + k, self.sum_c.at[k], self.buf_c.at[k, low], self.g.up)
            copies[2 + k].wait_recv()
            self.sum_d[k] = (x[self.at("down", k, 1)].astype(F32) + self.buf_b[k].astype(F32)).astype(BF)
            self.send(10 + k, self.sum_d.at[k], self.buf_d.at[k, high], self.g.down)
        for k in range(2):
            yield
            for i in (4, 6, 8, 10):
                copies[i + k].wait_recv()
            slot = self.slots["own"][k] * self.rows
            total = x[slot : slot + self.rows].astype(F32) + self.buf_c[k].astype(F32) + self.buf_d[k].astype(F32)
            if k == 0:
                self.buf_e[0] = total.astype(BF)
                self.send(12, self.buf_e.at[0], self.buf_e.at[1], self.g.across)
            else:
                yield
                copies[12].wait_recv()
                self.o[...] = total + self.buf_e[1].astype(F32)
        for copy in copies.values():
            copy.wait_send()


def forward_block(n, w_gate, w_up, w_down, inner_ref, gelu_ref, slope_ref, terms_ref, rows):
    gate = dot(n, w_gate[...], NT)
    up = dot(n, w_up[...], NT)
    bend, grow = math.sqrt(2.0 / math.pi), 0.044715
    square = gate * gate
    wave = jnp.tanh(bend * gate * (1.0 + grow * square))
    rise = 0.5 * (1.0 + wave)
    gelu = gate * rise
    slope = rise + 0.5 * bend * gate * (1.0 - wave * wave) * (1.0 + 3.0 * grow * square)
    gelu_ref[rows] = gelu.astype(BF)
    slope_ref[rows] = (up * slope).astype(BF)
    inner_ref[rows] = (gelu * up).astype(BF)
    terms_ref[rows] = jnp.dot(inner_ref[rows], w_down[...], preferred_element_type=F32).astype(BF)


class FeedForward:
    def __init__(self, normed, resid, cot, gains, w_gate, w_up, w_down):
        (rows, width), units = normed.shape, w_down.shape[0]
        self.arrays = [normed, resid, cot, gains, w_gate, w_up, w_down]
        tokens = jax.ShapeDtypeStruct((8 * rows, width), BF)
        hidden = jax.ShapeDtypeStruct((8 * rows, units), BF)
        self.grads = FeedForwardGrads(hidden, hidden, hidden, tokens, tokens)
        self.groups = {"wsh"} | self.grads.groups
        shapes = [((rows, width), BF), ((1, width), F32), ((rows, width), F32)]
        self.outs = [jax.ShapeDtypeStruct(*shape) for shape in shapes] + self.grads.outs
        self.in_spaces, self.out_spaces = [pltpu.VMEM] * 7, [pltpu.VMEM] * 5
        wide, narrow = pltpu.VMEM(tokens.shape, BF), pltpu.VMEM(hidden.shape, BF)
        self.scratch = [wide] * 3 + [narrow] * 5 + [pltpu.VMEM((rows, width), F32), pltpu.VMEM((rows, width), BF)]
        self.scratch += [pltpu.SemaphoreType.DMA((2, 9))] * 2
        self.scratch += RingSum.scratch(rows, width) * 2 + self.grads.scratch

    def run(self, p, ins, outs, scratch):
        x, resid, cot, gains, w_gate, w_up, w_down = ins
        out, dg, d_normed, *grads = outs
        tokens, terms, d_all, inner, gelu, slope, d_gate, d_up, branch, low, sems, back_sems, *rest = scratch
        g = p.grids["wsh"]
        count = len(RingSum.scratch(*x.shape))
        there = RingSum(g, terms, branch, rest[:count])
        back = RingSum(g, terms, d_normed, rest[count : 2 * count])
        pair = 2 * x.shape[0]

        def sends(ring, i):
            if i in (1, 2):
                ring.near(2 - i)
            if i == 3:
                ring.far(0)
                ring.far(1)

        p.ready(0)
        for i in ring_blocks(g, x, tokens, sems):
            if i == 0:
                p.ready()
            rows = slice(i * pair, (i + 1) * pair)
            forward_block(tokens[rows], w_gate, w_up, w_down, inner, gelu, slope, terms, rows)
            sends(there, i)
        yield from there.rest()
        total, gain, c = branch[...], gains[3:4], cot[...].astype(F32)
        scale = scale_of(total)
        d_branch, dg_terms = norm_back(total, scale, gain, c)
        low[...] = d_branch.astype(BF)
        out[...] = (resid[...] + total * scale * gain).astype(BF)
        dg[...] = jnp.sum(dg_terms, axis=0, keepdims=True)
        for i in ring_blocks(g, low, d_all, back_sems):
            rows = slice(i * pair, (i + 1) * pair)
            d_inner = dot(d_all[rows], w_down[...], NT)
            d_gate[rows] = (d_inner * slope[rows].astype(F32)).astype(BF)
            d_up[rows] = (d_inner * gelu[rows].astype(F32)).astype(BF)
            terms[rows] = (
                jnp.dot(d_gate[rows], w_gate[...], preferred_element_type=F32)
                + jnp.dot(d_up[rows], w_up[...], preferred_element_type=F32)
            ).astype(BF)
            sends(back, i)
        turns = [
            self.grads.run(p, [d_gate, d_up, inner, tokens, d_all], grads, rest[2 * count :]),
            back.rest(),
        ]
        while turns:
            turns = [turn for turn in turns if next(turn, "end") != "end"]
            yield


class Tables:
    def __init__(self, tokens):
        self.tokens, self.arrays, self.groups = tokens, [], set()
        self.outs = [jax.ShapeDtypeStruct((tokens, HD // 2), F32)] * 2
        self.in_spaces, self.out_spaces, self.scratch = [], [pltpu.VMEM] * 2, []

    def run(self, p, ins, outs, scratch):
        shape = outs[0].shape
        token = lax.broadcasted_iota(jnp.int32, shape, 0) + p.ctx * self.tokens
        power = lax.broadcasted_iota(jnp.int32, shape, 1).astype(F32) * (-2.0 / HD)
        angles = token.astype(F32) * jnp.exp(power * math.log(ROPE_BASE))
        outs[0][...] = jnp.cos(angles)
        outs[1][...] = jnp.sin(angles)
        yield


def transfer_kernel(parts, ins, outs, scratch, ready, store):
    place = Place()
    place.ready, place.store = ready, store
    meet(place, set().union(*(part.groups for part in parts)))

    def take(refs, counts):
        refs = list(refs)
        return [[refs.pop(0) for _ in range(count)] for count in counts]

    ins = take(ins, [len(part.arrays) for part in parts])
    outs = take(outs, [len(part.outs) for part in parts])
    scratch = take(scratch, [len(part.scratch) for part in parts])
    active = [part.run(place, i, o, s) for part, i, o, s in zip(parts, ins, outs, scratch)]
    while active:
        active = [run for run in active if next(run, "end") != "end"]


def staged(body, name, us, arrays, in_spaces, outs, out_spaces, scratch, cid=None):
    picked_in = [i for i, space in enumerate(in_spaces) if space == pltpu.VMEM]
    picked_out = [i for i, space in enumerate(out_spaces) if space == pltpu.VMEM]
    held = [pltpu.VMEM(arrays[i].shape, arrays[i].dtype) for i in picked_in]
    held += [pltpu.VMEM(outs[i].shape, outs[i].dtype) for i in picked_out]
    counts = (len(arrays), len(outs), len(picked_in), len(picked_out))

    def kernel(*refs):
        ends = [sum(counts[:k]) for k in range(5)]
        far_in, far_out, near_in, near_out = (refs[ends[k] : ends[k + 1]] for k in range(4))
        in_sems, out_sems, *rest = refs[ends[4] :]
        ins, results = list(far_in), list(far_out)
        loads = []
        for k, i in enumerate(picked_in):
            loads.append(pltpu.make_async_copy(far_in[i], near_in[k], in_sems.at[k]))
            loads[-1].start()
            ins[i] = near_in[k]
        for k, i in enumerate(picked_out):
            results[i] = near_out[k]

        waiting = dict(zip(picked_in, loads))

        def ready(*indices):
            for i in indices or tuple(waiting):
                waiting.pop(i).wait()

        stores = {}

        def store(i):
            k = picked_out.index(i)
            stores[i] = pltpu.make_async_copy(near_out[k], far_out[i], out_sems.at[k])
            stores[i].start()

        body(ins, results, rest, ready, store)
        for i in picked_out:
            if i not in stores:
                store(i)
        for copy in stores.values():
            copy.wait()

    sems = [pltpu.SemaphoreType.DMA((max(len(picked), 1),)) for picked in (picked_in, picked_out)]
    extra = {} if cid is None else {"collective_id": cid, "has_side_effects": True}
    return pl.pallas_call(
        kernel,
        out_shape=list(outs),
        in_specs=[pl.BlockSpec(memory_space=HBM)] * counts[0],
        out_specs=[pl.BlockSpec(memory_space=HBM)] * counts[1],
        scratch_shapes=held + sems + list(scratch),
        compiler_params=pltpu.CompilerParams(vmem_limit_bytes=ROOM, **extra),
        cost_estimate=cost(us),
        name=name,
    )(*arrays)


def transfer(cid, name, us, *parts):
    every = lambda field: [item for part in parts for item in getattr(part, field)]
    return staged(
        functools.partial(transfer_kernel, parts), name, us, every("arrays"), every("in_spaces"),
        every("outs"), every("out_spaces"), every("scratch"), cid,
    )


NT = (((1,), (1,)), ((), ()))
TN = (((0,), (0,)), ((), ()))


def dot(a, b, dims):
    return lax.dot_general(a, b, dims, preferred_element_type=F32)


def masked_scores(q, keys, block, ctx, tokens):
    scores = dot(q, keys, NT)
    row = lax.rem(lax.broadcasted_iota(jnp.int32, scores.shape, 0), tokens) + ctx * tokens
    col = lax.broadcasted_iota(jnp.int32, scores.shape, 1) + block * KB
    return jnp.where(col <= row, scores, MASKED)


def widen_kernel(first, sizes, gate_ref, *refs):
    ups, mores, lows = refs[:3], refs[3:6], refs[6:9]
    grads_ref, small_ref, both_ref, down_ref, qkv_ref, out_ref, gains_ref, qk_ref = refs[9:]
    step = ups[0].shape[0]
    place = pl.program_id(0)
    both_ref[:, 0, :] = gate_ref[...].astype(F32)
    for k in range(3):
        rows = slice(k * step, (k + 1) * step)
        down_ref[rows] = lows[k][...].astype(F32)

        def put(value, rows=rows):
            both_ref[rows, 1, :] = value[...].astype(F32)

        pl.when(3 * place + k < first)(functools.partial(put, ups[k]))
        pl.when(3 * place + k >= first)(functools.partial(put, mores[k]))

    @pl.when(place == 0)
    def _():
        share, split = (qkv_ref.shape[0] + out_ref.shape[0]) // 16, qkv_ref.shape[0]
        for i in range(16):
            value = grads_ref[i // 2, i % 2].astype(F32)
            start, stop = i * share, (i + 1) * share
            middle = min(max(split, start), stop)
            if middle > start:
                qkv_ref[start:middle] = value[: middle - start]
            if stop > middle:
                out_ref[middle - split : stop - split] = value[middle - start : share]
        total = jnp.sum(small_ref[...], axis=0)
        gains_ref[...] = total[0:4, : sizes[0]]
        qk_ref[...] = total[4:6, : sizes[1]]


def widen(early, late, rows, grads, small, parts, sizes):
    width = early.shape[1]
    step = 96
    count = rows // step
    first = early.shape[0] // step - count
    spec = lambda index: pl.BlockSpec((step, width), lambda i: (index(i), 0))
    large = pl.BlockSpec((3 * step, width), lambda i: (i, 0))
    whole = lambda shape: pl.BlockSpec(shape, lambda i: (0,) * len(shape))
    outs = [(rows, 2, width), (rows, width), (parts[0], width), (parts[1], width), (4, sizes[0]), (2, sizes[1])]
    return pl.pallas_call(
        functools.partial(widen_kernel, first, sizes),
        grid=(count // 3,),
        out_shape=[jax.ShapeDtypeStruct(shape, F32) for shape in outs],
        in_specs=[large]
        + [spec(lambda i, k=k: jnp.minimum(3 * i + k, first - 1) + count) for k in range(3)]
        + [spec(lambda i, k=k: jnp.maximum(3 * i + k - first, 0)) for k in range(3)]
        + [spec(lambda i, k=k: 3 * i + k + count - first) for k in range(3)]
        + [whole(grads.shape), whole(small.shape)],
        out_specs=[pl.BlockSpec((3 * step, 2, width), lambda i: (i, 0, 0)), large]
        + [whole(shape) for shape in outs[2:]],
        compiler_params=pltpu.CompilerParams(vmem_limit_bytes=ROOM),
        cost_estimate=cost(9),
        name="widen",
    )(early, *[early] * 3, *[late] * 6, grads, small)


def scale_of(values):
    return lax.rsqrt(jnp.mean(values * values, axis=-1, keepdims=True) + EPS)


def norm_back(v, r, g, dy):
    gdy = g * dy
    dv = r * gdy - v * (r * r * r) * jnp.mean(gdy * v, axis=-1, keepdims=True)
    return dv, dy * v * r


def rope(v, cosine, sine):
    a, b = v[..., : HD // 2], v[..., HD // 2 :]
    return jnp.concatenate([a * cosine - b * sine, b * cosine + a * sine], axis=-1)


def rope_back(u, cosine, sine):
    a, b = u[..., : HD // 2], u[..., HD // 2 :]
    return jnp.concatenate([a * cosine + b * sine, b * cosine - a * sine], axis=-1)


def compute(kernel, name, us, outs, scratch, *args):
    def body(ins, results, rest, ready, store):
        ready()
        kernel(*ins, *results, *rest)

    outs = [jax.ShapeDtypeStruct(shape, dtype) for shape, dtype in outs]
    return staged(
        body, name, us, args, [pltpu.VMEM] * len(args), outs, [pltpu.VMEM] * len(outs), scratch
    )


def prepare_kernel(parts, x_ref, w_ref, packed_ref, cos_ref, sin_ref, g_ref, qk_ref, normed_ref, raw_ref, q_ref, kv_ref):
    gain_part, qk_part = parts
    g_ref[...] = jnp.zeros_like(g_ref)
    qk_ref[...] = jnp.zeros_like(qk_ref)
    for i in range(packed_ref.shape[0]):
        values = packed_ref[i].astype(F32)
        g_ref[0:4, i * gain_part : (i + 1) * gain_part] = values[0:4, :gain_part]
        qk_ref[0:2, i * qk_part : (i + 1) * qk_part] = values[4:6, :qk_part]
    x = x_ref[...].astype(F32)
    tokens = x.shape[0]
    normed = (x * scale_of(x) * g_ref[0:1]).astype(BF)
    normed_ref[...] = normed
    raw_ref[...] = dot(normed, w_ref[...].reshape(-1, w_ref.shape[-1]), NT)
    cosine, sine = cos_ref[...], sin_ref[...]
    for head in range(HEADS + 1):
        v = raw_ref[:, head * HD : (head + 1) * HD]
        column = 0 if head < HEADS else 1
        turned = rope(v * scale_of(v) * qk_ref[column : column + 1], cosine, sine)
        if head < HEADS:
            q_ref[head * tokens : (head + 1) * tokens] = (turned * HD ** (-0.5)).astype(BF)
        else:
            kv_ref[:, :HD] = turned.astype(BF)
    kv_ref[:, HD:] = raw_ref[:, (HEADS + 1) * HD :].astype(BF)


def attend_kernel(q_ref, kv_ref, x_ref, w_ref, g_ref, out_ref, lse_ref, parts_ref, branch_ref,
                  resid_ref, normed_ref, top, total, accum, att_ref, ctx):
    tokens = x_ref.shape[0]
    last = lax.div(ctx * tokens, KB)
    q = q_ref[...]

    def block_of(index, half):
        per = KB // tokens
        return kv_ref[pl.ds(index * per, per), :, half * HD : (half + 1) * HD].reshape(KB, HD)

    scores = masked_scores(q, block_of(last, 0), last, ctx, tokens)
    start = jnp.max(scores, axis=-1, keepdims=True)
    probs = jnp.exp(scores - start)
    top[...] = jnp.broadcast_to(start, top.shape)
    total[...] = jnp.broadcast_to(jnp.sum(probs, axis=-1, keepdims=True), total.shape)
    accum[...] = jnp.dot(
        probs.astype(BF), block_of(last, 1), preferred_element_type=F32
    )

    def body(index, carry):
        scores = dot(q, block_of(index, 0), NT)
        old = top[:, :1]
        new = jnp.maximum(old, jnp.max(scores, axis=-1, keepdims=True))
        probs = jnp.exp(scores - new)
        keep = jnp.exp(old - new)
        top[...] = jnp.broadcast_to(new, top.shape)
        total[...] = total[...] * keep + jnp.sum(probs, axis=-1, keepdims=True)
        accum[...] = accum[...] * keep + jnp.dot(
            probs.astype(BF), block_of(index, 1), preferred_element_type=F32
        )
        return carry

    lax.fori_loop(0, last, body, 0)
    out_ref[...] = accum[...] / total[:, :1]
    lse_ref[...] = top[...] + jnp.log(total[...])
    for head in range(HEADS):
        att_ref[:, head * HD : (head + 1) * HD] = out_ref[
            head * tokens : (head + 1) * tokens
        ].astype(BF)
    part = parts_ref.shape[2]
    for i in range(parts_ref.shape[0]):
        parts_ref[i] = att_ref[:, i * part : (i + 1) * part]
    branch = jnp.dot(att_ref[...], w_ref[...].reshape(-1, w_ref.shape[-1]), preferred_element_type=F32)
    branch_ref[...] = branch
    resid = x_ref[...].astype(F32) + branch * scale_of(branch) * g_ref[1:2]
    resid_ref[...] = resid
    normed_ref[...] = (resid * scale_of(resid) * g_ref[2:3]).astype(BF)


def attend_back_kernel(dn_ref, resid_ref, branch_ref, cot_ref, g_ref, w_ref, q_ref, kv_ref, out_ref,
                       lse_ref, dres_ref, low_ref, dg_ref, dq_ref, dkv_ref, d_ref, ctx):
    tokens = resid_ref.shape[0]
    last = lax.div(ctx * tokens, KB)
    resid = resid_ref[...]
    d_more, dg2 = norm_back(resid, scale_of(resid), g_ref[2:3], dn_ref[...])
    d_resid = cot_ref[...].astype(F32) + d_more
    dres_ref[...] = d_resid
    branch = branch_ref[...]
    d_branch, dg1 = norm_back(branch, scale_of(branch), g_ref[1:2], d_resid)
    low_ref[...] = d_branch.astype(BF)
    dg_ref[0:1] = jnp.sum(dg1, axis=0, keepdims=True)
    dg_ref[1:2] = jnp.sum(dg2, axis=0, keepdims=True)
    d_att = dot(low_ref[...], w_ref[...], NT)
    for head in range(HEADS):
        d_ref[head * tokens : (head + 1) * tokens] = d_att[:, head * HD : (head + 1) * HD].astype(BF)
    q = q_ref[...]
    d_out = d_ref[...]
    lse = lse_ref[:, :1]
    delta = jnp.sum(d_out.astype(F32) * out_ref[...], axis=-1, keepdims=True)

    def block_of(index):
        return pl.ds(pl.multiple_of(index * KB, KB), KB)

    def work(index, scores):
        block = block_of(index)
        probs = jnp.exp(scores - lse)
        d_probs = dot(d_out, kv_ref[block, HD:], NT)
        d_scores = (probs * (d_probs - delta)).astype(BF)
        d_keys = dot(d_scores, q, TN).astype(BF)
        d_values = dot(probs.astype(BF), d_out, TN).astype(BF)
        for i in range(KB // tokens):
            part = slice(i * tokens, (i + 1) * tokens)
            dkv_ref[index * (KB // tokens) + i, :, :HD] = d_keys[part]
            dkv_ref[index * (KB // tokens) + i, :, HD:] = d_values[part]
        return jnp.dot(d_scores, kv_ref[block, :HD], preferred_element_type=F32)

    dq_ref[...] = work(last, masked_scores(q, kv_ref[block_of(last), :HD], last, ctx, tokens))

    def body(index, carry):
        dq_ref[...] += work(index, dot(q, kv_ref[block_of(index), :HD], NT))
        return carry

    lax.fori_loop(0, last, body, 0)

    def clear(index, carry):
        dkv_ref[index] = jnp.zeros(dkv_ref.shape[1:], BF)
        return carry

    lax.fori_loop((last + 1) * (KB // tokens), dkv_ref.shape[0], clear, 0)


def finish_kernel(sizes, own_ref, dq_ref, raw_ref, cos_ref, sin_ref, w_ref, x_ref, g_ref, qk_ref, dres_ref, dg12_ref,
                  dg3_ref, parts_ref, grad_ref, small_ref, mixed_ref, dqk_ref):
    tokens = x_ref.shape[0]
    cosine, sine = cos_ref[...], sin_ref[...]
    total = jnp.zeros((1, HD), F32)
    for head in range(HEADS + 1):
        v = raw_ref[:, head * HD : (head + 1) * HD]
        if head < HEADS:
            u = dq_ref[head * tokens : (head + 1) * tokens] * HD ** (-0.5)
        else:
            u = own_ref[:, :HD]
        column = 0 if head < HEADS else 1
        dv, dg = norm_back(
            v, scale_of(v), qk_ref[column : column + 1], rope_back(u, cosine, sine)
        )
        mixed_ref[:, head * HD : (head + 1) * HD] = dv.astype(BF)
        dg = jnp.sum(dg, axis=0, keepdims=True)
        if head < HEADS:
            total = total + dg
        else:
            dqk_ref[0:1] = total
            dqk_ref[1:2] = dg
    mixed_ref[:, (HEADS + 1) * HD :] = own_ref[:, HD:].astype(BF)
    d_mixed = mixed_ref[...]
    part = parts_ref.shape[2]
    for i in range(parts_ref.shape[0]):
        parts_ref[i] = d_mixed[:, i * part : (i + 1) * part]
    d_normed = jnp.dot(d_mixed, w_ref[...], preferred_element_type=F32)
    x = x_ref[...].astype(F32)
    d_input, dg0 = norm_back(x, scale_of(x), g_ref[0:1], d_normed)
    dg = (jnp.sum(dg0, axis=0, keepdims=True), dg12_ref[0:1], dg12_ref[1:2], dg3_ref[...])
    small_ref[...] = jnp.zeros_like(small_ref)
    for i in range(small_ref.shape[0]):
        for row in range(4):
            small_ref[i, row : row + 1, : sizes[0]] = dg[row][:, i * sizes[0] : (i + 1) * sizes[0]]
        small_ref[i, 4:6, : sizes[1]] = dqk_ref[:, i * sizes[1] : (i + 1) * sizes[1]]
    grad_ref[...] = (dres_ref[...] + d_input).astype(BF)


class Front:
    def __init__(self, parts, x, packed, w_qkv, w_out, w_gate_up):
        self.parts = parts
        self.arrays = [x, packed, w_qkv, w_out, w_gate_up]
        like = lambda shape, dtype=BF: jax.ShapeDtypeStruct(shape, dtype)
        (rows, width), units = x.shape, w_gate_up.shape[0]
        heads = HEADS * rows
        self.subs = {
            "packed": DirectWsh("gather", packed),
            "qkv": Gather(w_qkv, pair=True),
            "out": Gather(w_out, pair=True),
            "kv": Gather(like((rows, 2 * HD)), "ctx"),
        }
        self.tables = Tables(rows)
        self.groups = set().union(*(sub.groups for sub in self.subs.values()))
        self.outs = [
            like((8, width), F32), like((8, HD), F32), like((rows, width)), like((rows, (HEADS + 2) * HD), F32),
            like((heads, HD)), self.subs["kv"].outs[0], self.subs["qkv"].outs[0], self.subs["out"].outs[0],
            *self.tables.outs, like((units, width)), like((units, width)),
            like((heads, HD), F32), like((heads, 128), F32), like((8, rows, w_out.shape[0])), like((rows, width), F32),
            like((rows, width), F32), like((rows, width)),
        ]
        self.in_spaces, self.out_spaces = [pltpu.VMEM] * 5, [pltpu.VMEM] * len(self.outs)
        self.scratch = [
            pltpu.VMEM((8,) + packed.shape, BF), pltpu.VMEM((rows, 2 * HD), BF), pltpu.VMEM((heads, 128), F32),
            pltpu.VMEM((heads, 128), F32), pltpu.VMEM((heads, HD), F32), pltpu.VMEM((rows, HEADS * HD), BF),
        ]
        self.own = len(self.scratch)
        for sub in self.subs.values():
            self.scratch += sub.scratch

    def run(self, p, ins, outs, scratch):
        x, packed, w_qkv, w_out, w_gate_up = ins
        (gains, qk_gain, normed, raw, q, kv_all, qkv_all, out_all, cosine, sine, w_gate, w_up, heads, lse, parts,
         branch, resid, normed2) = outs
        packed_all, kv, top, total, accum, att = scratch[: self.own]
        rest = list(scratch[self.own :])
        held = {name: [rest.pop(0) for _ in sub.scratch] for name, sub in self.subs.items()}

        def begin(name, source, result):
            return self.subs[name].run(p, [source], [result], held[name])

        p.ready(1, 2)
        small = begin("packed", packed, packed_all)
        first = begin("qkv", w_qkv, qkv_all)
        next(small)
        next(first)
        for _ in self.tables.run(p, [], [cosine, sine], []):
            pass
        p.ready()
        split = unpair(w_gate_up, w_gate, w_up)
        second = begin("out", w_out, out_all)
        for i, _ in enumerate(first):
            next(split, None)
            if i >= 2:
                next(second, None)
        for _ in small:
            pass
        prepare_kernel(
            self.parts, x, qkv_all, packed_all, cosine, sine, gains, qk_gain, normed, raw, q, kv
        )
        p.store(2)
        p.store(6)
        turns = [begin("kv", kv, kv_all), second, split]
        while turns:
            turns = [turn for turn in turns if next(turn, "end") != "end"]
            yield
        for i in (3, 4, 5, 7, 10, 11):
            p.store(i)
        attend_kernel(
            q, kv_all, x, out_all, gains, heads, lse, parts, branch, resid, normed2, top, total, accum,
            att, p.ctx,
        )


class Back:
    attention = ("d_normed", "resid", "branch", "cot", "gains", "w_out", "q", "kv", "out", "lse")
    names = attention + (
        "raw", "cosine", "sine", "w_qkv", "x", "qk_gain", "dg3", "attended", "normed", "early", "late"
    )

    def __init__(self, parts, **arrays):
        self.parts = parts
        self.arrays = [arrays[name] for name in self.names]
        like = lambda shape, dtype=BF: jax.ShapeDtypeStruct(shape, dtype)
        (rows, width), heads = arrays["resid"].shape, arrays["q"].shape[0]
        qkv = arrays["w_qkv"].shape[0] // 8
        out = arrays["attended"].shape[2]
        mixed, small = like((8, rows, qkv)), like((8, 8, 256), F32)
        every = like((8, rows, width))
        self.subs = {
            "early": Gather(arrays["early"], "ctx"),
            "late": Gather(arrays["late"], "ctx", ring=True),
            "kv": ScatterCtx(like((8, 2, rows, 2 * HD))),
            "d_branch": Gather(like((rows, width))),
            "normed": Gather(like((rows, width))),
            "attended": DirectWsh("scatter", arrays["attended"]),
            "mixed": DirectWsh("scatter", mixed, 3),
            "small": DirectWsh("scatter", small, 3),
            "sum": SumCtx(mixed, every, like((8, rows, out)), every),
            "share": ShareCtx(like((8, 256), F32)),
        }
        self.groups = set().union(*(sub.groups for sub in self.subs.values()))
        self.outs = [like((rows, width))]
        self.outs += [self.subs[name].outs[0] for name in ("sum", "share", "early", "late")]
        self.in_spaces = [pltpu.VMEM] * (len(self.names) - 3) + [HBM] * 3
        self.out_spaces = [pltpu.VMEM, pltpu.VMEM, HBM, HBM, HBM]
        shapes = [
            ((rows, width), F32), ((rows, width), BF), ((2, width), F32), ((heads, HD), F32), ((8 * 2, rows, 2 * HD), BF),
            ((heads, HD), BF), ((rows, 2 * HD), F32), ((8, rows, width), BF), ((8, rows, out), BF), ((8, rows, qkv), BF),
            ((8, 8, 256), F32), ((8, rows, qkv), BF), ((8, 8, 256), F32), ((8, 256), F32),
            ((rows, (HEADS + 2) * HD), BF), ((2, HD), F32),
            ((8, rows, width), BF),
        ]
        self.own = len(shapes)
        self.scratch = [pltpu.VMEM(*shape) for shape in shapes]
        for sub in self.subs.values():
            self.scratch += sub.scratch

    def run(self, p, ins, outs, scratch):
        a = dict(zip(self.names, ins))
        grad, grads, small_parts, early_all, late_all = outs
        (d_resid, low, dg12, d_q, d_kv, d_heads, own_kv, db_all, at_all, d_mixed, small, dm_all, small_all, small_sum,
         mixed, dqk, normed_all) = scratch[: self.own]
        rest = list(scratch[self.own :])
        held = {}
        for name, sub in self.subs.items():
            held[name] = [rest.pop(0) for _ in sub.scratch]

        def begin(name, sources, result):
            return self.subs[name].run(p, sources, [result], held[name])

        early = begin("early", [a["early"]], early_all)
        late = begin("late", [a["late"]], late_all)
        attended = begin("attended", [a["attended"]], at_all)
        normed = begin("normed", [a["normed"]], normed_all)
        next(normed)
        next(early)
        p.ready()
        next(attended)
        attend_back_kernel(
            *(a[name] for name in self.attention),
            d_resid, low, dg12, d_q, d_kv, d_heads, p.ctx,
        )
        kv = begin("kv", [d_kv], own_kv)
        turns = [kv, normed, begin("d_branch", [low], db_all), early]
        while kv in turns:
            turns = [turn for turn in turns if next(turn, "end") != "end"]
        next(late)
        finish_kernel(
            self.parts, own_kv, d_q, a["raw"], a["cosine"], a["sine"], a["w_qkv"], a["x"], a["gains"], a["qk_gain"],
            d_resid, dg12, a["dg3"], d_mixed, grad, small, mixed, dqk,
        )
        columns = [begin("mixed", [d_mixed], dm_all), begin("small", [small], small_all)]
        turns = columns + turns + [late]
        while any(turn in turns for turn in columns):
            turns = [turn for turn in turns if next(turn, "end") != "end"]
        for turn in turns[:-1] if late in turns else turns:
            for _ in turn:
                pass
        for _ in attended:
            pass
        small_sum[...] = jnp.sum(small_all[...], axis=0)
        share = begin("share", [small_sum], small_parts)
        total = begin("sum", [dm_all, normed_all, at_all, db_all], grads)
        turns = [share, total] + ([late] if late in turns else [])
        while turns:
            turns = [turn for turn in turns if next(turn, "end") != "end"]
            yield


def on_device(hidden, w_qkv, w_out, norm_gains, qk_gains, w_gate_up, w_down, cotangent):
    tokens = hidden.shape[1]
    width = hidden.shape[2]
    gain_part, qk_part = norm_gains.shape[0], qk_gains.shape[0]
    packed = jnp.concatenate(
        [
            jnp.pad(norm_gains.T, ((0, 0), (0, 256 - gain_part))),
            jnp.pad(qk_gains.T, ((0, 10), (0, 256 - qk_part))),
        ]
    )
    (gains, qk_gain, normed, raw, q_low, whole_kv, full_qkv, full_out, cosine, sine, w_gate, w_up, out_heads, lse,
     attended, branch, resid, normed2) = transfer(
        1, "front", 70, Front((gain_part, qk_part), hidden[0], packed, w_qkv, w_out, w_gate_up)
    )
    full_qkv, full_out = full_qkv.reshape(-1, width), full_out.reshape(-1, width)
    whole_kv = whole_kv.reshape(-1, 2 * HD)

    output, dg3, d_normed2, ff_early, ff_late = transfer(
        3, "feed_forward", 100, FeedForward(normed2, resid, cotangent[0], gains, w_gate, w_up, w_down)
    )
    grad_hidden, grads, small_parts, early_all, late_all = transfer(
        7, "backward", 80,
        Back(
            (gain_part, qk_part), d_normed=d_normed2, resid=resid, branch=branch, cot=cotangent[0], gains=gains,
            w_out=full_out, q=q_low, kv=whole_kv, out=out_heads, lse=lse, raw=raw, cosine=cosine, sine=sine,
            w_qkv=full_qkv, x=hidden[0], qk_gain=qk_gain, dg3=dg3, attended=attended, normed=normed,
            early=ff_early, late=ff_late,
        ),
    )
    grad_gate_up, grad_down, grad_qkv, grad_out, grad_gains, grad_qk = widen(
        early_all.reshape(-1, width), late_all.reshape(-1, width), w_down.shape[0], grads, small_parts,
        (w_qkv.shape[0], w_out.shape[0]), (gain_part, qk_part),
    )
    return (
        output[None],
        grad_hidden[None],
        grad_qkv,
        grad_out,
        grad_gains.T,
        grad_qk.T,
        grad_gate_up,
        grad_down,
    )


def solution(mesh):
    return jax.shard_map(
        on_device,
        mesh=mesh,
        in_specs=(
            P("wsh", "ctx", None),
            P("wsh", None),
            P("wsh", None),
            P("wsh", None),
            P("wsh", None),
            P("wsh", None, None),
            P("wsh", None),
            P("wsh", "ctx", None),
        ),
        out_specs=(
            P("wsh", "ctx", None),
            P("wsh", "ctx", None),
            P("wsh", None),
            P("wsh", None),
            P("wsh", None),
            P("wsh", None),
            P("wsh", None, None),
            P("wsh", None),
        ),
        check_vma=False,
    )
```
